256 devices in a mesh: xy: 64 (over y, x_hi, z), gz: 4 (over x_lo, core).
Axes of the slice: x: 4 (x_hi: 2, x_lo: 2; x = x_hi * 2 + x_lo), y: 4, z: 8, core: 2. Of those that a mesh axis runs over, the one named last changes fastest.
Arguments:
- e_field: float32 [64, 3, 16, 32, 512], P('xy', None, None, None, 'gz'), may hold values from -6 to 6
- h_field: float32 [64, 3, 16, 32, 512], P('xy', None, None, None, 'gz'), may hold values from -6 to 6
- material: int32 [64, 16, 32, 512], P('xy', None, None, 'gz'), may hold values from 0 to 3
- permittivity: float32 [4], replicated, may hold values from 1 to 12
- pml_x: int32 [128], replicated, may hold values from 0 to 8, as said below
- pml_y: int32 [256], replicated, may hold values from 0 to 8, as said below
- pml_z: int32 [512], replicated, may hold values from 0 to 8, as said below
- monitor_z: int32 [3], replicated, may hold values from 8 to 503
- omega: float32 [4], replicated, may hold values from 0.3 to 1.2
- focus: float32 [64, 512], P('xy'), may hold values from 0.1 to 3
Outputs:
- e_out: float32 [64, 3, 16, 32, 512], P('xy', None, None, None, 'gz')
- h_out: float32 [64, 3, 16, 32, 512], P('xy', None, None, None, 'gz')
- spectra: float32 [64, 72, 512], P('xy')
- objective: float32 [], replicated
The draws below stay inside these ranges and needn't reach their ends.
Inputs may be any that keep to these rules, and one draw needn't show every extreme that they name: `pml_x`: a layer of 4 to 8 cells at each end, level 8 at the outermost cell and 1 or more inside the layer; 0 between the layers. `pml_y`: as pml_x, along the second dimension. `pml_z`: as pml_x, along the third dimension.
All inputs are finite; a program needn't handle non-finite values.
Results may differ from the reference program's by a relative error of at most 0.00007.
Values sent between devices are 32-bit elements; how exact they have to be, the bound alone decides.
A program may use at most 64 MiB of HBM per device.

```python
import math
import jax
import jax.numpy as jnp
from jax import lax

CX = 16
CY = 32
TILES_Y = 8
STEPS = 4
WAVES = 4
MON = 3
NMAT = 4
DEPTH = 8
NX = 128
NY = 256
NZ = 512
SPEC = 72
N_XY = 64


def graded_layer(key, count):
    key_low = jax.random.fold_in(key, 1)
    key_high = jax.random.fold_in(key, 2)
    key_levels = jax.random.fold_in(key, 3)
    low_thick = jax.random.randint(key_low, (), DEPTH // 2, DEPTH + 1)
    high_thick = jax.random.randint(key_high, (), DEPTH // 2, DEPTH + 1)
    position = jnp.arange(count, dtype=jnp.int32)
    inner = jax.random.randint(key_levels, (count,), 1, DEPTH + 1)
    in_low = position < low_thick
    in_high = position >= count - high_thick
    edge = (position == 0) | (position == count - 1)
    level = jnp.where(edge, DEPTH, inner)
    return jnp.where(in_low | in_high, level, 0).astype(jnp.int32)


def draw_pml_x(key, part):
    key = jax.random.fold_in(key, 11)
    return graded_layer(key, NX)


def draw_pml_y(key, part):
    key = jax.random.fold_in(key, 12)
    return graded_layer(key, NY)


def draw_pml_z(key, part):
    key = jax.random.fold_in(key, 13)
    return graded_layer(key, NZ)


def draw_focus(key, part):
    key = jax.random.fold_in(key, 31)
    tiles = jnp.arange(N_XY, dtype=jnp.float32)[:, None]
    ramp = 1.0 + 2.0 * tiles / max(N_XY - 1, 1)
    base = jnp.exp(jax.random.uniform(key, (N_XY, CX * CY), jnp.float32, math.log(0.1), 0.0))
    return (base * ramp).astype(jnp.float32)


def with_ends(result, key, low, high):
    extent = result.shape
    place = [jax.random.randint(jax.random.fold_in(key, axis), (), 0, extent[axis]) for axis in range(len(extent))]
    result = result.at[tuple(place)].set(low)
    longest = extent.index(max(extent))
    place[longest] = (place[longest] + 1) % extent[longest]
    return result.at[tuple(place)].set(high)


def block_scale(key, dims, cuts, smallest, high):
    def one(dim, blocks):
        steps = jax.random.uniform(jax.random.fold_in(jax.random.fold_in(key, 6), dim), (blocks,), jnp.float32, smallest / len(cuts), high / len(cuts))
        return jnp.repeat(jnp.exp(steps), dims[dim] // blocks).reshape((-1,) + (1,) * (len(dims) - dim - 1))

    level = one(*cuts[0])
    for cut in cuts[1:]:
        level = level * one(*cut)
    return level


def normal_values(stream_key, dims, width, most, shards=(), kind=jnp.bfloat16):
    values = width * jax.random.normal(stream_key, dims, jnp.float32)
    if shards:
        values = values * block_scale(stream_key, dims, shards, -0.22, 0.18)
    return jnp.clip(values, -most, most).astype(kind)


def setup_inputs(seed: int = 0) -> dict:
    splits = jax.random.split(jax.random.key(seed), 11)
    e_field = normal_values(splits[0], (N_XY, 3, CX, CY, NZ), 1.0, 6.0, ((0, 64), (4, 4)), jnp.float32)
    h_field = normal_values(splits[1], (N_XY, 3, CX, CY, NZ), 1.0, 6.0, ((0, 64), (4, 4)), jnp.float32)
    material = with_ends(jax.random.randint(splits[2], (N_XY, CX, CY, NZ), 0, NMAT), jax.random.fold_in(splits[2], 1), 0, NMAT - 1).astype(jnp.int32)
    permittivity = jnp.clip(jnp.exp(jax.random.uniform(splits[3], (NMAT,), jnp.float32, math.log(1.0), math.log(12.0))), 1.0, 12.0)
    pml_x = draw_pml_x(jax.random.fold_in(splits[10], 71), 0)
    pml_y = draw_pml_y(jax.random.fold_in(splits[10], 71), 0)
    pml_z = draw_pml_z(jax.random.fold_in(splits[10], 71), 0)
    monitor_z = jax.random.randint(splits[7], (MON,), DEPTH, NZ - DEPTH).astype(jnp.int32)
    omega = jnp.clip(jax.random.uniform(splits[8], (WAVES,), jnp.float32, 0.3, 1.2), 0.3, 1.2)
    focus = draw_focus(jax.random.fold_in(splits[10], 71), 0)
    return {"e_field": e_field, "h_field": h_field, "material": material, "permittivity": permittivity, "pml_x": pml_x, "pml_y": pml_y, "pml_z": pml_z, "monitor_z": monitor_z, "omega": omega, "focus": focus}


TIME_STEP = 0.5
SIGMA_PEAK = 0.8


def grade(level):
    scaled = level.astype(jnp.float32) / DEPTH
    return scaled * scaled


def coefficients(permit, sigma):
    loss = sigma * (0.5 * TIME_STEP) / permit
    decay_elec = (1.0 - loss) / (1.0 + loss)
    drive_elec = TIME_STEP / (permit * (1.0 + loss))
    loss_magn = sigma * (0.5 * TIME_STEP)
    decay_magn = (1.0 - loss_magn) / (1.0 + loss_magn)
    drive_magn = TIME_STEP / (1.0 + loss_magn)
    return decay_elec, drive_elec, decay_magn, drive_magn


def lower_diff(field, border, axis):
    count = field.shape[axis]
    before = jnp.concatenate([jnp.expand_dims(border, axis), lax.slice_in_dim(field, 0, count - 1, axis=axis)], axis)
    return field - before


def upper_diff(field, border, axis):
    count = field.shape[axis]
    after = jnp.concatenate([lax.slice_in_dim(field, 1, count, axis=axis), jnp.expand_dims(border, axis)], axis)
    return after - field


def rotate(field, rims, differ):
    first, second, third = rims
    return jnp.stack([
        differ(field[2], second[1], 1) - differ(field[1], third[1], 2),
        differ(field[0], third[0], 2) - differ(field[2], first[1], 0),
        differ(field[1], first[0], 0) - differ(field[0], second[0], 1)])


def make_zeros(field):
    size_a, size_b, size_c = field.shape[1], field.shape[2], field.shape[3]
    return (jnp.zeros((2, size_b, size_c), jnp.float32), jnp.zeros((2, size_a, size_c), jnp.float32),
            jnp.zeros((2, size_a, size_b), jnp.float32))


def to_grid(tiles):
    rows = N_XY // TILES_Y
    comps = tiles.shape[1]
    shaped = tiles.reshape(rows, TILES_Y, comps, CX, CY, tiles.shape[4])
    return shaped.transpose(2, 0, 3, 1, 4, 5).reshape(comps, rows * CX, TILES_Y * CY, tiles.shape[4])


def to_tiles(grid):
    rows = N_XY // TILES_Y
    comps = grid.shape[0]
    rest = grid.shape[3:]
    shaped = grid.reshape((comps, rows, CX, TILES_Y, CY) + rest)
    order = (1, 3, 0, 2, 4) + tuple(range(5, 5 + len(rest)))
    return shaped.transpose(order).reshape((N_XY, comps, CX, CY) + rest)


def reference(e_field, h_field, material, permittivity, pml_x, pml_y, pml_z, monitor_z, omega, focus):
    efield = to_grid(e_field)
    hfield = to_grid(h_field)
    permit = permittivity[to_grid(material[:, None])[0]]
    sigma = SIGMA_PEAK * ((grade(pml_x)[:, None, None] + grade(pml_y)[None, :, None]) + grade(pml_z)[None, None, :])
    decay_elec, drive_elec, decay_magn, drive_magn = coefficients(permit, sigma)
    zeros = make_zeros(efield)
    real_part = jnp.zeros((WAVES, MON, 3, NX, NY), jnp.float32)
    imag_part = jnp.zeros((WAVES, MON, 3, NX, NY), jnp.float32)
    for instant in range(STEPS):
        efield = decay_elec[None] * efield + drive_elec[None] * rotate(hfield, zeros, lower_diff)
        plane = jnp.take(efield, monitor_z, axis=3).transpose(3, 0, 1, 2)
        phase = omega * ((instant + 1) * TIME_STEP)
        real_part = real_part + jnp.cos(phase)[:, None, None, None, None] * plane[None]
        imag_part = imag_part - jnp.sin(phase)[:, None, None, None, None] * plane[None]
        hfield = decay_magn[None] * hfield - drive_magn[None] * rotate(efield, zeros, upper_diff)
    stacked = jnp.stack([real_part, imag_part]).reshape(SPEC, NX, NY)
    spectra = to_tiles(stacked).reshape(N_XY, SPEC, CX * CY)
    half = SPEC // 2
    weighted = focus[:, None, :] * (spectra[:, :half] ** 2 + spectra[:, half:] ** 2)
    count = N_XY * WAVES * MON * 3 * CX * CY
    objective = jnp.sum(weighted) / jnp.float32(count)
    return to_tiles(efield), to_tiles(hfield), spectra, objective
```

```python
import functools

import jax
import jax.numpy as jnp
from jax import lax
from jax.experimental import pallas as pl
from jax.experimental.pallas import tpu as pltpu
from jax.sharding import PartitionSpec as P

MESH = pl.DeviceIdType.MESH
TILES_X = 8
TILES_Y = 8
SLABS = 4
STEPS = 4
WAVES = 4
MON = 3
DEPTH = 8
TIME_STEP = 0.5
SIGMA_PEAK = 0.8
CX, CY, CZ = 16, 32, 128
F32 = jnp.float32
EDGES = ((1, 0, -1), (-1, 0, 1), (1, -1, 0), (-1, 1, 0), (0, 1, -1), (0, -1, 1))


def roll(value, shift, axis):
    return pltpu.roll(value, shift % value.shape[axis], axis)


def grade(level):
    scaled = level.astype(F32) / DEPTH
    return scaled * scaled


def magnetic(sigma):
    loss = sigma * (0.5 * TIME_STEP)
    return (1.0 - loss) / (1.0 + loss), TIME_STEP / (1.0 + loss)


def electric(sigma, permit):
    loss = sigma * (0.5 * TIME_STEP) / permit
    return (1.0 - loss) / (1.0 + loss), TIME_STEP / (permit * (1.0 + loss))


def kernel(
    e_in, h_in, m_in, focus, permit, pml_x, pml_y, pml_z, monitor, omega,
    e_out, h_out, spec, objective,
    es, hs, kinds, ca, cb, da, db, grades_x, grades_y, trig, acc, planes, first, second,
    hy, hz, dax, day, daz,
    s_hy, s_hz, r_hx, r_hy, r_hz,
    s_ey, s_ez, r_ex, r_ey, r_ez,
    s_uy, s_uz, r_ux, r_uy, r_uz, r_edge,
    local_sem, send_sem, recv_sem, plane_send, plane_recv, total_send, total_recv,
):
    tile = lax.axis_index("xy")
    slab = lax.axis_index("gz")
    row, col = tile // TILES_Y, tile % TILES_Y

    def valid(off):
        r, c, g = row + off[0], col + off[1], slab + off[2]
        return (r >= 0) & (r < TILES_X) & (c >= 0) & (c < TILES_Y) & (g >= 0) & (g < SLABS)

    def device(off):
        return ((row + off[0]) * TILES_Y + col + off[1], slab + off[2])

    def minus(off):
        return tuple(-o for o in off)

    class Move:
        def __init__(self, n, k, off, src, dst):
            self.off = off
            self.copy = lambda: pltpu.make_async_remote_copy(
                src_ref=src, dst_ref=dst, send_sem=send_sem.at[n, k], recv_sem=recv_sem.at[n, k],
                device_id=device(off), device_id_type=MESH)

        def start(self):
            @pl.when(valid(self.off))
            def _():
                self.copy().start()

        def wait_send(self):
            @pl.when(valid(self.off))
            def _():
                self.copy().wait_send()

        def wait_recv(self):
            @pl.when(valid(minus(self.off)))
            def _():
                self.copy().wait_recv()

    barrier = pltpu.get_barrier_semaphore()

    def greet(where):
        pl.semaphore_signal(barrier, inc=1, device_id=where, device_id_type=MESH)

    for i in range(1, TILES_Y):
        greet((row * TILES_Y + (col + i) % TILES_Y, slab))
    for i in range(1, TILES_X):
        greet(((row + i) % TILES_X * TILES_Y + col, slab))
    for i in range(1, SLABS):
        greet((tile, (slab + i) % SLABS))
    for off in EDGES:
        @pl.when(valid(off))
        def _(off=off):
            greet(device(off))

    loads = []
    for k in range(3):
        loads.append(pltpu.make_async_copy(
            h_in.at[0, k], hs.at[k, pl.ds(1, CX), pl.ds(8, CY), :], local_sem.at[k]))
    loads.append(pltpu.make_async_copy(m_in.at[0], kinds, local_sem.at[3]))
    for k in range(3):
        loads.append(pltpu.make_async_copy(
            e_in.at[0, k], es.at[k, pl.ds(0, CX), pl.ds(0, CY), :], local_sem.at[4 + k]))
    for load in loads:
        load.start()

    lane8 = lax.broadcasted_iota(jnp.int32, (8, 128), 1)
    row8 = lax.broadcasted_iota(jnp.int32, (8, 128), 0)
    lane16 = lax.broadcasted_iota(jnp.int32, (16, 128), 1)
    row16 = lax.broadcasted_iota(jnp.int32, (16, 128), 0)
    lane32 = lax.broadcasted_iota(jnp.int32, (CY, 128), 1)
    row32 = lax.broadcasted_iota(jnp.int32, (CY, 128), 0)
    zero8 = jnp.zeros((8, 128), F32)

    def clear(off, *refs):
        @pl.when(jnp.logical_not(valid(minus(off))))
        def _():
            for ref in refs:
                ref[...] = jnp.zeros(ref.shape, F32)

    clear((1, 0, 0), r_hx, r_ux)
    clear((0, 1, 0), r_hy, r_uy)
    clear((0, 0, 1), r_hz, r_uz)
    clear((-1, 0, 0), r_ex)
    clear((0, -1, 0), r_ey)
    clear((0, 0, -1), r_ez)
    for k, off in enumerate(EDGES):
        clear(off, r_edge.at[k])

    def pack(total, field, source, start):
        for k in range(CY // 8):
            piece = roll(field[8 * k:8 * k + 8], start + k - source, 1)
            total = jnp.where(lane8 == start + k, piece, total)
        return total

    def unpack(packed, start, target):
        return jnp.concatenate([roll(packed, target - start - k, 1) for k in range(CY // 8)], axis=0)

    for k in range(3):
        loads[k].wait()

    def pack_h(x, total):
        total = roll(total, -4, 1)
        h0 = hs[0, x + 1, 8:8 + CY, :]
        h1 = hs[1, x + 1, 8:8 + CY, :]
        s_hy[0, pl.ds(x, 1), :] = h0[CY - 1:CY]
        s_hy[1, pl.ds(x, 1), :] = hs[2, x + 1, 7 + CY:8 + CY, :]
        return pack(pack(total, h0, 127, 60), h1, 127, 124)

    s_hz[...] = lax.fori_loop(0, CX, pack_h, zero8)

    greeted = TILES_Y - 1 + TILES_X - 1 + SLABS - 1
    for off in EDGES:
        greeted = greeted + jnp.where(valid(off), 1, 0)
    pl.semaphore_wait(barrier, greeted)

    opening = [
        Move(STEPS, 0, (1, 0, 0), hs.at[pl.ds(1, 2), CX, pl.ds(8, CY), :], r_hx),
        Move(STEPS, 1, (0, 1, 0), s_hy, r_hy),
        Move(STEPS, 2, (0, 0, 1), s_hz, r_hz),
    ]
    for move in opening:
        move.start()

    for i in range(CX):
        grades_x[i:i + 1, :] = jnp.full((1, 128), grade(pml_x[row * CX + i]), F32)
    for j in range(CY):
        grades_y[j:j + 1, :] = jnp.full((1, 128), grade(pml_y[col * CY + j]), F32)

    def lay(k, levels):
        return jnp.where(lane8 == k, pml_z[slab * CZ + k], levels)

    along_z = grade(lax.fori_loop(0, CZ, lay, jnp.zeros((8, 128), jnp.int32)))
    along_z32 = jnp.concatenate([along_z] * 4, axis=0)

    loads[3].wait()

    def fill(x, _):
        g = jnp.full((CY, 128), grade(pml_x[row * CX + x]), F32)
        sigma = SIGMA_PEAK * ((g + grades_y[...]) + along_z32)
        kind = kinds[x]
        eps = jnp.full((CY, 128), permit[0], F32)
        for which in range(1, 4):
            eps = jnp.where(kind == which, permit[which], eps)
        ca[x], cb[x] = electric(sigma, eps)
        da[x], db[x] = magnetic(sigma)
        return 0

    lax.fori_loop(0, CX, fill, 0)

    def below(ref, off, sigma):
        inside = jnp.where(valid(off), 1.0, 0.0).astype(F32)
        decay, drive = magnetic(sigma)
        ref[0] = decay * inside
        ref[1] = drive * inside

    g = grade(pml_x[jnp.maximum(row * CX - 1, 0)])
    below(dax, (-1, 0, 0), SIGMA_PEAK * ((g + grades_y[...]) + along_z32))
    g = grade(pml_y[jnp.maximum(col * CY - 1, 0)])
    below(day, (0, -1, 0), SIGMA_PEAK * ((grades_x[...] + g) + along_z32[0:CX]))
    g = grade(pml_z[jnp.maximum(slab * CZ - 1, 0)])
    packed_x = zero8
    for i in range(CX):
        packed_x = jnp.where((lane8 % 64) // 4 == i, grades_x[i:i + 1, :], packed_x)
    packed_y = zero8
    for k in range(CY // 8):
        packed_y = jnp.where(lane8 % 4 == k, grades_y[8 * k:8 * k + 8, :], packed_y)
    below(daz, (0, 0, -1), SIGMA_PEAK * ((packed_x + packed_y) + g))

    for n in range(STEPS):
        for w in range(WAVES):
            phase = jnp.full((8, 128), omega[w] * ((n + 1) * TIME_STEP), F32)
            trig[0, w, n] = jnp.cos(phase)
            trig[1, w, n] = -jnp.sin(phase)
    acc[...] = jnp.zeros(acc.shape, F32)

    for k in range(3):
        loads[4 + k].wait()
    for move in opening:
        move.wait_recv()
    hs[1, 0, 8:8 + CY, :] = r_hx[0]
    hs[2, 0, 8:8 + CY, :] = r_hx[1]
    hy[...] = r_hy[...]
    hz[...] = r_hz[...]
    for move in opening:
        move.wait_send()

    def electric_phase(n):
        def body(x, carry):
            halo, low, high, high2 = carry
            hs[0, x + 1, 7:8, :] = hy[0, pl.ds(x, 1), :]
            hs[2, x + 1, 7:8, :] = hy[1, pl.ds(x, 1), :]
            h0 = hs[0, x + 1, 8:8 + CY, :]
            h1 = hs[1, x + 1, 8:8 + CY, :]
            h2 = hs[2, x + 1, 8:8 + CY, :]
            h0y = hs[0, x + 1, 7:7 + CY, :]
            h2y = hs[2, x + 1, 7:7 + CY, :]
            h1x = hs[1, x, 8:8 + CY, :]
            h2x = hs[2, x, 8:8 + CY, :]
            h0z = jnp.where(lane32 == 0, unpack(halo, 0, 0), roll(h0, 1, 1))
            h1z = jnp.where(lane32 == 0, unpack(halo, 64, 0), roll(h1, 1, 1))
            decay, drive = ca[x], cb[x]
            e0 = decay * es[0, x, 0:CY, :] + drive * ((h2 - h2y) - (h1 - h1z))
            e1 = decay * es[1, x, 0:CY, :] + drive * ((h0 - h0z) - (h2 - h2x))
            e2 = decay * es[2, x, 0:CY, :] + drive * ((h1 - h1x) - (h0 - h0y))
            es[0, x, 0:CY, :] = e0
            es[1, x, 0:CY, :] = e1
            es[2, x, 0:CY, :] = e2
            s_ey[n, 0, pl.ds(x, 1), :] = e0[0:1]
            s_ey[n, 1, pl.ds(x, 1), :] = e2[0:1]
            low = pack(pack(roll(low, -4, 1), e0, 0, 60), e1, 0, 124)
            if n < STEPS - 1:
                for k, e in enumerate((e0, e1, e2)):
                    s_uy[n, k, pl.ds(x, 1), :] = e[CY - 1:CY]
                high = pack(pack(roll(high, -4, 1), e0, 127, 60), e1, 127, 124)
                high2 = pack(pack(roll(high2, -4, 1), e2, 127, 60), e2, 127, 124)
            return roll(halo, -4, 1), low, high, high2

        _, low, high, high2 = lax.fori_loop(0, CX, body, (hz[...], zero8, zero8, zero8))
        s_ez[n] = low
        if n < STEPS - 1:
            s_uz[n, 0] = high
            s_uz[n, 1] = high2

    def electric_moves(n):
        moves = [
            Move(n, 0, (-1, 0, 0), es.at[pl.ds(1, 2), 0, pl.ds(0, CY), :], r_ex.at[n]),
            Move(n, 1, (0, -1, 0), s_ey.at[n], r_ey.at[n]),
            Move(n, 2, (0, 0, -1), s_ez.at[n], r_ez.at[n]),
        ]
        if n == STEPS - 1:
            return moves
        sources = (s_ez.at[n], s_uz.at[n, 1], es.at[0, CX - 1, pl.ds(0, 8), :], es.at[1, 0, pl.ds(CY - 8, 8), :], s_ez.at[n], s_uz.at[n, 1])
        edges = [Move(n, 6 + k, off, sources[k], r_edge.at[k, n]) for k, off in enumerate(EDGES)]
        return [
            edges[2], edges[3],
            Move(n, 3, (1, 0, 0), es.at[:, CX - 1, pl.ds(0, CY), :], r_ux.at[n]),
            moves[0],
            Move(n, 4, (0, 1, 0), s_uy.at[n], r_uy.at[n]),
            moves[1], edges[0], edges[1], edges[4], edges[5],
            Move(n, 5, (0, 0, 1), s_uz.at[n], r_uz.at[n]),
            moves[2],
        ]

    def below_phase(n):
        e0, e1, e2 = r_ux[n, 0], r_ux[n, 1], r_ux[n, 2]
        e0z = jnp.where(lane32 == 127, unpack(r_edge[0, n], 60, 127), roll(e0, -1, 1))
        e0y = jnp.where(row32 == CY - 1, r_edge[2, n, 0:1, :], roll(e0, -1, 0))
        h1 = hs[1, 0, 8:8 + CY, :]
        h2 = hs[2, 0, 8:8 + CY, :]
        hs[1, 0, 8:8 + CY, :] = dax[0] * h1 - dax[1] * ((e0z - e0) - (es[2, 0, 0:CY, :] - e2))
        hs[2, 0, 8:8 + CY, :] = dax[0] * h2 - dax[1] * ((es[1, 0, 0:CY, :] - e1) - (e0y - e0))

        e0, e1, e2 = r_uy[n, 0], r_uy[n, 1], r_uy[n, 2]
        corner = jnp.broadcast_to(r_edge[4, n, 7:8, :], (CX, 128))
        corner = jnp.sum(jnp.where(lane16 == 67 + 4 * row16, corner, 0.0), axis=1, keepdims=True)
        e1z = jnp.where(lane16 == 127, corner, roll(e1, -1, 1))
        e1x = jnp.where(row16 == CX - 1, r_edge[3, n, 7:8, :], roll(e1, -1, 0))
        hy[0] = day[0] * hy[0] - day[1] * ((s_ey[n, 1] - e2) - (e1z - e1))
        hy[1] = day[0] * hy[1] - day[1] * ((e1x - e1) - (s_ey[n, 0] - e0))

        e2 = r_uz[n, 1]
        along = roll(s_ez[n] - r_uz[n, 0], 64, 1)
        up = roll(e2, -1, 0)
        up_next = roll(up, -1, 1)
        up_edge = roll(roll(r_edge[5, n], -1, 0), 3, 1)
        e2y = jnp.where(row8 < 7, up, jnp.where(lane8 % 4 == 3, up_edge, up_next))
        e2x = jnp.where(lane8 >= 124, roll(r_edge[1, n], 124, 1), roll(e2, -4, 1))
        curl = jnp.where(lane8 < 64, (e2y - e2) - along, along - (e2x - e2))
        hz[...] = daz[0] * hz[...] - daz[1] * curl

    def magnetic_phase(n):
        es[1, CX, 0:CY, :] = r_ex[n, 0]
        es[2, CX, 0:CY, :] = r_ex[n, 1]

        def body(x, halo):
            es[0, x, CY:CY + 1, :] = r_ey[n, 0, pl.ds(x, 1), :]
            es[2, x, CY:CY + 1, :] = r_ey[n, 1, pl.ds(x, 1), :]
            e0 = es[0, x, 0:CY, :]
            e1 = es[1, x, 0:CY, :]
            e2 = es[2, x, 0:CY, :]
            e0y = es[0, x, 1:1 + CY, :]
            e2y = es[2, x, 1:1 + CY, :]
            e1x = es[1, x + 1, 0:CY, :]
            e2x = es[2, x + 1, 0:CY, :]
            e0z = jnp.where(lane32 == 127, unpack(halo, 0, 127), roll(e0, -1, 1))
            e1z = jnp.where(lane32 == 127, unpack(halo, 64, 127), roll(e1, -1, 1))
            decay, drive = da[x], db[x]
            hs[0, x + 1, 8:8 + CY, :] = decay * hs[0, x + 1, 8:8 + CY, :] - drive * ((e2y - e2) - (e1z - e1))
            hs[1, x + 1, 8:8 + CY, :] = decay * hs[1, x + 1, 8:8 + CY, :] - drive * ((e0z - e0) - (e2x - e2))
            hs[2, x + 1, 8:8 + CY, :] = decay * hs[2, x + 1, 8:8 + CY, :] - drive * ((e1x - e1) - (e0y - e0))
            return roll(halo, -4, 1)

        lax.fori_loop(0, CX, body, r_ez[n])

    def extract_planes(n):
        weights = []
        for c in range(3):
            weight = jnp.zeros((16, 128), F32)
            for p in range(MON):
                weight = jnp.where((row16 == 3 * p + c) & (lane16 + slab * CZ == monitor[p]), 1.0, weight)
            weights.append(weight.astype(jnp.bfloat16))
        planes[n, slab, 32:40, :] = zero8

        for k in range(CX // 4):
            total = jnp.zeros((16, 128), F32)
            for c in range(3):
                rest = es[c, 4 * k:4 * k + 4, 0:CY, :].reshape(128, 128)
                for _ in range(3):
                    piece = rest.astype(jnp.bfloat16)
                    rest = rest - piece.astype(F32)
                    total = total + lax.dot_general(
                        weights[c], piece, (((1,), (1,)), ((), ())), preferred_element_type=F32)
            planes[n, slab, 8 * k:8 * k + 8, :] = total[0:8]
            planes[n, slab, 32 + k:33 + k, :] = total[8:9]

    def plane_move(n, i):
        return pltpu.make_async_remote_copy(
            src_ref=planes.at[n, slab], dst_ref=planes.at[n, slab],
            send_sem=plane_send.at[n, i - 1], recv_sem=plane_recv.at[n, i - 1],
            device_id=(tile, (slab + i) % SLABS), device_id_type=MESH)

    def plane_arrival(n, i):
        source = (slab + SLABS - i) % SLABS
        return pltpu.make_async_remote_copy(
            src_ref=planes.at[n, source], dst_ref=planes.at[n, source],
            send_sem=plane_send.at[n, i - 1], recv_sem=plane_recv.at[n, i - 1],
            device_id=(tile, (slab + i) % SLABS), device_id_type=MESH)

    def accumulate(n):
        for i in range(1, SLABS):
            plane_arrival(n, i).wait_recv()
        for k in range(5):
            whole = planes[n, 0, 8 * k:8 * k + 8, :]
            for g in range(1, SLABS):
                whole = whole + planes[n, g, 8 * k:8 * k + 8, :]
            for q in range(2):
                for w in range(WAVES):
                    acc[q, w, k] = acc[q, w, k] + trig[q, w, n] * whole

    for n in range(STEPS):
        electric_phase(n)
        moves = electric_moves(n)
        for move in moves:
            move.start()
        extract_planes(n)
        for i in range(1, SLABS):
            plane_move(n, i).start()
        if n == STEPS - 1:
            break
        if n:
            accumulate(n - 1)
        for move in moves:
            move.wait_recv()
        magnetic_phase(n)
        below_phase(n)
        for move in moves:
            move.wait_send()

    stores = [pltpu.make_async_copy(
        es.at[k, pl.ds(0, CX), pl.ds(0, CY), :], e_out.at[0, k], local_sem.at[7 + k]) for k in range(3)]
    for store in stores:
        store.start()
    accumulate(STEPS - 2)
    accumulate(STEPS - 1)

    part = jnp.zeros((1, 128), F32)
    odd = jnp.zeros((8, 128), F32)
    for w in range(WAVES):
        odd = odd + (acc[0, w, 4] * acc[0, w, 4] + acc[1, w, 4] * acc[1, w, 4])
    for k in range(4):
        power = jnp.zeros((8, 128), F32)
        for w in range(WAVES):
            power = power + (acc[0, w, k] * acc[0, w, k] + acc[1, w, k] * acc[1, w, k])
        power = jnp.sum(power, axis=0, keepdims=True) + odd[k:k + 1]
        part = part + power * focus[0:1, 128 * k:128 * k + 128]

    def total_moves(stage, count, mine, where):
        buf = (first, second)[stage]

        def one(slot, i):
            return pltpu.make_async_remote_copy(
                src_ref=buf.at[pl.ds(slot, 1), :], dst_ref=buf.at[pl.ds(slot, 1), :],
                send_sem=total_send.at[stage, i], recv_sem=total_recv.at[stage, i],
                device_id=where(i), device_id_type=MESH)

        return ([one(mine, i) for i in range(1, count)],
                [one((mine + count - i) % count, i) for i in range(1, count)])

    first[pl.ds(col, 1), :] = part
    out1, in1 = total_moves(0, TILES_Y, col, lambda i: (row * TILES_Y + (col + i) % TILES_Y, slab))
    for move in out1:
        move.start()

    for q in range(2):
        for w in range(WAVES):
            base = 36 * q + 9 * w
            for k in range(4):
                spec[0, base:base + 8, 128 * k:128 * k + 128] = acc[q, w, k]
                spec[0, base + 8:base + 9, 128 * k:128 * k + 128] = acc[q, w, 4, k:k + 1, :]

    for move in moves:
        move.wait_recv()
    magnetic_phase(STEPS - 1)
    for k in range(3):
        stores.append(pltpu.make_async_copy(
            hs.at[k, pl.ds(1, CX), pl.ds(8, CY), :], h_out.at[0, k], local_sem.at[10 + k]))
        stores[-1].start()

    for move in in1:
        move.wait_recv()
    second[pl.ds(row, 1), :] = jnp.sum(first[0:TILES_Y, :], axis=0, keepdims=True)
    out2, in2 = total_moves(1, TILES_X, row, lambda i: ((row + i) % TILES_X * TILES_Y + col, slab))
    for move in out2:
        move.start()
    for move in moves:
        move.wait_send()
    for n in range(STEPS):
        for i in range(1, SLABS):
            plane_move(n, i).wait_send()
    for move in out1:
        move.wait_send()
    for store in stores:
        store.wait()
    for move in in2:
        move.wait_recv()
    for move in out2:
        move.wait_send()
    cells = TILES_X * TILES_Y * WAVES * MON * 3 * CX * CY
    objective[0] = jnp.sum(second[0:TILES_X, :]) / jnp.float32(cells)


def step(e_field, h_field, material, permittivity, pml_x, pml_y, pml_z, monitor_z, omega, focus):
    vmem = lambda *shape: pltpu.VMEM(shape, F32)
    dma = lambda *shape: pltpu.SemaphoreType.DMA(shape)
    anywhere = pl.BlockSpec(memory_space=pl.ANY)
    smem = pl.BlockSpec(memory_space=pltpu.SMEM)
    inside = pl.BlockSpec(memory_space=pltpu.VMEM)
    early = STEPS - 1
    e_out, h_out, spectra, objective = pl.pallas_call(
        kernel,
        out_shape=(
            jax.ShapeDtypeStruct(e_field.shape, F32),
            jax.ShapeDtypeStruct(h_field.shape, F32),
            jax.ShapeDtypeStruct((1, 2 * WAVES * MON * 3, CX * CY), F32),
            jax.ShapeDtypeStruct((1,), F32),
        ),
        in_specs=[anywhere] * 3 + [inside] + [smem] * 6,
        out_specs=(anywhere, anywhere, inside, smem),
        scratch_shapes=[
            vmem(3, CX + 1, CY + 8, CZ), vmem(3, CX + 1, CY + 8, CZ), pltpu.VMEM((CX, CY, CZ), jnp.int32),
            vmem(CX, CY, CZ), vmem(CX, CY, CZ), vmem(CX, CY, CZ), vmem(CX, CY, CZ),
            vmem(CX, 128), vmem(CY, 128),
            vmem(2, WAVES, STEPS, 8, 128), vmem(2, WAVES, 5, 8, 128), vmem(STEPS, SLABS, 40, 128),
            vmem(8, 128), vmem(8, 128),
            vmem(2, CX, 128), vmem(8, 128), vmem(2, CY, 128), vmem(2, CX, 128), vmem(2, 8, 128),
            vmem(2, CX, 128), vmem(8, 128), vmem(2, CY, 128), vmem(2, CX, 128), vmem(8, 128),
            vmem(STEPS, 2, CX, 128), vmem(STEPS, 8, 128),
            vmem(STEPS, 2, CY, 128), vmem(STEPS, 2, CX, 128), vmem(STEPS, 8, 128),
            vmem(early, 3, CX, 128), vmem(early, 2, 8, 128),
            vmem(early, 3, CY, 128), vmem(early, 3, CX, 128), vmem(early, 2, 8, 128),
            vmem(6, early, 8, 128),
            dma(13), dma(STEPS + 1, 12), dma(STEPS + 1, 12),
            dma(STEPS, SLABS), dma(STEPS, SLABS), dma(2, 8), dma(2, 8),
        ],
        compiler_params=pltpu.CompilerParams(
            collective_id=0, has_side_effects=True, vmem_limit_bytes=32 * 1024 * 1024),
    )(e_field, h_field, material, focus, permittivity, pml_x, pml_y, pml_z, monitor_z, omega)
    return e_out, h_out, spectra, objective.reshape(())


def solution(mesh):
    field = P("xy", None, None, None, "gz")
    return jax.shard_map(
        step,
        mesh=mesh,
        in_specs=(field, field, P("xy", None, None, "gz"), P(), P(), P(), P(), P(), P(), P("xy", None)),
        out_specs=(field, field, P("xy", None, None), P()),
        check_vma=False,
    )
```

```python
import functools

import jax
import jax.numpy as jnp
from jax import lax
from jax.experimental import pallas as pl
from jax.experimental.pallas import tpu as pltpu
from jax.sharding import PartitionSpec as P

MESH = pl.DeviceIdType.MESH
TILES_X = 8
TILES_Y = 8
SLABS = 4
STEPS = 4
WAVES = 4
MON = 3
DEPTH = 8
TIME_STEP = 0.5
SIGMA_PEAK = 0.8
CX, CY, CZ = 16, 32, 128
F32 = jnp.float32
EDGES = ((1, 0, -1), (-1, 0, 1), (1, -1, 0), (-1, 1, 0), (0, 1, -1), (0, -1, 1))


def roll(value, shift, axis):
    return pltpu.roll(value, shift % value.shape[axis], axis)


def grade(level):
    scaled = level.astype(F32) / DEPTH
    return scaled * scaled


def magnetic(sigma):
    loss = sigma * (0.5 * TIME_STEP)
    return (1.0 - loss) / (1.0 + loss), TIME_STEP / (1.0 + loss)


def electric(sigma, permit):
    loss = sigma * (0.5 * TIME_STEP) / permit
    return (1.0 - loss) / (1.0 + loss), TIME_STEP / (permit * (1.0 + loss))


def kernel(
    e_in, h_in, m_in, focus, permit, pml_x, pml_y, pml_z, monitor, omega,
    e_out, h_out, spec, objective,
    es, hs, kinds, ca, cb, da, db, grades_x, grades_y, trig, acc, planes, first, second,
    hy, hz, dax, day, daz, dby, dbz,
    s_hy, s_hz, r_hx, r_hy, r_hz,
    s_ey, s_ez, r_ex, r_ey, r_ez,
    s_uy, s_uz, r_ux, r_uy, r_uz, r_edge,
    local_sem, send_sem, recv_sem, plane_send, plane_recv, total_send, total_recv,
):
    tile = lax.axis_index("xy")
    slab = lax.axis_index("gz")
    row, col = tile // TILES_Y, tile % TILES_Y
    half, core = slab // 2, slab % 2

    def valid(off):
        r, c, g = row + off[0], col + off[1], slab + off[2]
        return (r >= 0) & (r < TILES_X) & (c >= 0) & (c < TILES_Y) & (g >= 0) & (g < SLABS)

    def device(off):
        return ((row + off[0]) * TILES_Y + col + off[1], slab + off[2])

    def minus(off):
        return tuple(-o for o in off)

    class Move:
        def __init__(self, n, k, off, src, dst):
            self.off = off
            self.copy = lambda: pltpu.make_async_remote_copy(
                src_ref=src, dst_ref=dst, send_sem=send_sem.at[n, k], recv_sem=recv_sem.at[n, k],
                device_id=device(off), device_id_type=MESH)

        def start(self):
            @pl.when(valid(self.off))
            def _():
                self.copy().start()

        def wait_send(self):
            @pl.when(valid(self.off))
            def _():
                self.copy().wait_send()

        def wait_recv(self):
            @pl.when(valid(minus(self.off)))
            def _():
                self.copy().wait_recv()

    barrier = pltpu.get_barrier_semaphore()

    def greet(where):
        pl.semaphore_signal(barrier, inc=1, device_id=where, device_id_type=MESH)

    def in_row(i):
        k = (col * 2 + core + i) % (2 * TILES_Y)
        return row * TILES_Y + k // 2, half * 2 + k % 2

    def in_column(i):
        k = (row * 2 + half + i) % (2 * TILES_X)
        return k // 2 * TILES_Y + col, k % 2 * 2 + core

    for i in range(1, 2 * TILES_Y):
        greet(in_row(i))
    for i in range(1, 2 * TILES_X):
        greet(in_column(i))
    greet((tile, SLABS - 1 - slab))
    for off in EDGES:
        @pl.when(valid(off))
        def _(off=off):
            greet(device(off))

    loads = []
    for k in range(3):
        loads.append(pltpu.make_async_copy(
            h_in.at[0, k], hs.at[k, pl.ds(1, CX), pl.ds(8, CY), :], local_sem.at[k]))
    loads.append(pltpu.make_async_copy(m_in.at[0], kinds, local_sem.at[3]))
    for k in range(3):
        loads.append(pltpu.make_async_copy(
            e_in.at[0, k], es.at[k, pl.ds(0, CX), pl.ds(0, CY), :], local_sem.at[4 + k]))
    for load in loads:
        load.start()

    lane8 = lax.broadcasted_iota(jnp.int32, (8, 128), 1)
    row8 = lax.broadcasted_iota(jnp.int32, (8, 128), 0)
    lane16 = lax.broadcasted_iota(jnp.int32, (16, 128), 1)
    row16 = lax.broadcasted_iota(jnp.int32, (16, 128), 0)
    lane32 = lax.broadcasted_iota(jnp.int32, (CY, 128), 1)
    row32 = lax.broadcasted_iota(jnp.int32, (CY, 128), 0)
    zero8 = jnp.zeros((8, 128), F32)

    def clear(off, *refs):
        @pl.when(jnp.logical_not(valid(minus(off))))
        def _():
            for ref in refs:
                ref[...] = jnp.zeros(ref.shape, F32)

    clear((1, 0, 0), r_hx, r_ux)
    clear((0, 1, 0), r_hy, r_uy)
    clear((0, 0, 1), r_hz, r_uz)
    clear((-1, 0, 0), r_ex)
    clear((0, -1, 0), r_ey)
    clear((0, 0, -1), r_ez)
    for k, off in enumerate(EDGES):
        clear(off, r_edge.at[k])

    def pack(total, field, source, start):
        for k in range(CY // 8):
            piece = roll(field[8 * k:8 * k + 8], start + k - source, 1)
            total = jnp.where(lane8 == start + k, piece, total)
        return total

    def unpack(packed, start, target):
        return jnp.concatenate([roll(packed, target - start - k, 1) for k in range(CY // 8)], axis=0)

    for k in range(3):
        loads[k].wait()

    total = zero8
    for x in range(CX):
        s_hy[0, x:x + 1, :] = hs[0, x + 1, 7 + CY:8 + CY, :]
        s_hy[1, x:x + 1, :] = hs[2, x + 1, 7 + CY:8 + CY, :]
        total = pack(total, hs[0, x + 1, 8:8 + CY, :], 127, 4 * x)
        total = pack(total, hs[1, x + 1, 8:8 + CY, :], 127, 64 + 4 * x)
    s_hz[...] = total

    greeted = 2 * TILES_Y - 1 + 2 * TILES_X - 1 + 1
    for off in EDGES:
        greeted = greeted + jnp.where(valid(off), 1, 0)
    pl.semaphore_wait(barrier, greeted)

    opening = [
        Move(STEPS, 0, (1, 0, 0), hs.at[pl.ds(1, 2), CX, pl.ds(8, CY), :], r_hx),
        Move(STEPS, 1, (0, 1, 0), s_hy, r_hy),
        Move(STEPS, 2, (0, 0, 1), s_hz, r_hz),
    ]
    for move in opening:
        move.start()

    for i in range(CX):
        grades_x[i:i + 1, :] = jnp.full((1, 128), grade(pml_x[row * CX + i]), F32)
    for j in range(CY):
        grades_y[j:j + 1, :] = jnp.full((1, 128), grade(pml_y[col * CY + j]), F32)

    def lay(k, levels):
        return jnp.where(lane8 == k, pml_z[slab * CZ + k], levels)

    along_z = grade(lax.fori_loop(0, CZ, lay, jnp.zeros((8, 128), jnp.int32)))
    along_z32 = jnp.concatenate([along_z] * 4, axis=0)

    loads[3].wait()

    def fill(x, _):
        g = jnp.full((CY, 128), grade(pml_x[row * CX + x]), F32)
        sigma = SIGMA_PEAK * ((g + grades_y[...]) + along_z32)
        kind = kinds[x]
        eps = jnp.full((CY, 128), permit[0], F32)
        for which in range(1, 4):
            eps = jnp.where(kind == which, permit[which], eps)
        ca[x], cb[x] = electric(sigma, eps)
        da[x], db[x] = magnetic(sigma)
        return 0

    lax.fori_loop(0, CX, fill, 0)
    total = zero8
    for x in range(CX):
        dby[x:x + 1, :] = db[x, CY - 1:CY, :]
        total = pack(total, db[x], 127, 4 * x)
    dbz[...] = total + roll(total, 64, 1)
    for k in (1, 2):
        es[k, CX, 0:CY, :] = jnp.zeros((CY, 128), F32)
    for x in range(CX):
        es[0, x, CY:CY + 1, :] = jnp.zeros((1, 128), F32)
        es[2, x, CY:CY + 1, :] = jnp.zeros((1, 128), F32)

    def below(ref, off, sigma):
        inside = jnp.where(valid(off), 1.0, 0.0).astype(F32)
        decay, drive = magnetic(sigma)
        ref[0] = decay * inside
        ref[1] = drive * inside

    g = grade(pml_x[jnp.maximum(row * CX - 1, 0)])
    below(dax, (-1, 0, 0), SIGMA_PEAK * ((g + grades_y[...]) + along_z32))
    g = grade(pml_y[jnp.maximum(col * CY - 1, 0)])
    below(day, (0, -1, 0), SIGMA_PEAK * ((grades_x[...] + g) + along_z32[0:CX]))
    g = grade(pml_z[jnp.maximum(slab * CZ - 1, 0)])
    packed_x = zero8
    for i in range(CX):
        packed_x = jnp.where((lane8 % 64) // 4 == i, grades_x[i:i + 1, :], packed_x)
    packed_y = zero8
    for k in range(CY // 8):
        packed_y = jnp.where(lane8 % 4 == k, grades_y[8 * k:8 * k + 8, :], packed_y)
    below(daz, (0, 0, -1), SIGMA_PEAK * ((packed_x + packed_y) + g))

    for n in range(STEPS):
        for w in range(WAVES):
            phase = jnp.full((8, 128), omega[w] * ((n + 1) * TIME_STEP), F32)
            trig[0, w, n] = jnp.cos(phase)
            trig[1, w, n] = -jnp.sin(phase)
    acc[...] = jnp.zeros(acc.shape, F32)

    for k in range(3):
        loads[4 + k].wait()
    for move in opening:
        move.wait_recv()
    hs[1, 0, 8:8 + CY, :] = r_hx[0]
    hs[2, 0, 8:8 + CY, :] = r_hx[1]
    hy[...] = r_hy[...]
    hz[...] = r_hz[...]
    for move in opening:
        move.wait_send()

    def electric_planes(n, where, last, packs):
        for x in where:
            hs[0, x + 1, 7:8, :] = hy[0, x:x + 1, :]
            hs[2, x + 1, 7:8, :] = hy[1, x:x + 1, :]
        halo = hz[...]
        low, high, high2 = packs
        for x in where:
            h0 = hs[0, x + 1, 8:8 + CY, :]
            h1 = hs[1, x + 1, 8:8 + CY, :]
            h2 = hs[2, x + 1, 8:8 + CY, :]
            h0y = hs[0, x + 1, 7:7 + CY, :]
            h2y = hs[2, x + 1, 7:7 + CY, :]
            h1x = hs[1, x, 8:8 + CY, :]
            h2x = hs[2, x, 8:8 + CY, :]
            h0z = jnp.where(lane32 == 0, unpack(halo, 4 * x, 0), roll(h0, 1, 1))
            h1z = jnp.where(lane32 == 0, unpack(halo, 64 + 4 * x, 0), roll(h1, 1, 1))
            decay, drive = ca[x], cb[x]
            e0 = decay * es[0, x, 0:CY, :] + drive * ((h2 - h2y) - (h1 - h1z))
            e1 = decay * es[1, x, 0:CY, :] + drive * ((h0 - h0z) - (h2 - h2x))
            e2 = decay * es[2, x, 0:CY, :] + drive * ((h1 - h1x) - (h0 - h0y))
            es[0, x, 0:CY, :] = e0
            es[1, x, 0:CY, :] = e1
            es[2, x, 0:CY, :] = e2
            s_ey[n, 0, x:x + 1, :] = e0[0:1]
            s_ey[n, 1, x:x + 1, :] = e2[0:1]
            low = pack(pack(low, e0, 0, 4 * x), e1, 0, 64 + 4 * x)
            if not last:
                for k, e in enumerate((e0, e1, e2)):
                    s_uy[n, k, x:x + 1, :] = e[CY - 1:CY]
                high = pack(pack(high, e0, 127, 4 * x), e1, 127, 64 + 4 * x)
                high2 = pack(pack(high2, e2, 127, 4 * x), e2, 127, 64 + 4 * x)
        return low, high, high2

    def electric_phase(n, last):
        first_moves = [Move(n, 0, (-1, 0, 0), es.at[pl.ds(1, 2), 0, pl.ds(0, CY), :], r_ex.at[n])]
        moves = [
            Move(n, 1, (0, -1, 0), s_ey.at[n], r_ey.at[n]),
            Move(n, 2, (0, 0, -1), s_ez.at[n], r_ez.at[n]),
        ]
        if not last:
            sources = (s_ez.at[n], s_uz.at[n, 1], es.at[0, CX - 1, pl.ds(0, 8), :],
                       es.at[1, 0, pl.ds(CY - 8, 8), :], s_ez.at[n], s_uz.at[n, 1])
            edges = [Move(n, 6 + k, off, sources[k], r_edge.at[k, n]) for k, off in enumerate(EDGES)]
            first_moves = edges[2:4] + [
                Move(n, 3, (1, 0, 0), es.at[:, CX - 1, pl.ds(0, CY), :], r_ux.at[n])] + first_moves
            moves = [moves[0], Move(n, 4, (0, 1, 0), s_uy.at[n], r_uy.at[n])] + edges[0:2] + edges[4:6] + [
                moves[1], Move(n, 5, (0, 0, 1), s_uz.at[n], r_uz.at[n])]
        packs = electric_planes(n, (0,) if last else (0, CX - 1), last, (zero8, zero8, zero8))
        for move in first_moves:
            move.start()
        low, high, high2 = electric_planes(n, range(1, CX if last else CX - 1), last, packs)
        s_ez[n] = low
        if not last:
            s_uz[n, 0] = high
            s_uz[n, 1] = high2
        for move in moves:
            move.start()
        return first_moves + moves

    def below_phase(n):
        e0, e1, e2 = r_ux[n, 0], r_ux[n, 1], r_ux[n, 2]
        e0z = jnp.where(lane32 == 127, unpack(r_edge[0, n], 60, 127), roll(e0, -1, 1))
        e0y = jnp.where(row32 == CY - 1, r_edge[2, n, 0:1, :], roll(e0, -1, 0))
        h1 = hs[1, 0, 8:8 + CY, :]
        h2 = hs[2, 0, 8:8 + CY, :]
        hs[1, 0, 8:8 + CY, :] = dax[0] * h1 - dax[1] * ((e0z - e0) - (es[2, 0, 0:CY, :] - e2))
        hs[2, 0, 8:8 + CY, :] = dax[0] * h2 - dax[1] * ((es[1, 0, 0:CY, :] - e1) - (e0y - e0))

        e0, e1, e2 = r_uy[n, 0], r_uy[n, 1], r_uy[n, 2]
        corner = jnp.broadcast_to(r_edge[4, n, 7:8, :], (CX, 128))
        corner = jnp.sum(jnp.where(lane16 == 67 + 4 * row16, corner, 0.0), axis=1, keepdims=True)
        e1z = jnp.where(lane16 == 127, corner, roll(e1, -1, 1))
        e1x = jnp.where(row16 == CX - 1, r_edge[3, n, 7:8, :], roll(e1, -1, 0))
        hy[0] = day[0] * hy[0] - day[1] * ((s_ey[n, 1] - e2) - (e1z - e1))
        hy[1] = day[0] * hy[1] - day[1] * ((e1x - e1) - (s_ey[n, 0] - e0))

        e2 = r_uz[n, 1]
        along = roll(s_ez[n] - r_uz[n, 0], 64, 1)
        up = roll(e2, -1, 0)
        up_next = roll(up, -1, 1)
        up_edge = roll(roll(r_edge[5, n], -1, 0), 3, 1)
        e2y = jnp.where(row8 < 7, up, jnp.where(lane8 % 4 == 3, up_edge, up_next))
        e2x = jnp.where(lane8 >= 124, roll(r_edge[1, n], 124, 1), roll(e2, -4, 1))
        curl = jnp.where(lane8 < 64, (e2y - e2) - along, along - (e2x - e2))
        hz[...] = daz[0] * hz[...] - daz[1] * curl

    def magnetic_phase():
        for x in range(CX):
            e0 = es[0, x, 0:CY, :]
            e1 = es[1, x, 0:CY, :]
            e2 = es[2, x, 0:CY, :]
            e0y = es[0, x, 1:1 + CY, :]
            e2y = es[2, x, 1:1 + CY, :]
            e1x = es[1, x + 1, 0:CY, :]
            e2x = es[2, x + 1, 0:CY, :]
            e0z = jnp.where(lane32 == 127, 0.0, roll(e0, -1, 1))
            e1z = jnp.where(lane32 == 127, 0.0, roll(e1, -1, 1))
            decay, drive = da[x], db[x]
            h0 = decay * hs[0, x + 1, 8:8 + CY, :] - drive * ((e2y - e2) - (e1z - e1))
            h1 = decay * hs[1, x + 1, 8:8 + CY, :] - drive * ((e0z - e0) - (e2x - e2))
            h2 = decay * hs[2, x + 1, 8:8 + CY, :] - drive * ((e1x - e1) - (e0y - e0))
            hs[0, x + 1, 8:8 + CY, :] = h0
            hs[1, x + 1, 8:8 + CY, :] = h1
            hs[2, x + 1, 8:8 + CY, :] = h2

    def above_phase(n):
        drive = db[CX - 1]
        hs[1, CX, 8:8 + CY, :] = hs[1, CX, 8:8 + CY, :] + drive * r_ex[n, 1]
        hs[2, CX, 8:8 + CY, :] = hs[2, CX, 8:8 + CY, :] - drive * r_ex[n, 0]
        term0 = dby[...] * r_ey[n, 1]
        term2 = dby[...] * r_ey[n, 0]
        for x in range(CX):
            hs[0, x + 1, 7 + CY:8 + CY, :] = hs[0, x + 1, 7 + CY:8 + CY, :] - term0[x:x + 1]
            hs[2, x + 1, 7 + CY:8 + CY, :] = hs[2, x + 1, 7 + CY:8 + CY, :] + term2[x:x + 1]
        terms = dbz[...] * r_ez[n]
        for x in range(CX):
            hs[0, x + 1, 8:8 + CY, :] = hs[0, x + 1, 8:8 + CY, :] + jnp.where(
                lane32 == 127, unpack(terms, 64 + 4 * x, 127), 0.0)
            hs[1, x + 1, 8:8 + CY, :] = hs[1, x + 1, 8:8 + CY, :] - jnp.where(
                lane32 == 127, unpack(terms, 4 * x, 127), 0.0)

    def extract_planes(n):
        weights = []
        for c in range(3):
            weight = jnp.zeros((16, 128), F32)
            for p in range(MON):
                weight = jnp.where((row16 == 3 * p + c) & (lane16 + slab * CZ == monitor[p]), 1.0, weight)
            weights += [weight.astype(jnp.bfloat16)] * 3
        weights = jnp.concatenate(weights, axis=1)
        planes[n, slab, 32:40, :] = zero8
        for k in range(0, CX // 4, 2):
            pieces = []
            for c in range(3):
                rest = es[c, 4 * k:4 * k + 8, 0:CY, :].reshape(256, 128)
                for _ in range(3):
                    pieces.append(rest.astype(jnp.bfloat16))
                    rest = rest - pieces[-1].astype(F32)
            total = lax.dot_general(weights, jnp.concatenate(pieces, axis=1), (((1,), (1,)), ((), ())),
                                    preferred_element_type=F32)
            for j in range(2):
                part = total[:, 128 * j:128 * j + 128]
                planes[n, slab, 8 * (k + j):8 * (k + j) + 8, :] = part[0:8]
                planes[n, slab, 32 + k + j:33 + k + j, :] = part[8:9]
        for k in range(5):
            whole = planes[n, slab, 8 * k:8 * k + 8, :]
            for q in range(2):
                for w in range(WAVES):
                    acc[q, w, k] = acc[q, w, k] + trig[q, w, n] * whole

    def plane_move(n, i):
        return pltpu.make_async_remote_copy(
            src_ref=planes.at[n, slab], dst_ref=planes.at[n, slab],
            send_sem=plane_send.at[n, i - 1], recv_sem=plane_recv.at[n, i - 1],
            device_id=(tile, (slab + i) % SLABS), device_id_type=MESH)

    def plane_arrival(n, i):
        source = (slab + SLABS - i) % SLABS
        return pltpu.make_async_remote_copy(
            src_ref=planes.at[n, source], dst_ref=planes.at[n, source],
            send_sem=plane_send.at[n, i - 1], recv_sem=plane_recv.at[n, i - 1],
            device_id=(tile, (slab + i) % SLABS), device_id_type=MESH)

    def full_step(n, carry):
        moves = electric_phase(n, False)
        extract_planes(n)
        for i in range(1, SLABS):
            plane_move(n, i).start()
        magnetic_phase()
        for move in moves:
            move.wait_send()
        for move in moves:
            move.wait_recv()
        above_phase(n)
        below_phase(n)
        return carry

    lax.fori_loop(0, STEPS - 1, full_step, 0)
    moves = electric_phase(STEPS - 1, True)
    extract_planes(STEPS - 1)
    for i in range(1, SLABS):
        plane_move(STEPS - 1, i).start()

    part = jnp.zeros((1, 128), F32)
    odd = zero8
    for w in range(WAVES):
        odd = odd + (acc[0, w, 4] * acc[0, w, 4] + acc[1, w, 4] * acc[1, w, 4])
    for k in range(4):
        power = zero8
        for w in range(WAVES):
            power = power + (acc[0, w, k] * acc[0, w, k] + acc[1, w, k] * acc[1, w, k])
        power = jnp.sum(power, axis=0, keepdims=True) + odd[k:k + 1]
        part = part + power * focus[0:1, 128 * k:128 * k + 128]

    def total_moves(stage, count, mine, where):
        buf = (first, second)[stage]

        def one(slot, i):
            return pltpu.make_async_remote_copy(
                src_ref=buf.at[pl.ds(slot, 1), :], dst_ref=buf.at[pl.ds(slot, 1), :],
                send_sem=total_send.at[stage, i], recv_sem=total_recv.at[stage, i],
                device_id=where(i), device_id_type=MESH)

        order = sorted(range(1, count), key=lambda i: -min(i, count - i))
        return ([one(mine, i) for i in order],
                [one((mine + count - i) % count, i) for i in order])

    first[pl.ds(col * 2 + core, 1), :] = part
    out1, in1 = total_moves(0, 2 * TILES_Y, col * 2 + core, in_row)
    for move in out1:
        move.start()

    stores = [pltpu.make_async_copy(
        es.at[k, pl.ds(0, CX), pl.ds(0, CY), :], e_out.at[0, k], local_sem.at[7 + k]) for k in range(3)]
    for store in stores:
        store.start()
    magnetic_phase()
    for move in moves:
        move.wait_send()
    for move in moves:
        move.wait_recv()
    above_phase(STEPS - 1)
    for k in range(3):
        stores.append(pltpu.make_async_copy(
            hs.at[k, pl.ds(1, CX), pl.ds(8, CY), :], h_out.at[0, k], local_sem.at[10 + k]))
        stores[-1].start()

    for move in in1:
        move.wait_recv()
    second[pl.ds(row * 2 + half, 1), :] = jnp.sum(first[...], axis=0, keepdims=True)
    out2, in2 = total_moves(1, 2 * TILES_X, row * 2 + half, in_column)
    for move in out2:
        move.start()

    for n in range(STEPS):
        for i in range(1, SLABS):
            plane_arrival(n, i).wait_recv()
    for k in range(5):
        spectrum = [[zero8] * WAVES, [zero8] * WAVES]
        for n in range(STEPS):
            whole = planes[n, 0, 8 * k:8 * k + 8, :]
            for g in range(1, SLABS):
                whole = whole + planes[n, g, 8 * k:8 * k + 8, :]
            for q in range(2):
                for w in range(WAVES):
                    spectrum[q][w] = spectrum[q][w] + trig[q, w, n] * whole
        for q in range(2):
            for w in range(WAVES):
                base = 36 * q + 9 * w
                if k < 4:
                    spec[0, base:base + 8, 128 * k:128 * k + 128] = spectrum[q][w]
                else:
                    for j in range(4):
                        spec[0, base + 8:base + 9, 128 * j:128 * j + 128] = spectrum[q][w][j:j + 1]

    for n in range(STEPS):
        for i in range(1, SLABS):
            plane_move(n, i).wait_send()
    for move in out1:
        move.wait_send()
    for store in stores:
        store.wait()
    for move in in2:
        move.wait_recv()
    for move in out2:
        move.wait_send()
    cells = TILES_X * TILES_Y * WAVES * MON * 3 * CX * CY
    objective[0] = jnp.sum(second[...]) / jnp.float32(cells)


def hand_on(e_in, h_in, s_in, e_out, h_out, s_out, e_mid, h_mid, s_mid, sem):
    pieces = [(e_in.at[0, k], e_mid.at[k], e_out.at[0, k]) for k in range(3)]
    pieces += [(h_in.at[0, k], h_mid.at[k], h_out.at[0, k]) for k in range(3)]
    pieces += [(s_in, s_mid, s_out)]
    arrive = [pltpu.make_async_copy(a, b, sem.at[0, k]) for k, (a, b, c) in enumerate(pieces)]
    leave = [pltpu.make_async_copy(b, c, sem.at[1, k]) for k, (a, b, c) in enumerate(pieces)]
    for copy in arrive:
        copy.start()
    for before, after in zip(arrive, leave):
        before.wait()
        after.start()
    for copy in leave:
        copy.wait()


def step(e_field, h_field, material, permittivity, pml_x, pml_y, pml_z, monitor_z, omega, focus):
    vmem = lambda *shape: pltpu.VMEM(shape, F32)
    dma = lambda *shape: pltpu.SemaphoreType.DMA(shape)
    anywhere = pl.BlockSpec(memory_space=pl.ANY)
    smem = pl.BlockSpec(memory_space=pltpu.SMEM)
    inside = pl.BlockSpec(memory_space=pltpu.VMEM)
    early = STEPS - 1
    e_out, h_out, spectra, objective = pl.pallas_call(
        kernel,
        out_shape=(
            jax.ShapeDtypeStruct(e_field.shape, F32),
            jax.ShapeDtypeStruct(h_field.shape, F32),
            jax.ShapeDtypeStruct((1, 2 * WAVES * MON * 3, CX * CY), F32),
            jax.ShapeDtypeStruct((1,), F32),
        ),
        in_specs=[anywhere] * 3 + [inside] + [smem] * 6,
        out_specs=(anywhere, anywhere, inside, smem),
        scratch_shapes=[
            vmem(3, CX + 1, CY + 8, CZ), vmem(3, CX + 1, CY + 8, CZ), pltpu.VMEM((CX, CY, CZ), jnp.int32),
            vmem(CX, CY, CZ), vmem(CX, CY, CZ), vmem(CX, CY, CZ), vmem(CX, CY, CZ),
            vmem(CX, 128), vmem(CY, 128),
            vmem(2, WAVES, STEPS, 8, 128), vmem(2, WAVES, 5, 8, 128), vmem(STEPS, SLABS, 40, 128),
            vmem(2 * TILES_Y, 128), vmem(2 * TILES_X, 128),
            vmem(2, CX, 128), vmem(8, 128), vmem(2, CY, 128), vmem(2, CX, 128), vmem(2, 8, 128), vmem(CX, 128), vmem(8, 128),
            vmem(2, CX, 128), vmem(8, 128), vmem(2, CY, 128), vmem(2, CX, 128), vmem(8, 128),
            vmem(STEPS, 2, CX, 128), vmem(STEPS, 8, 128),
            vmem(STEPS, 2, CY, 128), vmem(STEPS, 2, CX, 128), vmem(STEPS, 8, 128),
            vmem(early, 3, CX, 128), vmem(early, 2, 8, 128),
            vmem(early, 3, CY, 128), vmem(early, 3, CX, 128), vmem(early, 2, 8, 128),
            vmem(6, early, 8, 128),
            dma(13), dma(STEPS + 1, 12), dma(STEPS + 1, 12),
            dma(STEPS, SLABS), dma(STEPS, SLABS), dma(2, 16), dma(2, 16),
        ],
        compiler_params=pltpu.CompilerParams(
            collective_id=0, has_side_effects=True, vmem_limit_bytes=60 * 1024 * 1024),
    )(e_field, h_field, material, focus, permittivity, pml_x, pml_y, pml_z, monitor_z, omega)
    e_out, h_out, spectra = pl.pallas_call(
        hand_on,
        out_shape=tuple(jax.ShapeDtypeStruct(a.shape, F32) for a in (e_out, h_out, spectra)),
        in_specs=[anywhere] * 3,
        out_specs=(anywhere,) * 3,
        scratch_shapes=[vmem(3, CX, CY, CZ), vmem(3, CX, CY, CZ), vmem(1, 72, 512), dma(2, 7)],
    )(e_out, h_out, spectra)
    return e_out, h_out, spectra, objective.reshape(())


def solution(mesh):
    field = P("xy", None, None, None, "gz")
    return jax.shard_map(
        step,
        mesh=mesh,
        in_specs=(field, field, P("xy", None, None, "gz"), P(), P(), P(), P(), P(), P(), P("xy", None)),
        out_specs=(field, field, P("xy", None, None), P()),
        check_vma=False,
    )
```

```python
import functools

import jax
import jax.numpy as jnp
from jax import lax
from jax.experimental import pallas as pl
from jax.experimental.pallas import tpu as pltpu
from jax.sharding import PartitionSpec as P

MESH = pl.DeviceIdType.MESH
TILES_X = 8
TILES_Y = 8
SLABS = 4
STEPS = 4
WAVES = 4
MON = 3
DEPTH = 8
TIME_STEP = 0.5
SIGMA_PEAK = 0.8
CX, CY, CZ = 16, 32, 128
F32 = jnp.float32
EDGES = ((1, 0, -1), (-1, 0, 1), (1, -1, 0), (-1, 1, 0), (0, 1, -1), (0, -1, 1))


def roll(value, shift, axis):
    return pltpu.roll(value, shift % value.shape[axis], axis)


def grade(level):
    scaled = level.astype(F32) / DEPTH
    return scaled * scaled


def magnetic(sigma):
    loss = sigma * (0.5 * TIME_STEP)
    return (1.0 - loss) / (1.0 + loss), TIME_STEP / (1.0 + loss)


def electric(sigma, permit):
    loss = sigma * (0.5 * TIME_STEP) / permit
    return (1.0 - loss) / (1.0 + loss), TIME_STEP / (permit * (1.0 + loss))


def kernel(
    e_in, h_in, m_in, focus, permit, pml_x, pml_y, pml_z, monitor, omega,
    e_out, h_out, spec, objective,
    es, hs, kinds, ca, cb, da, db, grades_x, grades_y, trig, acc, planes, first, second,
    hy, hz, dax, day, daz, dby, dbz,
    s_hy, s_hz, r_hx, r_hy, r_hz,
    s_ey, s_ez, r_ex, r_ey, r_ez,
    s_ux, s_uy, s_uz, s_far, top, r_ux, r_uy, r_uz, r_edge,
    local_sem, send_sem, recv_sem, plane_send, plane_recv, total_send, total_recv,
):
    tile = lax.axis_index("xy")
    slab = lax.axis_index("gz")
    row, col = tile // TILES_Y, tile % TILES_Y
    half, core = slab // 2, slab % 2

    def valid(off):
        r, c, g = row + off[0], col + off[1], slab + off[2]
        return (r >= 0) & (r < TILES_X) & (c >= 0) & (c < TILES_Y) & (g >= 0) & (g < SLABS)

    def device(off):
        return ((row + off[0]) * TILES_Y + col + off[1], slab + off[2])

    def minus(off):
        return tuple(-o for o in off)

    class Move:
        def __init__(self, n, k, off, src, dst):
            self.off = off
            self.copy = lambda: pltpu.make_async_remote_copy(
                src_ref=src, dst_ref=dst, send_sem=send_sem.at[n, k], recv_sem=recv_sem.at[n, k],
                device_id=device(off), device_id_type=MESH)

        def start(self):
            @pl.when(valid(self.off))
            def _():
                self.copy().start()

        def wait_send(self):
            @pl.when(valid(self.off))
            def _():
                self.copy().wait_send()

        def wait_recv(self):
            @pl.when(valid(minus(self.off)))
            def _():
                self.copy().wait_recv()

    barrier = pltpu.get_barrier_semaphore()

    def greet(where):
        pl.semaphore_signal(barrier, inc=1, device_id=where, device_id_type=MESH)

    def in_row(i):
        k = (col * 2 + core + i) % (2 * TILES_Y)
        return row * TILES_Y + k // 2, half * 2 + k % 2

    def in_column(i):
        k = (row * 2 + half + i) % (2 * TILES_X)
        return k // 2 * TILES_Y + col, k % 2 * 2 + core

    for i in range(1, 2 * TILES_Y):
        greet(in_row(i))
    for i in range(1, 2 * TILES_X):
        greet(in_column(i))
    greet((tile, SLABS - 1 - slab))
    for off in EDGES:
        @pl.when(valid(off))
        def _(off=off):
            greet(device(off))

    loads = []
    for k in range(3):
        loads.append(pltpu.make_async_copy(
            h_in.at[0, k], hs.at[k, pl.ds(1, CX), pl.ds(8, CY), :], local_sem.at[k]))
    loads.append(pltpu.make_async_copy(m_in.at[0], kinds, local_sem.at[3]))
    for k in range(3):
        loads.append(pltpu.make_async_copy(
            e_in.at[0, k], es.at[k, pl.ds(0, CX), pl.ds(0, CY), :], local_sem.at[4 + k]))
    for load in loads:
        load.start()

    lane8 = lax.broadcasted_iota(jnp.int32, (8, 128), 1)
    row8 = lax.broadcasted_iota(jnp.int32, (8, 128), 0)
    lane16 = lax.broadcasted_iota(jnp.int32, (16, 128), 1)
    row16 = lax.broadcasted_iota(jnp.int32, (16, 128), 0)
    lane32 = lax.broadcasted_iota(jnp.int32, (CY, 128), 1)
    row32 = lax.broadcasted_iota(jnp.int32, (CY, 128), 0)
    zero8 = jnp.zeros((8, 128), F32)

    def clear(off, *refs):
        @pl.when(jnp.logical_not(valid(minus(off))))
        def _():
            for ref in refs:
                ref[...] = jnp.zeros(ref.shape, F32)

    clear((1, 0, 0), r_hx, r_ux)
    clear((0, 1, 0), r_hy, r_uy)
    clear((0, 0, 1), r_hz, r_uz)
    clear((-1, 0, 0), r_ex)
    clear((0, -1, 0), r_ey)
    clear((0, 0, -1), r_ez)
    for k, off in enumerate(EDGES):
        clear(off, r_edge.at[k])

    def pack(total, field, source, start):
        for k in range(CY // 8):
            piece = roll(field[8 * k:8 * k + 8], start + k - source, 1)
            total = jnp.where(lane8 == start + k, piece, total)
        return total

    def unpack(packed, start, target):
        return jnp.concatenate([roll(packed, target - start - k, 1) for k in range(CY // 8)], axis=0)

    for k in range(3):
        loads[k].wait()

    total = zero8
    for x in range(CX):
        s_hy[0, x:x + 1, :] = hs[0, x + 1, 7 + CY:8 + CY, :]
        s_hy[1, x:x + 1, :] = hs[2, x + 1, 7 + CY:8 + CY, :]
        total = pack(total, hs[0, x + 1, 8:8 + CY, :], 127, 4 * x)
        total = pack(total, hs[1, x + 1, 8:8 + CY, :], 127, 64 + 4 * x)
    s_hz[...] = total

    greeted = 2 * TILES_Y - 1 + 2 * TILES_X - 1 + 1
    for off in EDGES:
        greeted = greeted + jnp.where(valid(off), 1, 0)
    pl.semaphore_wait(barrier, greeted)

    opening = [
        Move(STEPS, 0, (1, 0, 0), hs.at[pl.ds(1, 2), CX, pl.ds(8, CY), :], r_hx),
        Move(STEPS, 1, (0, 1, 0), s_hy, r_hy),
        Move(STEPS, 2, (0, 0, 1), s_hz, r_hz),
    ]
    for move in opening:
        move.start()

    for i in range(CX):
        grades_x[i:i + 1, :] = jnp.full((1, 128), grade(pml_x[row * CX + i]), F32)
    for j in range(CY):
        grades_y[j:j + 1, :] = jnp.full((1, 128), grade(pml_y[col * CY + j]), F32)

    def lay(k, levels):
        return jnp.where(lane8 == k, pml_z[slab * CZ + k], levels)

    along_z = grade(lax.fori_loop(0, CZ, lay, jnp.zeros((8, 128), jnp.int32)))
    along_z32 = jnp.concatenate([along_z] * 4, axis=0)

    loads[3].wait()

    def fill(x, _):
        g = jnp.full((CY, 128), grade(pml_x[row * CX + x]), F32)
        sigma = SIGMA_PEAK * ((g + grades_y[...]) + along_z32)
        kind = kinds[x]
        eps = jnp.full((CY, 128), permit[0], F32)
        for which in range(1, 4):
            eps = jnp.where(kind == which, permit[which], eps)
        ca[x], cb[x] = electric(sigma, eps)
        da[x], db[x] = magnetic(sigma)
        return 0

    lax.fori_loop(0, CX, fill, 0)
    total = zero8
    for x in range(CX):
        dby[x:x + 1, :] = db[x, CY - 1:CY, :]
        total = pack(total, db[x], 127, 4 * x)
    dbz[...] = total + roll(total, 64, 1)
    for k in (1, 2):
        es[k, CX, 0:CY, :] = jnp.zeros((CY, 128), F32)
    for x in range(CX):
        es[0, x, CY:CY + 1, :] = jnp.zeros((1, 128), F32)
        es[2, x, CY:CY + 1, :] = jnp.zeros((1, 128), F32)

    def below(ref, off, sigma):
        inside = jnp.where(valid(off), 1.0, 0.0).astype(F32)
        decay, drive = magnetic(sigma)
        ref[0] = decay * inside
        ref[1] = drive * inside

    g = grade(pml_x[jnp.maximum(row * CX - 1, 0)])
    below(dax, (-1, 0, 0), SIGMA_PEAK * ((g + grades_y[...]) + along_z32))
    g = grade(pml_y[jnp.maximum(col * CY - 1, 0)])
    below(day, (0, -1, 0), SIGMA_PEAK * ((grades_x[...] + g) + along_z32[0:CX]))
    g = grade(pml_z[jnp.maximum(slab * CZ - 1, 0)])
    packed_x = zero8
    for i in range(CX):
        packed_x = jnp.where((lane8 % 64) // 4 == i, grades_x[i:i + 1, :], packed_x)
    packed_y = zero8
    for k in range(CY // 8):
        packed_y = jnp.where(lane8 % 4 == k, grades_y[8 * k:8 * k + 8, :], packed_y)
    below(daz, (0, 0, -1), SIGMA_PEAK * ((packed_x + packed_y) + g))

    for n in range(STEPS):
        for w in range(WAVES):
            phase = jnp.full((8, 128), omega[w] * ((n + 1) * TIME_STEP), F32)
            trig[0, w, n] = jnp.cos(phase)
            trig[1, w, n] = -jnp.sin(phase)
    acc[...] = jnp.zeros(acc.shape, F32)

    for k in range(3):
        loads[4 + k].wait()
    for move in opening:
        move.wait_recv()
    hs[1, 0, 8:8 + CY, :] = r_hx[0]
    hs[2, 0, 8:8 + CY, :] = r_hx[1]
    hy[...] = r_hy[...]
    hz[...] = r_hz[...]
    for move in opening:
        move.wait_send()

    def electric_planes(n, where, last, packs):
        for x in where:
            hs[0, x + 1, 7:8, :] = hy[0, x:x + 1, :]
            hs[2, x + 1, 7:8, :] = hy[1, x:x + 1, :]
        halo = hz[...]
        low, high, high2 = packs
        for x in where:
            h0 = hs[0, x + 1, 8:8 + CY, :]
            h1 = hs[1, x + 1, 8:8 + CY, :]
            h2 = hs[2, x + 1, 8:8 + CY, :]
            h0y = hs[0, x + 1, 7:7 + CY, :]
            h2y = hs[2, x + 1, 7:7 + CY, :]
            h1x = hs[1, x, 8:8 + CY, :]
            h2x = hs[2, x, 8:8 + CY, :]
            h0z = jnp.where(lane32 == 0, unpack(halo, 4 * x, 0), roll(h0, 1, 1))
            h1z = jnp.where(lane32 == 0, unpack(halo, 64 + 4 * x, 0), roll(h1, 1, 1))
            decay, drive = ca[x], cb[x]
            e0 = decay * es[0, x, 0:CY, :] + drive * ((h2 - h2y) - (h1 - h1z))
            e1 = decay * es[1, x, 0:CY, :] + drive * ((h0 - h0z) - (h2 - h2x))
            e2 = decay * es[2, x, 0:CY, :] + drive * ((h1 - h1x) - (h0 - h0y))
            es[0, x, 0:CY, :] = e0
            es[1, x, 0:CY, :] = e1
            es[2, x, 0:CY, :] = e2
            s_ey[n, 0, x:x + 1, :] = e0[0:1]
            s_ey[n, 1, x:x + 1, :] = e2[0:1]
            low = pack(pack(low, e0, 0, 4 * x), e1, 0, 64 + 4 * x)
            if not last:
                for k, e in enumerate((e0, e1, e2)):
                    top[k, x:x + 1, :] = e[CY - 1:CY]
                high = pack(pack(high, e0, 127, 4 * x), e1, 127, 64 + 4 * x)
                high2 = pack(pack(high2, e2, 127, 4 * x), e2, 127, 64 + 4 * x)
                if x == CX - 1:
                    e0z = jnp.where(lane32 == 127, 0.0, roll(e0, -1, 1))
                    e0y = jnp.where(row32 == CY - 1, 0.0, roll(e0, -1, 0))
                    s_ux[n, 0] = (e0z - e0) + e2
                    s_ux[n, 1] = (e0 - e0y) - e1
        return low, high, high2

    def electric_phase(n, last):
        first_moves = [Move(n, 0, (-1, 0, 0), es.at[pl.ds(1, 2), 0, pl.ds(0, CY), :], r_ex.at[n])]
        moves = [
            Move(n, 1, (0, -1, 0), s_ey.at[n], r_ey.at[n]),
            Move(n, 2, (0, 0, -1), s_ez.at[n], r_ez.at[n]),
        ]
        if not last:
            sources = (s_ez.at[n], s_far.at[n], es.at[0, CX - 1, pl.ds(0, 8), :],
                       es.at[1, 0, pl.ds(CY - 8, 8), :], s_ez.at[n], s_far.at[n])
            edges = [Move(n, 6 + k, off, sources[k], r_edge.at[k, n]) for k, off in enumerate(EDGES)]
            first_moves = edges[2:4] + [Move(n, 3, (1, 0, 0), s_ux.at[n], r_ux.at[n])] + first_moves
            moves = [moves[0], Move(n, 4, (0, 1, 0), s_uy.at[n], r_uy.at[n])] + edges[0:2] + edges[4:6] + [
                moves[1], Move(n, 5, (0, 0, 1), s_uz.at[n], r_uz.at[n])]
        if n:
            terms = above_terms(n - 1)
            above_planes(terms, (0, CX - 2, CX - 1))
        packs = electric_planes(n, (0,) if last else (0, CX - 1), last, (zero8, zero8, zero8))
        for move in first_moves:
            move.start()
        if n:
            above_planes(terms, range(1, CX - 2))
        low, high, high2 = electric_planes(n, range(1, CX if last else CX - 1), last, packs)
        s_ez[n] = low
        if not last:
            e0, e1, e2 = top[0], top[1], top[2]
            s_uy[n, 0] = (e1 - jnp.where(lane16 == 127, 0.0, roll(e1, -1, 1))) - e2
            s_uy[n, 1] = (jnp.where(row16 == CX - 1, 0.0, roll(e1, -1, 0)) - e1) + e0
            s_far[n] = high2
            up = roll(high2, -1, 0)
            e2y = jnp.where(row8 < 7, up, jnp.where(lane8 % 4 == 3, 0.0, roll(up, -1, 1)))
            e2x = jnp.where(lane8 >= 124, 0.0, roll(high2, -4, 1))
            e01 = roll(high, 64, 1)
            s_uz[n] = jnp.where(lane8 < 64, (e2y - high2) + e01, (high2 - e2x) - e01)
        if not last:
            for move in moves:
                move.start()
        return first_moves, moves

    def below_phase(n):
        curl1 = r_ux[n, 0] + jnp.where(lane32 == 127, unpack(r_edge[0, n], 60, 127), 0.0) - es[2, 0, 0:CY, :]
        curl2 = r_ux[n, 1] - jnp.where(row32 == CY - 1, r_edge[2, n, 0:1, :], 0.0) + es[1, 0, 0:CY, :]
        hs[1, 0, 8:8 + CY, :] = dax[0] * hs[1, 0, 8:8 + CY, :] - dax[1] * curl1
        hs[2, 0, 8:8 + CY, :] = dax[0] * hs[2, 0, 8:8 + CY, :] - dax[1] * curl2

        corner = jnp.broadcast_to(r_edge[4, n, 7:8, :], (CX, 128))
        corner = jnp.sum(jnp.where(lane16 == 67 + 4 * row16, corner, 0.0), axis=1, keepdims=True)
        curl0 = r_uy[n, 0] - jnp.where(lane16 == 127, corner, 0.0) + s_ey[n, 1]
        curl2 = r_uy[n, 1] + jnp.where(row16 == CX - 1, r_edge[3, n, 7:8, :], 0.0) - s_ey[n, 0]
        hy[0] = day[0] * hy[0] - day[1] * curl0
        hy[1] = day[0] * hy[1] - day[1] * curl2

        own = roll(s_ez[n], 64, 1)
        up_edge = roll(roll(r_edge[5, n], -1, 0), 3, 1)
        up_edge = jnp.where((row8 == 7) & (lane8 % 4 == 3), up_edge, 0.0) - own
        far_edge = jnp.where(lane8 >= 124, roll(r_edge[1, n], 124, 1), 0.0) - own
        curl = r_uz[n] + jnp.where(lane8 < 64, up_edge, -far_edge)
        hz[...] = daz[0] * hz[...] - daz[1] * curl

    def magnetic_phase():
        for x in range(CX):
            e0 = es[0, x, 0:CY, :]
            e1 = es[1, x, 0:CY, :]
            e2 = es[2, x, 0:CY, :]
            e0y = es[0, x, 1:1 + CY, :]
            e2y = es[2, x, 1:1 + CY, :]
            e1x = es[1, x + 1, 0:CY, :]
            e2x = es[2, x + 1, 0:CY, :]
            e0z = jnp.where(lane32 == 127, 0.0, roll(e0, -1, 1))
            e1z = jnp.where(lane32 == 127, 0.0, roll(e1, -1, 1))
            decay, drive = da[x], db[x]
            h0 = decay * hs[0, x + 1, 8:8 + CY, :] - drive * ((e2y - e2) - (e1z - e1))
            h1 = decay * hs[1, x + 1, 8:8 + CY, :] - drive * ((e0z - e0) - (e2x - e2))
            h2 = decay * hs[2, x + 1, 8:8 + CY, :] - drive * ((e1x - e1) - (e0y - e0))
            hs[0, x + 1, 8:8 + CY, :] = h0
            hs[1, x + 1, 8:8 + CY, :] = h1
            hs[2, x + 1, 8:8 + CY, :] = h2

    def above_terms(n):
        return n, dby[...] * r_ey[n, 1], dby[...] * r_ey[n, 0], dbz[...] * r_ez[n]

    def above_planes(terms, where):
        n, term0, term2, packed = terms
        for x in where:
            if x == CX - 1:
                hs[1, CX, 8:8 + CY, :] = hs[1, CX, 8:8 + CY, :] + db[x] * r_ex[n, 1]
                hs[2, CX, 8:8 + CY, :] = hs[2, CX, 8:8 + CY, :] - db[x] * r_ex[n, 0]
            hs[0, x + 1, 7 + CY:8 + CY, :] = hs[0, x + 1, 7 + CY:8 + CY, :] - term0[x:x + 1]
            hs[2, x + 1, 7 + CY:8 + CY, :] = hs[2, x + 1, 7 + CY:8 + CY, :] + term2[x:x + 1]
        for x in where:
            h0 = hs[0, x + 1, 8:8 + CY, :] + jnp.where(lane32 == 127, unpack(packed, 64 + 4 * x, 127), 0.0)
            h1 = hs[1, x + 1, 8:8 + CY, :] - jnp.where(lane32 == 127, unpack(packed, 4 * x, 127), 0.0)
            hs[0, x + 1, 8:8 + CY, :] = h0
            hs[1, x + 1, 8:8 + CY, :] = h1

    def extract_planes(n):
        weights = []
        for c in range(3):
            weight = jnp.zeros((16, 128), F32)
            for p in range(MON):
                weight = jnp.where((row16 == 3 * p + c) & (lane16 + slab * CZ == monitor[p]), 1.0, weight)
            weights += [weight.astype(jnp.bfloat16)] * 3
        weights = jnp.concatenate(weights, axis=1)
        planes[slab, n, 32:40, :] = zero8
        for k in range(0, CX // 4, 2):
            pieces = []
            for c in range(3):
                rest = es[c, 4 * k:4 * k + 8, 0:CY, :].reshape(256, 128)
                for _ in range(3):
                    pieces.append(rest.astype(jnp.bfloat16))
                    rest = rest - pieces[-1].astype(F32)
            total = lax.dot_general(weights, jnp.concatenate(pieces, axis=1), (((1,), (1,)), ((), ())),
                                    preferred_element_type=F32)
            for j in range(2):
                part = total[:, 128 * j:128 * j + 128]
                planes[slab, n, 8 * (k + j):8 * (k + j) + 8, :] = part[0:8]
                planes[slab, n, 32 + k + j:33 + k + j, :] = part[8:9]
        for k in range(5):
            whole = planes[slab, n, 8 * k:8 * k + 8, :]
            for q in range(2):
                for w in range(WAVES):
                    acc[q, w, k] = acc[q, w, k] + trig[q, w, n] * whole

    def plane_move(i, source):
        return pltpu.make_async_remote_copy(
            src_ref=planes.at[source], dst_ref=planes.at[source],
            send_sem=plane_send.at[i - 1], recv_sem=plane_recv.at[i - 1],
            device_id=(tile, (slab + i) % SLABS), device_id_type=MESH)

    for n in range(STEPS - 1):
        moves = sum(electric_phase(n, False), [])
        extract_planes(n)
        magnetic_phase()
        for move in moves:
            move.wait_send()
        for move in reversed(moves):
            move.wait_recv()
        below_phase(n)

    moves, later = electric_phase(STEPS - 1, True)
    extract_planes(STEPS - 1)

    part = jnp.zeros((1, 128), F32)
    odd = zero8
    for w in range(WAVES):
        odd = odd + (acc[0, w, 4] * acc[0, w, 4] + acc[1, w, 4] * acc[1, w, 4])
    for k in range(4):
        power = zero8
        for w in range(WAVES):
            power = power + (acc[0, w, k] * acc[0, w, k] + acc[1, w, k] * acc[1, w, k])
        power = jnp.sum(power, axis=0, keepdims=True) + odd[k:k + 1]
        part = part + power * focus[0:1, 128 * k:128 * k + 128]

    def send_totals(stage, mine, where):
        buf = (first, second)[stage]
        for i in sorted(range(1, 16), key=lambda i: -min(i, 16 - i)):
            pltpu.make_async_remote_copy(
                src_ref=buf.at[pl.ds(mine, 1), :], dst_ref=buf.at[pl.ds(mine, 1), :],
                send_sem=total_send.at[stage], recv_sem=total_recv.at[stage],
                device_id=where(i), device_id_type=MESH).start()

    def all_totals(stage):
        buf = (first, second)[stage].at[pl.ds(0, 15), :]
        return pltpu.make_async_remote_copy(
            src_ref=buf, dst_ref=buf, send_sem=total_send.at[stage], recv_sem=total_recv.at[stage],
            device_id=(in_row, in_column)[stage](1), device_id_type=MESH)

    first[pl.ds(col * 2 + core, 1), :] = part
    send_totals(0, col * 2 + core, in_row)
    for move in later:
        move.start()
    for i in range(1, SLABS):
        plane_move(i, slab).start()
    moves = moves + later

    stores = [pltpu.make_async_copy(
        es.at[k, pl.ds(0, CX), pl.ds(0, CY), :], e_out.at[0, k], local_sem.at[7 + k]) for k in range(3)]
    for store in stores:
        store.start()
    magnetic_phase()
    for move in moves:
        move.wait_send()
    for move in reversed(moves):
        move.wait_recv()
    above_planes(above_terms(STEPS - 1), range(CX))
    for k in range(3):
        stores.append(pltpu.make_async_copy(
            hs.at[k, pl.ds(1, CX), pl.ds(8, CY), :], h_out.at[0, k], local_sem.at[10 + k]))
        stores[-1].start()

    all_totals(0).wait_recv()
    second[pl.ds(row * 2 + half, 1), :] = jnp.sum(first[...], axis=0, keepdims=True)
    send_totals(1, row * 2 + half, in_column)

    for i in range(1, SLABS):
        plane_move(i, (slab + SLABS - i) % SLABS).wait_recv()
    for k in range(5):
        spectrum = [[zero8] * WAVES, [zero8] * WAVES]
        for n in range(STEPS):
            whole = planes[0, n, 8 * k:8 * k + 8, :]
            for g in range(1, SLABS):
                whole = whole + planes[g, n, 8 * k:8 * k + 8, :]
            for q in range(2):
                for w in range(WAVES):
                    spectrum[q][w] = spectrum[q][w] + trig[q, w, n] * whole
        for q in range(2):
            for w in range(WAVES):
                base = 36 * q + 9 * w
                if k < 4:
                    spec[0, base:base + 8, 128 * k:128 * k + 128] = spectrum[q][w]
                else:
                    for j in range(4):
                        spec[0, base + 8:base + 9, 128 * j:128 * j + 128] = spectrum[q][w][j:j + 1]

    for i in range(1, SLABS):
        plane_move(i, slab).wait_send()
    all_totals(0).wait_send()
    for store in stores:
        store.wait()
    all_totals(1).wait()
    cells = TILES_X * TILES_Y * WAVES * MON * 3 * CX * CY
    objective[0] = jnp.sum(second[...]) / jnp.float32(cells)


def hand_on(e_in, h_in, s_in, e_out, h_out, s_out, e_mid, h_mid, s_mid, sem):
    pieces = [(e_in.at[0, k], e_mid.at[k], e_out.at[0, k]) for k in range(3)]
    pieces += [(h_in.at[0, k], h_mid.at[k], h_out.at[0, k]) for k in range(3)]
    pieces += [(s_in, s_mid, s_out)]
    arrive = [pltpu.make_async_copy(a, b, sem.at[0, k]) for k, (a, b, c) in enumerate(pieces)]
    leave = [pltpu.make_async_copy(b, c, sem.at[1, k]) for k, (a, b, c) in enumerate(pieces)]
    for copy in arrive:
        copy.start()
    for before, after in zip(arrive, leave):
        before.wait()
        after.start()
    for copy in leave:
        copy.wait()


def step(e_field, h_field, material, permittivity, pml_x, pml_y, pml_z, monitor_z, omega, focus):
    vmem = lambda *shape: pltpu.VMEM(shape, F32)
    dma = lambda *shape: pltpu.SemaphoreType.DMA(shape)
    anywhere = pl.BlockSpec(memory_space=pl.ANY)
    smem = pl.BlockSpec(memory_space=pltpu.SMEM)
    inside = pl.BlockSpec(memory_space=pltpu.VMEM)
    early = STEPS - 1
    e_out, h_out, spectra, objective = pl.pallas_call(
        kernel,
        out_shape=(
            jax.ShapeDtypeStruct(e_field.shape, F32),
            jax.ShapeDtypeStruct(h_field.shape, F32),
            jax.ShapeDtypeStruct((1, 2 * WAVES * MON * 3, CX * CY), F32),
            jax.ShapeDtypeStruct((1,), F32),
        ),
        in_specs=[anywhere] * 3 + [inside] + [smem] * 6,
        out_specs=(anywhere, anywhere, inside, smem),
        scratch_shapes=[
            vmem(3, CX + 1, CY + 8, CZ), vmem(3, CX + 1, CY + 8, CZ), pltpu.VMEM((CX, CY, CZ), jnp.int32),
            vmem(CX, CY, CZ), vmem(CX, CY, CZ), vmem(CX, CY, CZ), vmem(CX, CY, CZ),
            vmem(CX, 128), vmem(CY, 128),
            vmem(2, WAVES, STEPS, 8, 128), vmem(2, WAVES, 5, 8, 128), vmem(SLABS, STEPS, 40, 128),
            vmem(2 * TILES_Y, 128), vmem(2 * TILES_X, 128),
            vmem(2, CX, 128), vmem(8, 128), vmem(2, CY, 128), vmem(2, CX, 128), vmem(2, 8, 128), vmem(CX, 128), vmem(8, 128),
            vmem(2, CX, 128), vmem(8, 128), vmem(2, CY, 128), vmem(2, CX, 128), vmem(8, 128),
            vmem(STEPS, 2, CX, 128), vmem(STEPS, 8, 128),
            vmem(STEPS, 2, CY, 128), vmem(STEPS, 2, CX, 128), vmem(STEPS, 8, 128),
            vmem(early, 2, CY, 128), vmem(early, 2, CX, 128), vmem(early, 8, 128), vmem(early, 8, 128), vmem(3, CX, 128),
            vmem(early, 2, CY, 128), vmem(early, 2, CX, 128), vmem(early, 8, 128),
            vmem(6, early, 8, 128),
            dma(13), dma(STEPS + 1, 12), dma(STEPS + 1, 12),
            dma(SLABS), dma(SLABS), dma(2), dma(2),
        ],
        compiler_params=pltpu.CompilerParams(
            collective_id=0, has_side_effects=True, vmem_limit_bytes=60 * 1024 * 1024),
    )(e_field, h_field, material, focus, permittivity, pml_x, pml_y, pml_z, monitor_z, omega)
    e_out, h_out, spectra = pl.pallas_call(
        hand_on,
        out_shape=tuple(jax.ShapeDtypeStruct(a.shape, F32) for a in (e_out, h_out, spectra)),
        in_specs=[anywhere] * 3,
        out_specs=(anywhere,) * 3,
        scratch_shapes=[vmem(3, CX, CY, CZ), vmem(3, CX, CY, CZ), vmem(1, 72, 512), dma(2, 7)],
    )(e_out, h_out, spectra)
    return e_out, h_out, spectra, objective.reshape(())


def solution(mesh):
    field = P("xy", None, None, None, "gz")
    return jax.shard_map(
        step,
        mesh=mesh,
        in_specs=(field, field, P("xy", None, None, "gz"), P(), P(), P(), P(), P(), P(), P("xy", None)),
        out_specs=(field, field, P("xy", None, None), P()),
        check_vma=False,
    )
```

```python
import functools

import jax
import jax.numpy as jnp
from jax import lax
from jax.experimental import pallas as pl
from jax.experimental.pallas import tpu as pltpu
from jax.sharding import PartitionSpec as P

MESH = pl.DeviceIdType.MESH
TILES_X = 8
TILES_Y = 8
SLABS = 4
STEPS = 4
WAVES = 4
MON = 3
DEPTH = 8
TIME_STEP = 0.5
SIGMA_PEAK = 0.8
CX, CY, CZ = 16, 32, 128
F32 = jnp.float32
EDGES = ((1, 0, -1), (-1, 0, 1), (1, -1, 0), (-1, 1, 0), (0, 1, -1), (0, -1, 1))


def roll(value, shift, axis):
    return pltpu.roll(value, shift % value.shape[axis], axis)


def grade(level):
    scaled = level.astype(F32) / DEPTH
    return scaled * scaled


def magnetic(sigma):
    loss = sigma * (0.5 * TIME_STEP)
    return (1.0 - loss) / (1.0 + loss), TIME_STEP / (1.0 + loss)


def electric(sigma, permit):
    loss = sigma * (0.5 * TIME_STEP) / permit
    return (1.0 - loss) / (1.0 + loss), TIME_STEP / (permit * (1.0 + loss))


def kernel(
    e_in, h_in, m_in, focus_in, permit_in, pml_x_in, pml_y_in, pml_z_in, monitor_in, omega_in,
    e_out, h_out, spec_out, objective_out,
    focus, permit, pml_x, pml_y, pml_z, monitor, omega, spec, objective,
    es, hs, kinds, ca, cb, da, db, grades_x, grades_y, trig, acc, planes, first, second,
    hy, hz, dax, day, daz, dby, dbz,
    s_hy, s_hz, r_hx, r_hy, r_hz,
    s_ey, s_ez, r_ex, r_ey, r_ez,
    s_ux, s_uy, s_uz, s_far, top, r_ux, r_uy, r_uz, r_edge,
    local_sem, small_sem, send_sem, recv_sem, plane_send, plane_recv, total_send, total_recv,
):
    tile = lax.axis_index("xy")
    slab = lax.axis_index("gz")
    row, col = tile // TILES_Y, tile % TILES_Y
    half, core = slab // 2, slab % 2

    def valid(off):
        r, c, g = row + off[0], col + off[1], slab + off[2]
        return (r >= 0) & (r < TILES_X) & (c >= 0) & (c < TILES_Y) & (g >= 0) & (g < SLABS)

    def device(off):
        return ((row + off[0]) * TILES_Y + col + off[1], slab + off[2])

    def minus(off):
        return tuple(-o for o in off)

    class Move:
        def __init__(self, n, k, off, src, dst):
            self.off = off
            self.copy = lambda: pltpu.make_async_remote_copy(
                src_ref=src, dst_ref=dst, send_sem=send_sem.at[n, k], recv_sem=recv_sem.at[n, k],
                device_id=device(off), device_id_type=MESH)

        def start(self):
            @pl.when(valid(self.off))
            def _():
                self.copy().start()

        def wait_send(self):
            @pl.when(valid(self.off))
            def _():
                self.copy().wait_send()

        def wait_recv(self):
            @pl.when(valid(minus(self.off)))
            def _():
                self.copy().wait_recv()

    barrier = pltpu.get_barrier_semaphore()

    def greet(where):
        pl.semaphore_signal(barrier, inc=1, device_id=where, device_id_type=MESH)

    def in_row(i):
        k = (col * 2 + core + i) % (2 * TILES_Y)
        return row * TILES_Y + k // 2, half * 2 + k % 2

    def in_column(i):
        k = (row * 2 + half + i) % (2 * TILES_X)
        return k // 2 * TILES_Y + col, k % 2 * 2 + core

    for i in range(1, 2 * TILES_Y):
        greet(in_row(i))
    for i in range(1, 2 * TILES_X):
        greet(in_column(i))
    greet((tile, SLABS - 1 - slab))
    for off in EDGES:
        @pl.when(valid(off))
        def _(off=off):
            greet(device(off))

    loads = []
    for k in range(3):
        loads.append(pltpu.make_async_copy(
            h_in.at[0, k], hs.at[k, pl.ds(1, CX), pl.ds(8, CY), :], local_sem.at[k]))
    loads.append(pltpu.make_async_copy(m_in.at[0], kinds, local_sem.at[3]))
    for k in range(3):
        loads.append(pltpu.make_async_copy(
            e_in.at[0, k], es.at[k, pl.ds(0, CX), pl.ds(0, CY), :], local_sem.at[4 + k]))
    for load in loads:
        load.start()
    small = [pltpu.make_async_copy(source, target, small_sem.at[k]) for k, (source, target) in enumerate((
        (pml_x_in, pml_x), (pml_y_in, pml_y), (pml_z_in, pml_z), (permit_in, permit),
        (omega_in, omega), (monitor_in, monitor), (focus_in, focus)))]
    for load in small:
        load.start()

    lane8 = lax.broadcasted_iota(jnp.int32, (8, 128), 1)
    row8 = lax.broadcasted_iota(jnp.int32, (8, 128), 0)
    lane16 = lax.broadcasted_iota(jnp.int32, (16, 128), 1)
    row16 = lax.broadcasted_iota(jnp.int32, (16, 128), 0)
    lane32 = lax.broadcasted_iota(jnp.int32, (CY, 128), 1)
    row32 = lax.broadcasted_iota(jnp.int32, (CY, 128), 0)
    zero8 = jnp.zeros((8, 128), F32)

    def clear(off, *refs):
        @pl.when(jnp.logical_not(valid(minus(off))))
        def _():
            for ref in refs:
                ref[...] = jnp.zeros(ref.shape, F32)

    clear((1, 0, 0), r_hx, r_ux)
    clear((0, 1, 0), r_hy, r_uy)
    clear((0, 0, 1), r_hz, r_uz)
    clear((-1, 0, 0), r_ex)
    clear((0, -1, 0), r_ey)
    clear((0, 0, -1), r_ez)
    for k, off in enumerate(EDGES):
        clear(off, r_edge.at[k])

    def pack(total, field, source, start):
        for k in range(CY // 8):
            piece = roll(field[8 * k:8 * k + 8], start + k - source, 1)
            total = jnp.where(lane8 == start + k, piece, total)
        return total

    def unpack(packed, start, target):
        return jnp.concatenate([roll(packed, target - start - k, 1) for k in range(CY // 8)], axis=0)

    for k in range(3):
        loads[k].wait()

    total = zero8
    for x in range(CX):
        s_hy[0, x:x + 1, :] = hs[0, x + 1, 7 + CY:8 + CY, :]
        s_hy[1, x:x + 1, :] = hs[2, x + 1, 7 + CY:8 + CY, :]
        total = pack(total, hs[0, x + 1, 8:8 + CY, :], 127, 4 * x)
        total = pack(total, hs[1, x + 1, 8:8 + CY, :], 127, 64 + 4 * x)
    s_hz[...] = total

    greeted = 2 * TILES_Y - 1 + 2 * TILES_X - 1 + 1
    for off in EDGES:
        greeted = greeted + jnp.where(valid(off), 1, 0)
    pl.semaphore_wait(barrier, greeted)

    opening = [
        Move(STEPS, 0, (1, 0, 0), hs.at[pl.ds(1, 2), CX, pl.ds(8, CY), :], r_hx),
        Move(STEPS, 1, (0, 1, 0), s_hy, r_hy),
        Move(STEPS, 2, (0, 0, 1), s_hz, r_hz),
    ]
    for move in opening:
        move.start()

    for load in small:
        load.wait()
    for i in range(CX):
        grades_x[i:i + 1, :] = jnp.full((1, 128), grade(pml_x[row * CX + i]), F32)
    for j in range(CY):
        grades_y[j:j + 1, :] = jnp.full((1, 128), grade(pml_y[col * CY + j]), F32)

    def lay(k, levels):
        return jnp.where(lane8 == k, pml_z[slab * CZ + k], levels)

    along_z = grade(lax.fori_loop(0, CZ, lay, jnp.zeros((8, 128), jnp.int32)))
    along_z32 = jnp.concatenate([along_z] * 4, axis=0)

    loads[3].wait()

    def fill(x, _):
        g = jnp.full((CY, 128), grade(pml_x[row * CX + x]), F32)
        sigma = SIGMA_PEAK * ((g + grades_y[...]) + along_z32)
        kind = kinds[x]
        eps = jnp.full((CY, 128), permit[0], F32)
        for which in range(1, 4):
            eps = jnp.where(kind == which, permit[which], eps)
        ca[x], cb[x] = electric(sigma, eps)
        da[x], db[x] = magnetic(sigma)
        return 0

    lax.fori_loop(0, CX, fill, 0)
    total = zero8
    for x in range(CX):
        dby[x:x + 1, :] = db[x, CY - 1:CY, :]
        total = pack(total, db[x], 127, 4 * x)
    dbz[...] = total + roll(total, 64, 1)
    for k in (1, 2):
        es[k, CX, 0:CY, :] = jnp.zeros((CY, 128), F32)
    for x in range(CX):
        es[0, x, CY:CY + 1, :] = jnp.zeros((1, 128), F32)
        es[2, x, CY:CY + 1, :] = jnp.zeros((1, 128), F32)

    def below(ref, off, sigma):
        inside = jnp.where(valid(off), 1.0, 0.0).astype(F32)
        decay, drive = magnetic(sigma)
        ref[0] = decay * inside
        ref[1] = drive * inside

    g = grade(pml_x[jnp.maximum(row * CX - 1, 0)])
    below(dax, (-1, 0, 0), SIGMA_PEAK * ((g + grades_y[...]) + along_z32))
    g = grade(pml_y[jnp.maximum(col * CY - 1, 0)])
    below(day, (0, -1, 0), SIGMA_PEAK * ((grades_x[...] + g) + along_z32[0:CX]))
    g = grade(pml_z[jnp.maximum(slab * CZ - 1, 0)])
    packed_x = zero8
    for i in range(CX):
        packed_x = jnp.where((lane8 % 64) // 4 == i, grades_x[i:i + 1, :], packed_x)
    packed_y = zero8
    for k in range(CY // 8):
        packed_y = jnp.where(lane8 % 4 == k, grades_y[8 * k:8 * k + 8, :], packed_y)
    below(daz, (0, 0, -1), SIGMA_PEAK * ((packed_x + packed_y) + g))

    for n in range(STEPS):
        for w in range(WAVES):
            phase = jnp.full((8, 128), omega[w] * ((n + 1) * TIME_STEP), F32)
            trig[0, w, n] = jnp.cos(phase)
            trig[1, w, n] = -jnp.sin(phase)
    acc[...] = jnp.zeros(acc.shape, F32)

    for k in range(3):
        loads[4 + k].wait()
    for move in opening:
        move.wait_recv()
    hs[1, 0, 8:8 + CY, :] = r_hx[0]
    hs[2, 0, 8:8 + CY, :] = r_hx[1]
    hy[...] = r_hy[...]
    hz[...] = r_hz[...]
    for move in opening:
        move.wait_send()

    def electric_planes(n, where, last, packs):
        for x in where:
            hs[0, x + 1, 7:8, :] = hy[0, x:x + 1, :]
            hs[2, x + 1, 7:8, :] = hy[1, x:x + 1, :]
        halo = hz[...]
        low, high, high2 = packs
        for x in where:
            h0 = hs[0, x + 1, 8:8 + CY, :]
            h1 = hs[1, x + 1, 8:8 + CY, :]
            h2 = hs[2, x + 1, 8:8 + CY, :]
            h0y = hs[0, x + 1, 7:7 + CY, :]
            h2y = hs[2, x + 1, 7:7 + CY, :]
            h1x = hs[1, x, 8:8 + CY, :]
            h2x = hs[2, x, 8:8 + CY, :]
            h0z = jnp.where(lane32 == 0, unpack(halo, 4 * x, 0), roll(h0, 1, 1))
            h1z = jnp.where(lane32 == 0, unpack(halo, 64 + 4 * x, 0), roll(h1, 1, 1))
            decay, drive = ca[x], cb[x]
            e0 = decay * es[0, x, 0:CY, :] + drive * ((h2 - h2y) - (h1 - h1z))
            e1 = decay * es[1, x, 0:CY, :] + drive * ((h0 - h0z) - (h2 - h2x))
            e2 = decay * es[2, x, 0:CY, :] + drive * ((h1 - h1x) - (h0 - h0y))
            es[0, x, 0:CY, :] = e0
            es[1, x, 0:CY, :] = e1
            es[2, x, 0:CY, :] = e2
            s_ey[n, 0, x:x + 1, :] = e0[0:1]
            s_ey[n, 1, x:x + 1, :] = e2[0:1]
            low = pack(pack(low, e0, 0, 4 * x), e1, 0, 64 + 4 * x)
            if not last:
                for k, e in enumerate((e0, e1, e2)):
                    top[k, x:x + 1, :] = e[CY - 1:CY]
                high = pack(pack(high, e0, 127, 4 * x), e1, 127, 64 + 4 * x)
                high2 = pack(pack(high2, e2, 127, 4 * x), e2, 127, 64 + 4 * x)
                if x == CX - 1:
                    e0z = jnp.where(lane32 == 127, 0.0, roll(e0, -1, 1))
                    e0y = jnp.where(row32 == CY - 1, 0.0, roll(e0, -1, 0))
                    s_ux[n, 0] = (e0z - e0) + e2
                    s_ux[n, 1] = (e0 - e0y) - e1
        return low, high, high2

    def electric_phase(n, last):
        first_moves = [Move(n, 0, (-1, 0, 0), es.at[pl.ds(1, 2), 0, pl.ds(0, CY), :], r_ex.at[n])]
        moves = [
            Move(n, 1, (0, -1, 0), s_ey.at[n], r_ey.at[n]),
            Move(n, 2, (0, 0, -1), s_ez.at[n], r_ez.at[n]),
        ]
        if not last:
            sources = (s_ez.at[n], s_far.at[n], es.at[0, CX - 1, pl.ds(0, 8), :],
                       es.at[1, 0, pl.ds(CY - 8, 8), :], s_ez.at[n], s_far.at[n])
            edges = [Move(n, 6 + k, off, sources[k], r_edge.at[k, n]) for k, off in enumerate(EDGES)]
            first_moves = edges[2:4] + [Move(n, 3, (1, 0, 0), s_ux.at[n], r_ux.at[n])] + first_moves
            moves = [moves[0], Move(n, 4, (0, 1, 0), s_uy.at[n], r_uy.at[n])] + edges[0:2] + edges[4:6] + [
                moves[1], Move(n, 5, (0, 0, 1), s_uz.at[n], r_uz.at[n])]
        if n:
            terms = above_terms(n - 1)
            above_planes(terms, (0, CX - 2, CX - 1))
        packs = electric_planes(n, (0,) if last else (0, CX - 1), last, (zero8, zero8, zero8))
        for move in first_moves:
            move.start()
        if n:
            above_planes(terms, range(1, CX - 2))
        low, high, high2 = electric_planes(n, range(1, CX if last else CX - 1), last, packs)
        s_ez[n] = low
        if not last:
            e0, e1, e2 = top[0], top[1], top[2]
            s_uy[n, 0] = (e1 - jnp.where(lane16 == 127, 0.0, roll(e1, -1, 1))) - e2
            s_uy[n, 1] = (jnp.where(row16 == CX - 1, 0.0, roll(e1, -1, 0)) - e1) + e0
            s_far[n] = high2
            up = roll(high2, -1, 0)
            e2y = jnp.where(row8 < 7, up, jnp.where(lane8 % 4 == 3, 0.0, roll(up, -1, 1)))
            e2x = jnp.where(lane8 >= 124, 0.0, roll(high2, -4, 1))
            e01 = roll(high, 64, 1)
            s_uz[n] = jnp.where(lane8 < 64, (e2y - high2) + e01, (high2 - e2x) - e01)
        if not last:
            for move in moves:
                move.start()
        return first_moves, moves

    def below_phase(n):
        curl1 = r_ux[n, 0] + jnp.where(lane32 == 127, unpack(r_edge[0, n], 60, 127), 0.0) - es[2, 0, 0:CY, :]
        curl2 = r_ux[n, 1] - jnp.where(row32 == CY - 1, r_edge[2, n, 0:1, :], 0.0) + es[1, 0, 0:CY, :]
        hs[1, 0, 8:8 + CY, :] = dax[0] * hs[1, 0, 8:8 + CY, :] - dax[1] * curl1
        hs[2, 0, 8:8 + CY, :] = dax[0] * hs[2, 0, 8:8 + CY, :] - dax[1] * curl2

        corner = jnp.broadcast_to(r_edge[4, n, 7:8, :], (CX, 128))
        corner = jnp.sum(jnp.where(lane16 == 67 + 4 * row16, corner, 0.0), axis=1, keepdims=True)
        curl0 = r_uy[n, 0] - jnp.where(lane16 == 127, corner, 0.0) + s_ey[n, 1]
        curl2 = r_uy[n, 1] + jnp.where(row16 == CX - 1, r_edge[3, n, 7:8, :], 0.0) - s_ey[n, 0]
        hy[0] = day[0] * hy[0] - day[1] * curl0
        hy[1] = day[0] * hy[1] - day[1] * curl2

        own = roll(s_ez[n], 64, 1)
        up_edge = roll(roll(r_edge[5, n], -1, 0), 3, 1)
        up_edge = jnp.where((row8 == 7) & (lane8 % 4 == 3), up_edge, 0.0) - own
        far_edge = jnp.where(lane8 >= 124, roll(r_edge[1, n], 124, 1), 0.0) - own
        curl = r_uz[n] + jnp.where(lane8 < 64, up_edge, -far_edge)
        hz[...] = daz[0] * hz[...] - daz[1] * curl

    def magnetic_phase():
        for x in range(CX):
            e0 = es[0, x, 0:CY, :]
            e1 = es[1, x, 0:CY, :]
            e2 = es[2, x, 0:CY, :]
            e0y = es[0, x, 1:1 + CY, :]
            e2y = es[2, x, 1:1 + CY, :]
            e1x = es[1, x + 1, 0:CY, :]
            e2x = es[2, x + 1, 0:CY, :]
            e0z = jnp.where(lane32 == 127, 0.0, roll(e0, -1, 1))
            e1z = jnp.where(lane32 == 127, 0.0, roll(e1, -1, 1))
            decay, drive = da[x], db[x]
            h0 = decay * hs[0, x + 1, 8:8 + CY, :] - drive * ((e2y - e2) - (e1z - e1))
            h1 = decay * hs[1, x + 1, 8:8 + CY, :] - drive * ((e0z - e0) - (e2x - e2))
            h2 = decay * hs[2, x + 1, 8:8 + CY, :] - drive * ((e1x - e1) - (e0y - e0))
            hs[0, x + 1, 8:8 + CY, :] = h0
            hs[1, x + 1, 8:8 + CY, :] = h1
            hs[2, x + 1, 8:8 + CY, :] = h2

    def above_terms(n):
        return n, dby[...] * r_ey[n, 1], dby[...] * r_ey[n, 0], dbz[...] * r_ez[n]

    def above_planes(terms, where):
        n, term0, term2, packed = terms
        for x in where:
            if x == CX - 1:
                hs[1, CX, 8:8 + CY, :] = hs[1, CX, 8:8 + CY, :] + db[x] * r_ex[n, 1]
                hs[2, CX, 8:8 + CY, :] = hs[2, CX, 8:8 + CY, :] - db[x] * r_ex[n, 0]
            hs[0, x + 1, 7 + CY:8 + CY, :] = hs[0, x + 1, 7 + CY:8 + CY, :] - term0[x:x + 1]
            hs[2, x + 1, 7 + CY:8 + CY, :] = hs[2, x + 1, 7 + CY:8 + CY, :] + term2[x:x + 1]
        for x in where:
            h0 = hs[0, x + 1, 8:8 + CY, :] + jnp.where(lane32 == 127, unpack(packed, 64 + 4 * x, 127), 0.0)
            h1 = hs[1, x + 1, 8:8 + CY, :] - jnp.where(lane32 == 127, unpack(packed, 4 * x, 127), 0.0)
            hs[0, x + 1, 8:8 + CY, :] = h0
            hs[1, x + 1, 8:8 + CY, :] = h1

    def extract_planes(n):
        weights = []
        for c in range(3):
            weight = jnp.zeros((16, 128), F32)
            for p in range(MON):
                weight = jnp.where((row16 == 3 * p + c) & (lane16 + slab * CZ == monitor[p]), 1.0, weight)
            weights += [weight.astype(jnp.bfloat16)] * 3
        weights = jnp.concatenate(weights, axis=1)
        planes[slab, n, 32:40, :] = zero8
        for k in range(0, CX // 4, 2):
            pieces = []
            for c in range(3):
                rest = es[c, 4 * k:4 * k + 8, 0:CY, :].reshape(256, 128)
                for _ in range(3):
                    pieces.append(rest.astype(jnp.bfloat16))
                    rest = rest - pieces[-1].astype(F32)
            total = lax.dot_general(weights, jnp.concatenate(pieces, axis=1), (((1,), (1,)), ((), ())),
                                    preferred_element_type=F32)
            for j in range(2):
                part = total[:, 128 * j:128 * j + 128]
                planes[slab, n, 8 * (k + j):8 * (k + j) + 8, :] = part[0:8]
                planes[slab, n, 32 + k + j:33 + k + j, :] = part[8:9]
        for k in range(5):
            whole = planes[slab, n, 8 * k:8 * k + 8, :]
            for q in range(2):
                for w in range(WAVES):
                    acc[q, w, k] = acc[q, w, k] + trig[q, w, n] * whole

    def plane_move(i, source):
        return pltpu.make_async_remote_copy(
            src_ref=planes.at[source], dst_ref=planes.at[source],
            send_sem=plane_send.at[i - 1], recv_sem=plane_recv.at[i - 1],
            device_id=(tile, (slab + i) % SLABS), device_id_type=MESH)

    for n in range(STEPS - 1):
        moves = sum(electric_phase(n, False), [])
        extract_planes(n)
        magnetic_phase()
        for move in moves:
            move.wait_send()
        for move in reversed(moves):
            move.wait_recv()
        below_phase(n)

    moves, later = electric_phase(STEPS - 1, True)
    extract_planes(STEPS - 1)

    part = jnp.zeros((1, 128), F32)
    odd = zero8
    for w in range(WAVES):
        odd = odd + (acc[0, w, 4] * acc[0, w, 4] + acc[1, w, 4] * acc[1, w, 4])
    for k in range(4):
        power = zero8
        for w in range(WAVES):
            power = power + (acc[0, w, k] * acc[0, w, k] + acc[1, w, k] * acc[1, w, k])
        power = jnp.sum(power, axis=0, keepdims=True) + odd[k:k + 1]
        part = part + power * focus[0:1, 128 * k:128 * k + 128]

    def send_totals(stage, mine, where):
        buf = (first, second)[stage]
        for i in sorted(range(1, 16), key=lambda i: -min(i, 16 - i)):
            pltpu.make_async_remote_copy(
                src_ref=buf.at[pl.ds(mine, 1), :], dst_ref=buf.at[pl.ds(mine, 1), :],
                send_sem=total_send.at[stage], recv_sem=total_recv.at[stage],
                device_id=where(i), device_id_type=MESH).start()

    def all_totals(stage):
        buf = (first, second)[stage].at[pl.ds(0, 15), :]
        return pltpu.make_async_remote_copy(
            src_ref=buf, dst_ref=buf, send_sem=total_send.at[stage], recv_sem=total_recv.at[stage],
            device_id=(in_row, in_column)[stage](1), device_id_type=MESH)

    first[pl.ds(col * 2 + core, 1), :] = part
    send_totals(0, col * 2 + core, in_row)
    for move in later:
        move.start()
    for i in range(1, SLABS):
        plane_move(i, slab).start()
    moves = moves + later

    stores = [pltpu.make_async_copy(
        es.at[k, pl.ds(0, CX), pl.ds(0, CY), :], e_out.at[0, k], local_sem.at[7 + k]) for k in range(3)]
    for store in stores:
        store.start()
    magnetic_phase()
    for move in moves:
        move.wait_send()
    for move in reversed(moves):
        move.wait_recv()
    above_planes(above_terms(STEPS - 1), range(CX))
    for k in range(3):
        stores.append(pltpu.make_async_copy(
            hs.at[k, pl.ds(1, CX), pl.ds(8, CY), :], h_out.at[0, k], local_sem.at[10 + k]))
        stores[-1].start()

    all_totals(0).wait_recv()
    second[pl.ds(row * 2 + half, 1), :] = jnp.sum(first[...], axis=0, keepdims=True)
    send_totals(1, row * 2 + half, in_column)

    for i in range(1, SLABS):
        plane_move(i, (slab + SLABS - i) % SLABS).wait_recv()
    for k in range(5):
        spectrum = [[zero8] * WAVES, [zero8] * WAVES]
        for n in range(STEPS):
            whole = planes[0, n, 8 * k:8 * k + 8, :]
            for g in range(1, SLABS):
                whole = whole + planes[g, n, 8 * k:8 * k + 8, :]
            for q in range(2):
                for w in range(WAVES):
                    spectrum[q][w] = spectrum[q][w] + trig[q, w, n] * whole
        for q in range(2):
            for w in range(WAVES):
                base = 36 * q + 9 * w
                if k < 4:
                    spec[0, base:base + 8, 128 * k:128 * k + 128] = spectrum[q][w]
                else:
                    for j in range(4):
                        spec[0, base + 8:base + 9, 128 * j:128 * j + 128] = spectrum[q][w][j:j + 1]

    stores.append(pltpu.make_async_copy(spec, spec_out, small_sem.at[7]))
    stores[-1].start()
    for i in range(1, SLABS):
        plane_move(i, slab).wait_send()
    all_totals(0).wait_send()
    for store in stores:
        store.wait()
    all_totals(1).wait_recv()
    cells = TILES_X * TILES_Y * WAVES * MON * 3 * CX * CY
    objective[0] = jnp.sum(second[...]) / jnp.float32(cells)
    result = pltpu.make_async_copy(objective, objective_out, small_sem.at[8])
    result.start()
    all_totals(1).wait_send()
    result.wait()


def hand_on(e_in, h_in, s_in, o_in, e_out, h_out, s_out, o_out, e_mid, h_mid, s_mid, o_mid, sem):
    pieces = [(e_in.at[0, k], e_mid.at[k], e_out.at[0, k]) for k in range(3)]
    pieces += [(h_in.at[0, k], h_mid.at[k], h_out.at[0, k]) for k in range(3)]
    pieces += [(s_in, s_mid, s_out), (o_in, o_mid, o_out)]
    arrive = [pltpu.make_async_copy(a, b, sem.at[0, k]) for k, (a, b, c) in enumerate(pieces)]
    leave = [pltpu.make_async_copy(b, c, sem.at[1, k]) for k, (a, b, c) in enumerate(pieces)]
    for copy in arrive:
        copy.start()
    for before, after in zip(arrive, leave):
        before.wait()
        after.start()
    for copy in leave:
        copy.wait()


def step(e_field, h_field, material, permittivity, pml_x, pml_y, pml_z, monitor_z, omega, focus):
    vmem = lambda *shape: pltpu.VMEM(shape, F32)
    dma = lambda *shape: pltpu.SemaphoreType.DMA(shape)
    anywhere = pl.BlockSpec(memory_space=pl.ANY)
    early = STEPS - 1
    e_out, h_out, spectra, objective = pl.pallas_call(
        kernel,
        out_shape=(
            jax.ShapeDtypeStruct(e_field.shape, F32),
            jax.ShapeDtypeStruct(h_field.shape, F32),
            jax.ShapeDtypeStruct((1, 2 * WAVES * MON * 3, CX * CY), F32),
            pltpu.SMEM((1,), F32),
        ),
        in_specs=[anywhere] * 10,
        out_specs=(anywhere,) * 4,
        scratch_shapes=[
            vmem(*focus.shape), pltpu.SMEM(permittivity.shape, F32), pltpu.SMEM(pml_x.shape, jnp.int32),
            pltpu.SMEM(pml_y.shape, jnp.int32), pltpu.SMEM(pml_z.shape, jnp.int32),
            pltpu.SMEM(monitor_z.shape, jnp.int32), pltpu.SMEM(omega.shape, F32),
            vmem(1, 2 * WAVES * MON * 3, CX * CY), pltpu.SMEM((1,), F32),
            vmem(3, CX + 1, CY + 8, CZ), vmem(3, CX + 1, CY + 8, CZ), pltpu.VMEM((CX, CY, CZ), jnp.int32),
            vmem(CX, CY, CZ), vmem(CX, CY, CZ), vmem(CX, CY, CZ), vmem(CX, CY, CZ),
            vmem(CX, 128), vmem(CY, 128),
            vmem(2, WAVES, STEPS, 8, 128), vmem(2, WAVES, 5, 8, 128), vmem(SLABS, STEPS, 40, 128),
            vmem(2 * TILES_Y, 128), vmem(2 * TILES_X, 128),
            vmem(2, CX, 128), vmem(8, 128), vmem(2, CY, 128), vmem(2, CX, 128), vmem(2, 8, 128), vmem(CX, 128), vmem(8, 128),
            vmem(2, CX, 128), vmem(8, 128), vmem(2, CY, 128), vmem(2, CX, 128), vmem(8, 128),
            vmem(STEPS, 2, CX, 128), vmem(STEPS, 8, 128),
            vmem(STEPS, 2, CY, 128), vmem(STEPS, 2, CX, 128), vmem(STEPS, 8, 128),
            vmem(early, 2, CY, 128), vmem(early, 2, CX, 128), vmem(early, 8, 128), vmem(early, 8, 128), vmem(3, CX, 128),
            vmem(early, 2, CY, 128), vmem(early, 2, CX, 128), vmem(early, 8, 128),
            vmem(6, early, 8, 128),
            dma(13), dma(9), dma(STEPS + 1, 12), dma(STEPS + 1, 12),
            dma(SLABS), dma(SLABS), dma(2), dma(2),
        ],
        compiler_params=pltpu.CompilerParams(
            collective_id=0, has_side_effects=True, vmem_limit_bytes=60 * 1024 * 1024),
    )(e_field, h_field, material, focus, permittivity, pml_x, pml_y, pml_z, monitor_z, omega)
    results = (e_out, h_out, spectra, objective)
    e_out, h_out, spectra, objective = pl.pallas_call(
        hand_on,
        out_shape=tuple(jax.ShapeDtypeStruct(a.shape, F32) for a in results),
        in_specs=[anywhere] * 4,
        out_specs=(anywhere,) * 4,
        scratch_shapes=[vmem(3, CX, CY, CZ), vmem(3, CX, CY, CZ), vmem(*spectra.shape), pltpu.SMEM((1,), F32), dma(2, 8)],
    )(*results)
    return e_out, h_out, spectra, objective.reshape(())


def solution(mesh):
    field = P("xy", None, None, None, "gz")
    return jax.shard_map(
        step,
        mesh=mesh,
        in_specs=(field, field, P("xy", None, None, "gz"), P(), P(), P(), P(), P(), P(), P("xy", None)),
        out_specs=(field, field, P("xy", None, None), P()),
        check_vma=False,
    )
```

```python
import functools

import jax
import jax.numpy as jnp
from jax import lax
from jax.experimental import pallas as pl
from jax.experimental.pallas import tpu as pltpu
from jax.sharding import PartitionSpec as P

MESH = pl.DeviceIdType.MESH
TILES_X = 8
TILES_Y = 8
SLABS = 4
STEPS = 4
WAVES = 4
MON = 3
DEPTH = 8
TIME_STEP = 0.5
SIGMA_PEAK = 0.8
CX, CY, CZ = 16, 32, 128
F32 = jnp.float32
EDGES = ((1, 0, -1), (-1, 0, 1), (1, -1, 0), (-1, 1, 0), (0, 1, -1), (0, -1, 1))


def roll(value, shift, axis):
    return pltpu.roll(value, shift % value.shape[axis], axis)


def grade(level):
    scaled = level.astype(F32) / DEPTH
    return scaled * scaled


def magnetic(sigma):
    loss = sigma * (0.5 * TIME_STEP)
    return (1.0 - loss) / (1.0 + loss), TIME_STEP / (1.0 + loss)


def electric(sigma, permit):
    loss = sigma * (0.5 * TIME_STEP) / permit
    return (1.0 - loss) / (1.0 + loss), TIME_STEP / (permit * (1.0 + loss))


def kernel(
    e_in, h_in, m_in, focus_in, permit_in, pml_x_in, pml_y_in, pml_z_in, monitor_in, omega_in,
    e_out, h_out, spec_out, objective_out,
    focus, permit, pml_x, pml_y, pml_z, monitor, omega, spec,
    es, hs, kinds, ca, cb, da, db, grades_x, grades_y, trig, acc, planes, first, second,
    hy, hz, dax, day, daz, dby, dbz,
    s_hy, s_hz, r_hx, r_hy, r_hz,
    s_ey, s_ez, r_ex, r_ey, r_ez,
    s_ux, s_uy, s_uz, s_far, top, r_ux, r_uy, r_uz, r_edge,
    local_sem, small_sem, send_sem, recv_sem, plane_send, plane_recv, total_send, total_recv,
):
    tile = lax.axis_index("xy")
    slab = lax.axis_index("gz")
    row, col = tile // TILES_Y, tile % TILES_Y
    half, core = slab // 2, slab % 2

    def valid(off):
        r, c, g = row + off[0], col + off[1], slab + off[2]
        return (r >= 0) & (r < TILES_X) & (c >= 0) & (c < TILES_Y) & (g >= 0) & (g < SLABS)

    def device(off):
        return ((row + off[0]) * TILES_Y + col + off[1], slab + off[2])

    def minus(off):
        return tuple(-o for o in off)

    class Move:
        def __init__(self, n, k, off, src, dst):
            self.off = off
            self.copy = lambda: pltpu.make_async_remote_copy(
                src_ref=src, dst_ref=dst, send_sem=send_sem.at[n, k], recv_sem=recv_sem.at[n, k],
                device_id=device(off), device_id_type=MESH)

        def start(self):
            @pl.when(valid(self.off))
            def _():
                self.copy().start()

        def wait_send(self):
            @pl.when(valid(self.off))
            def _():
                self.copy().wait_send()

        def wait_recv(self):
            @pl.when(valid(minus(self.off)))
            def _():
                self.copy().wait_recv()

    barrier = pltpu.get_barrier_semaphore()

    def greet(where):
        pl.semaphore_signal(barrier, inc=1, device_id=where, device_id_type=MESH)

    def in_row(i):
        k = (col * 2 + core + i) % (2 * TILES_Y)
        return row * TILES_Y + k // 2, half * 2 + k % 2

    def in_column(i):
        k = (row * 2 + half + i) % (2 * TILES_X)
        return k // 2 * TILES_Y + col, k % 2 * 2 + core

    for i in range(1, 2 * TILES_Y):
        greet(in_row(i))
    for i in range(1, 2 * TILES_X):
        greet(in_column(i))
    greet((tile, SLABS - 1 - slab))
    for off in EDGES:
        @pl.when(valid(off))
        def _(off=off):
            greet(device(off))

    loads = []
    for k in range(3):
        loads.append(pltpu.make_async_copy(
            h_in.at[0, k], hs.at[k, pl.ds(1, CX), pl.ds(8, CY), :], local_sem.at[k]))
    loads.append(pltpu.make_async_copy(m_in.at[0], kinds, local_sem.at[3]))
    for k in range(3):
        loads.append(pltpu.make_async_copy(
            e_in.at[0, k], es.at[k, pl.ds(0, CX), pl.ds(0, CY), :], local_sem.at[4 + k]))
    for load in loads:
        load.start()
    small = [pltpu.make_async_copy(source, target, small_sem.at[k]) for k, (source, target) in enumerate((
        (pml_x_in, pml_x), (pml_y_in, pml_y), (pml_z_in, pml_z), (permit_in, permit),
        (omega_in, omega), (monitor_in, monitor), (focus_in, focus)))]
    for load in small:
        load.start()

    lane8 = lax.broadcasted_iota(jnp.int32, (8, 128), 1)
    row8 = lax.broadcasted_iota(jnp.int32, (8, 128), 0)
    lane16 = lax.broadcasted_iota(jnp.int32, (16, 128), 1)
    row16 = lax.broadcasted_iota(jnp.int32, (16, 128), 0)
    lane32 = lax.broadcasted_iota(jnp.int32, (CY, 128), 1)
    row32 = lax.broadcasted_iota(jnp.int32, (CY, 128), 0)
    zero8 = jnp.zeros((8, 128), F32)

    def clear(off, *refs):
        @pl.when(jnp.logical_not(valid(minus(off))))
        def _():
            for ref in refs:
                ref[...] = jnp.zeros(ref.shape, F32)

    clear((1, 0, 0), r_hx, r_ux)
    clear((0, 1, 0), r_hy, r_uy)
    clear((0, 0, 1), r_hz, r_uz)
    clear((-1, 0, 0), r_ex)
    clear((0, -1, 0), r_ey)
    clear((0, 0, -1), r_ez)
    for k, off in enumerate(EDGES):
        clear(off, r_edge.at[k])

    def pack(total, field, source, start):
        for k in range(CY // 8):
            piece = roll(field[8 * k:8 * k + 8], start + k - source, 1)
            total = jnp.where(lane8 == start + k, piece, total)
        return total

    def unpack(packed, start, target):
        return jnp.concatenate([roll(packed, target - start - k, 1) for k in range(CY // 8)], axis=0)

    for k in range(3):
        loads[k].wait()

    total = zero8
    for x in range(CX):
        s_hy[0, x:x + 1, :] = hs[0, x + 1, 7 + CY:8 + CY, :]
        s_hy[1, x:x + 1, :] = hs[2, x + 1, 7 + CY:8 + CY, :]
        total = pack(total, hs[0, x + 1, 8:8 + CY, :], 127, 4 * x)
        total = pack(total, hs[1, x + 1, 8:8 + CY, :], 127, 64 + 4 * x)
    s_hz[...] = total

    greeted = 2 * TILES_Y - 1 + 2 * TILES_X - 1 + 1
    for off in EDGES:
        greeted = greeted + jnp.where(valid(off), 1, 0)
    pl.semaphore_wait(barrier, greeted)

    opening = [
        Move(STEPS, 0, (1, 0, 0), hs.at[pl.ds(1, 2), CX, pl.ds(8, CY), :], r_hx),
        Move(STEPS, 1, (0, 1, 0), s_hy, r_hy),
        Move(STEPS, 2, (0, 0, 1), s_hz, r_hz),
    ]
    for move in opening:
        move.start()

    for load in small:
        load.wait()
    for i in range(CX):
        grades_x[i:i + 1, :] = jnp.full((1, 128), grade(pml_x[row * CX + i]), F32)
    for j in range(CY):
        grades_y[j:j + 1, :] = jnp.full((1, 128), grade(pml_y[col * CY + j]), F32)

    def lay(k, levels):
        return jnp.where(lane8 == k, pml_z[slab * CZ + k], levels)

    along_z = grade(lax.fori_loop(0, CZ, lay, jnp.zeros((8, 128), jnp.int32)))
    along_z32 = jnp.concatenate([along_z] * 4, axis=0)

    loads[3].wait()

    def fill(x, _):
        g = jnp.full((CY, 128), grade(pml_x[row * CX + x]), F32)
        sigma = SIGMA_PEAK * ((g + grades_y[...]) + along_z32)
        kind = kinds[x]
        eps = jnp.full((CY, 128), permit[0], F32)
        for which in range(1, 4):
            eps = jnp.where(kind == which, permit[which], eps)
        ca[x], cb[x] = electric(sigma, eps)
        da[x], db[x] = magnetic(sigma)
        return 0

    lax.fori_loop(0, CX, fill, 0)
    total = zero8
    for x in range(CX):
        dby[x:x + 1, :] = db[x, CY - 1:CY, :]
        total = pack(total, db[x], 127, 4 * x)
    dbz[...] = total + roll(total, 64, 1)
    for k in (1, 2):
        es[k, CX, 0:CY, :] = jnp.zeros((CY, 128), F32)
    for x in range(CX):
        es[0, x, CY:CY + 1, :] = jnp.zeros((1, 128), F32)
        es[2, x, CY:CY + 1, :] = jnp.zeros((1, 128), F32)

    def below(ref, off, sigma):
        inside = jnp.where(valid(off), 1.0, 0.0).astype(F32)
        decay, drive = magnetic(sigma)
        ref[0] = decay * inside
        ref[1] = drive * inside

    g = grade(pml_x[jnp.maximum(row * CX - 1, 0)])
    below(dax, (-1, 0, 0), SIGMA_PEAK * ((g + grades_y[...]) + along_z32))
    g = grade(pml_y[jnp.maximum(col * CY - 1, 0)])
    below(day, (0, -1, 0), SIGMA_PEAK * ((grades_x[...] + g) + along_z32[0:CX]))
    g = grade(pml_z[jnp.maximum(slab * CZ - 1, 0)])
    packed_x = zero8
    for i in range(CX):
        packed_x = jnp.where((lane8 % 64) // 4 == i, grades_x[i:i + 1, :], packed_x)
    packed_y = zero8
    for k in range(CY // 8):
        packed_y = jnp.where(lane8 % 4 == k, grades_y[8 * k:8 * k + 8, :], packed_y)
    below(daz, (0, 0, -1), SIGMA_PEAK * ((packed_x + packed_y) + g))

    for n in range(STEPS):
        for w in range(WAVES):
            phase = jnp.full((8, 128), omega[w] * ((n + 1) * TIME_STEP), F32)
            trig[0, w, n] = jnp.cos(phase)
            trig[1, w, n] = -jnp.sin(phase)
    acc[...] = jnp.zeros(acc.shape, F32)

    for k in range(3):
        loads[4 + k].wait()
    for move in opening:
        move.wait_recv()
    hs[1, 0, 8:8 + CY, :] = r_hx[0]
    hs[2, 0, 8:8 + CY, :] = r_hx[1]
    hy[...] = r_hy[...]
    hz[...] = r_hz[...]
    for move in opening:
        move.wait_send()

    def electric_planes(n, where, last, packs):
        for x in where:
            hs[0, x + 1, 7:8, :] = hy[0, x:x + 1, :]
            hs[2, x + 1, 7:8, :] = hy[1, x:x + 1, :]
        halo = hz[...]
        low, high, high2 = packs
        for x in where:
            h0 = hs[0, x + 1, 8:8 + CY, :]
            h1 = hs[1, x + 1, 8:8 + CY, :]
            h2 = hs[2, x + 1, 8:8 + CY, :]
            h0y = hs[0, x + 1, 7:7 + CY, :]
            h2y = hs[2, x + 1, 7:7 + CY, :]
            h1x = hs[1, x, 8:8 + CY, :]
            h2x = hs[2, x, 8:8 + CY, :]
            h0z = jnp.where(lane32 == 0, unpack(halo, 4 * x, 0), roll(h0, 1, 1))
            h1z = jnp.where(lane32 == 0, unpack(halo, 64 + 4 * x, 0), roll(h1, 1, 1))
            decay, drive = ca[x], cb[x]
            e0 = decay * es[0, x, 0:CY, :] + drive * ((h2 - h2y) - (h1 - h1z))
            e1 = decay * es[1, x, 0:CY, :] + drive * ((h0 - h0z) - (h2 - h2x))
            e2 = decay * es[2, x, 0:CY, :] + drive * ((h1 - h1x) - (h0 - h0y))
            es[0, x, 0:CY, :] = e0
            es[1, x, 0:CY, :] = e1
            es[2, x, 0:CY, :] = e2
            s_ey[n, 0, x:x + 1, :] = e0[0:1]
            s_ey[n, 1, x:x + 1, :] = e2[0:1]
            low = pack(pack(low, e0, 0, 4 * x), e1, 0, 64 + 4 * x)
            if not last:
                for k, e in enumerate((e0, e1, e2)):
                    top[k, x:x + 1, :] = e[CY - 1:CY]
                high = pack(pack(high, e0, 127, 4 * x), e1, 127, 64 + 4 * x)
                high2 = pack(pack(high2, e2, 127, 4 * x), e2, 127, 64 + 4 * x)
                if x == CX - 1:
                    e0z = jnp.where(lane32 == 127, 0.0, roll(e0, -1, 1))
                    e0y = jnp.where(row32 == CY - 1, 0.0, roll(e0, -1, 0))
                    s_ux[n, 0] = (e0z - e0) + e2
                    s_ux[n, 1] = (e0 - e0y) - e1
        return low, high, high2

    def electric_phase(n, last):
        first_moves = [Move(n, 0, (-1, 0, 0), es.at[pl.ds(1, 2), 0, pl.ds(0, CY), :], r_ex.at[n])]
        moves = [
            Move(n, 1, (0, -1, 0), s_ey.at[n], r_ey.at[n]),
            Move(n, 2, (0, 0, -1), s_ez.at[n], r_ez.at[n]),
        ]
        if not last:
            sources = (s_ez.at[n], s_far.at[n], es.at[0, CX - 1, pl.ds(0, 8), :],
                       es.at[1, 0, pl.ds(CY - 8, 8), :], s_ez.at[n], s_far.at[n])
            edges = [Move(n, 6 + k, off, sources[k], r_edge.at[k, n]) for k, off in enumerate(EDGES)]
            first_moves = edges[2:4] + [Move(n, 3, (1, 0, 0), s_ux.at[n], r_ux.at[n])] + first_moves
            moves = [moves[0], Move(n, 4, (0, 1, 0), s_uy.at[n], r_uy.at[n])] + edges[0:2] + edges[4:6] + [
                moves[1], Move(n, 5, (0, 0, 1), s_uz.at[n], r_uz.at[n])]
        packs = electric_planes(n, (0,) if last else (0, CX - 1), last, (zero8, zero8, zero8))
        for move in first_moves:
            move.start()
        low, high, high2 = electric_planes(n, range(1, CX if last else CX - 1), last, packs)
        s_ez[n] = low
        if not last:
            e0, e1, e2 = top[0], top[1], top[2]
            s_uy[n, 0] = (e1 - jnp.where(lane16 == 127, 0.0, roll(e1, -1, 1))) - e2
            s_uy[n, 1] = (jnp.where(row16 == CX - 1, 0.0, roll(e1, -1, 0)) - e1) + e0
            s_far[n] = high2
            up = roll(high2, -1, 0)
            e2y = jnp.where(row8 < 7, up, jnp.where(lane8 % 4 == 3, 0.0, roll(up, -1, 1)))
            e2x = jnp.where(lane8 >= 124, 0.0, roll(high2, -4, 1))
            e01 = roll(high, 64, 1)
            s_uz[n] = jnp.where(lane8 < 64, (e2y - high2) + e01, (high2 - e2x) - e01)
        if not last:
            for move in moves:
                move.start()
        return first_moves, moves

    def below_phase(n):
        curl1 = r_ux[n, 0] + jnp.where(lane32 == 127, unpack(r_edge[0, n], 60, 127), 0.0) - es[2, 0, 0:CY, :]
        curl2 = r_ux[n, 1] - jnp.where(row32 == CY - 1, r_edge[2, n, 0:1, :], 0.0) + es[1, 0, 0:CY, :]
        hs[1, 0, 8:8 + CY, :] = dax[0] * hs[1, 0, 8:8 + CY, :] - dax[1] * curl1
        hs[2, 0, 8:8 + CY, :] = dax[0] * hs[2, 0, 8:8 + CY, :] - dax[1] * curl2

        corner = jnp.broadcast_to(r_edge[4, n, 7:8, :], (CX, 128))
        corner = jnp.sum(jnp.where(lane16 == 67 + 4 * row16, corner, 0.0), axis=1, keepdims=True)
        curl0 = r_uy[n, 0] - jnp.where(lane16 == 127, corner, 0.0) + s_ey[n, 1]
        curl2 = r_uy[n, 1] + jnp.where(row16 == CX - 1, r_edge[3, n, 7:8, :], 0.0) - s_ey[n, 0]
        hy[0] = day[0] * hy[0] - day[1] * curl0
        hy[1] = day[0] * hy[1] - day[1] * curl2

        own = roll(s_ez[n], 64, 1)
        up_edge = roll(roll(r_edge[5, n], -1, 0), 3, 1)
        up_edge = jnp.where((row8 == 7) & (lane8 % 4 == 3), up_edge, 0.0) - own
        far_edge = jnp.where(lane8 >= 124, roll(r_edge[1, n], 124, 1), 0.0) - own
        curl = r_uz[n] + jnp.where(lane8 < 64, up_edge, -far_edge)
        hz[...] = daz[0] * hz[...] - daz[1] * curl

    def magnetic_phase():
        for x in range(CX):
            e0 = es[0, x, 0:CY, :]
            e1 = es[1, x, 0:CY, :]
            e2 = es[2, x, 0:CY, :]
            e0y = es[0, x, 1:1 + CY, :]
            e2y = es[2, x, 1:1 + CY, :]
            e1x = es[1, x + 1, 0:CY, :]
            e2x = es[2, x + 1, 0:CY, :]
            e0z = jnp.where(lane32 == 127, 0.0, roll(e0, -1, 1))
            e1z = jnp.where(lane32 == 127, 0.0, roll(e1, -1, 1))
            decay, drive = da[x], db[x]
            h0 = decay * hs[0, x + 1, 8:8 + CY, :] - drive * ((e2y - e2) - (e1z - e1))
            h1 = decay * hs[1, x + 1, 8:8 + CY, :] - drive * ((e0z - e0) - (e2x - e2))
            h2 = decay * hs[2, x + 1, 8:8 + CY, :] - drive * ((e1x - e1) - (e0y - e0))
            hs[0, x + 1, 8:8 + CY, :] = h0
            hs[1, x + 1, 8:8 + CY, :] = h1
            hs[2, x + 1, 8:8 + CY, :] = h2

    def arrivals(n, moves):
        for move in moves:
            move.wait_send()
        for move in moves:
            if move.off[0] == 0:
                move.wait_recv()
        term0, term2, packed = dby[...] * r_ey[n, 1], dby[...] * r_ey[n, 0], dbz[...] * r_ez[n]
        for x in range(CX):
            hs[0, x + 1, 7 + CY:8 + CY, :] = hs[0, x + 1, 7 + CY:8 + CY, :] - term0[x:x + 1]
            hs[2, x + 1, 7 + CY:8 + CY, :] = hs[2, x + 1, 7 + CY:8 + CY, :] + term2[x:x + 1]
        for x in range(CX):
            h0 = hs[0, x + 1, 8:8 + CY, :] + jnp.where(lane32 == 127, unpack(packed, 64 + 4 * x, 127), 0.0)
            h1 = hs[1, x + 1, 8:8 + CY, :] - jnp.where(lane32 == 127, unpack(packed, 4 * x, 127), 0.0)
            hs[0, x + 1, 8:8 + CY, :] = h0
            hs[1, x + 1, 8:8 + CY, :] = h1
        for move in reversed(moves):
            if move.off[0] != 0:
                move.wait_recv()
        drive = db[CX - 1]
        hs[1, CX, 8:8 + CY, :] = hs[1, CX, 8:8 + CY, :] + drive * r_ex[n, 1]
        hs[2, CX, 8:8 + CY, :] = hs[2, CX, 8:8 + CY, :] - drive * r_ex[n, 0]

    def extract_planes(n):
        weights = []
        for c in range(3):
            weight = jnp.zeros((16, 128), F32)
            for p in range(MON):
                weight = jnp.where((row16 == 3 * p + c) & (lane16 + slab * CZ == monitor[p]), 1.0, weight)
            weights += [weight.astype(jnp.bfloat16)] * 3
        weights = jnp.concatenate(weights, axis=1)
        planes[slab, n, 32:40, :] = zero8
        for k in range(0, CX // 4, 2):
            pieces = []
            for c in range(3):
                rest = es[c, 4 * k:4 * k + 8, 0:CY, :].reshape(256, 128)
                for _ in range(3):
                    pieces.append(rest.astype(jnp.bfloat16))
                    rest = rest - pieces[-1].astype(F32)
            total = lax.dot_general(weights, jnp.concatenate(pieces, axis=1), (((1,), (1,)), ((), ())),
                                    preferred_element_type=F32)
            for j in range(2):
                part = total[:, 128 * j:128 * j + 128]
                planes[slab, n, 8 * (k + j):8 * (k + j) + 8, :] = part[0:8]
                planes[slab, n, 32 + k + j:33 + k + j, :] = part[8:9]
        for k in range(5):
            whole = planes[slab, n, 8 * k:8 * k + 8, :]
            for q in range(2):
                for w in range(WAVES):
                    acc[q, w, k] = acc[q, w, k] + trig[q, w, n] * whole

    def plane_move(i, source):
        return pltpu.make_async_remote_copy(
            src_ref=planes.at[source], dst_ref=planes.at[source],
            send_sem=plane_send.at[i - 1], recv_sem=plane_recv.at[i - 1],
            device_id=(tile, (slab + i) % SLABS), device_id_type=MESH)

    for n in range(STEPS - 1):
        moves = sum(electric_phase(n, False), [])
        extract_planes(n)
        magnetic_phase()
        arrivals(n, moves)
        below_phase(n)

    moves, later = electric_phase(STEPS - 1, True)
    extract_planes(STEPS - 1)

    part = jnp.zeros((1, 128), F32)
    odd = zero8
    for w in range(WAVES):
        odd = odd + (acc[0, w, 4] * acc[0, w, 4] + acc[1, w, 4] * acc[1, w, 4])
    for k in range(4):
        power = zero8
        for w in range(WAVES):
            power = power + (acc[0, w, k] * acc[0, w, k] + acc[1, w, k] * acc[1, w, k])
        power = jnp.sum(power, axis=0, keepdims=True) + odd[k:k + 1]
        part = part + power * focus[0:1, 128 * k:128 * k + 128]

    def send_totals(stage, mine, where):
        buf = (first, second)[stage]
        for i in sorted(range(1, 16), key=lambda i: -min(i, 16 - i)):
            pltpu.make_async_remote_copy(
                src_ref=buf.at[pl.ds(mine, 1), :], dst_ref=buf.at[pl.ds(mine, 1), :],
                send_sem=total_send.at[stage], recv_sem=total_recv.at[stage],
                device_id=where(i), device_id_type=MESH).start()

    def all_totals(stage):
        buf = (first, second)[stage].at[pl.ds(0, 15), :]
        return pltpu.make_async_remote_copy(
            src_ref=buf, dst_ref=buf, send_sem=total_send.at[stage], recv_sem=total_recv.at[stage],
            device_id=(in_row, in_column)[stage](1), device_id_type=MESH)

    first[pl.ds(col * 2 + core, 1), :] = part
    send_totals(0, col * 2 + core, in_row)
    for move in later:
        move.start()
    for i in range(1, SLABS):
        plane_move(i, slab).start()
    moves = moves + later

    stores = [pltpu.make_async_copy(
        es.at[k, pl.ds(0, CX), pl.ds(0, CY), :], e_out.at[0, k], local_sem.at[7 + k]) for k in range(3)]
    for store in stores:
        store.start()
    magnetic_phase()
    arrivals(STEPS - 1, moves)
    for k in range(3):
        stores.append(pltpu.make_async_copy(
            hs.at[k, pl.ds(1, CX), pl.ds(8, CY), :], h_out.at[0, k], local_sem.at[10 + k]))
        stores[-1].start()

    all_totals(0).wait_recv()
    second[pl.ds(row * 2 + half, 1), :] = jnp.sum(first[...], axis=0, keepdims=True)
    send_totals(1, row * 2 + half, in_column)

    for i in range(1, SLABS):
        plane_move(i, (slab + SLABS - i) % SLABS).wait_recv()
    for k in range(5):
        spectrum = [[zero8] * WAVES, [zero8] * WAVES]
        for n in range(STEPS):
            whole = planes[0, n, 8 * k:8 * k + 8, :]
            for g in range(1, SLABS):
                whole = whole + planes[g, n, 8 * k:8 * k + 8, :]
            for q in range(2):
                for w in range(WAVES):
                    spectrum[q][w] = spectrum[q][w] + trig[q, w, n] * whole
        for q in range(2):
            for w in range(WAVES):
                base = 36 * q + 9 * w
                if k < 4:
                    spec[0, base:base + 8, 128 * k:128 * k + 128] = spectrum[q][w]
                else:
                    for j in range(4):
                        spec[0, base + 8:base + 9, 128 * j:128 * j + 128] = spectrum[q][w][j:j + 1]

    stores.append(pltpu.make_async_copy(spec, spec_out, small_sem.at[7]))
    stores[-1].start()
    for i in range(1, SLABS):
        plane_move(i, slab).wait_send()
    all_totals(0).wait_send()
    for store in stores:
        store.wait()
    all_totals(1).wait_recv()
    cells = TILES_X * TILES_Y * WAVES * MON * 3 * CX * CY
    objective_out[0] = jnp.sum(second[...]) / jnp.float32(cells)
    all_totals(1).wait_send()


def hand_on(e_in, h_in, s_in, o_in, e_out, h_out, s_out, o_out, sem):
    pieces = [(e_in.at[0, k], e_out.at[0, k]) for k in range(3)]
    pieces += [(h_in.at[0, k], h_out.at[0, k]) for k in range(3)]
    pieces += [(s_in, s_out), (o_in, o_out)]
    copies = [pltpu.make_async_copy(a, b, sem.at[k]) for k, (a, b) in enumerate(pieces)]
    for copy in copies:
        copy.start()
    for copy in copies:
        copy.wait()


def step(e_field, h_field, material, permittivity, pml_x, pml_y, pml_z, monitor_z, omega, focus):
    vmem = lambda *shape: pltpu.VMEM(shape, F32)
    dma = lambda *shape: pltpu.SemaphoreType.DMA(shape)
    anywhere = pl.BlockSpec(memory_space=pl.ANY)
    early = STEPS - 1
    e_out, h_out, spectra, objective = pl.pallas_call(
        kernel,
        out_shape=(
            pltpu.VMEM(e_field.shape, F32),
            pltpu.VMEM(h_field.shape, F32),
            pltpu.VMEM((1, 2 * WAVES * MON * 3, CX * CY), F32),
            pltpu.SMEM((1,), F32),
        ),
        in_specs=[anywhere] * 10,
        out_specs=(anywhere,) * 3 + (pl.BlockSpec(memory_space=pltpu.SMEM),),
        scratch_shapes=[
            vmem(*focus.shape), pltpu.SMEM(permittivity.shape, F32), pltpu.SMEM(pml_x.shape, jnp.int32),
            pltpu.SMEM(pml_y.shape, jnp.int32), pltpu.SMEM(pml_z.shape, jnp.int32),
            pltpu.SMEM(monitor_z.shape, jnp.int32), pltpu.SMEM(omega.shape, F32),
            vmem(1, 2 * WAVES * MON * 3, CX * CY),
            vmem(3, CX + 1, CY + 8, CZ), vmem(3, CX + 1, CY + 8, CZ), pltpu.VMEM((CX, CY, CZ), jnp.int32),
            vmem(CX, CY, CZ), vmem(CX, CY, CZ), vmem(CX, CY, CZ), vmem(CX, CY, CZ),
            vmem(CX, 128), vmem(CY, 128),
            vmem(2, WAVES, STEPS, 8, 128), vmem(2, WAVES, 5, 8, 128), vmem(SLABS, STEPS, 40, 128),
            vmem(2 * TILES_Y, 128), vmem(2 * TILES_X, 128),
            vmem(2, CX, 128), vmem(8, 128), vmem(2, CY, 128), vmem(2, CX, 128), vmem(2, 8, 128), vmem(CX, 128), vmem(8, 128),
            vmem(2, CX, 128), vmem(8, 128), vmem(2, CY, 128), vmem(2, CX, 128), vmem(8, 128),
            vmem(STEPS, 2, CX, 128), vmem(STEPS, 8, 128),
            vmem(STEPS, 2, CY, 128), vmem(STEPS, 2, CX, 128), vmem(STEPS, 8, 128),
            vmem(early, 2, CY, 128), vmem(early, 2, CX, 128), vmem(early, 8, 128), vmem(early, 8, 128), vmem(3, CX, 128),
            vmem(early, 2, CY, 128), vmem(early, 2, CX, 128), vmem(early, 8, 128),
            vmem(6, early, 8, 128),
            dma(13), dma(8), dma(STEPS + 1, 12), dma(STEPS + 1, 12),
            dma(SLABS), dma(SLABS), dma(2), dma(2),
        ],
        compiler_params=pltpu.CompilerParams(
            collective_id=0, has_side_effects=True, vmem_limit_bytes=60 * 1024 * 1024),
    )(e_field, h_field, material, focus, permittivity, pml_x, pml_y, pml_z, monitor_z, omega)
    results = (e_out, h_out, spectra, objective)
    e_out, h_out, spectra, objective = pl.pallas_call(
        hand_on,
        out_shape=tuple(jax.ShapeDtypeStruct(a.shape, F32) for a in results),
        in_specs=[anywhere] * 4,
        out_specs=(anywhere,) * 4,
        scratch_shapes=[dma(8)],
        compiler_params=pltpu.CompilerParams(vmem_limit_bytes=1024 * 1024),
    )(*results)
    return e_out, h_out, spectra, objective.reshape(())


def solution(mesh):
    field = P("xy", None, None, None, "gz")
    return jax.shard_map(
        step,
        mesh=mesh,
        in_specs=(field, field, P("xy", None, None, "gz"), P(), P(), P(), P(), P(), P(), P("xy", None)),
        out_specs=(field, field, P("xy", None, None), P()),
        check_vma=False,
    )
```

```python
import functools

import jax
import jax.numpy as jnp
from jax import lax
from jax.experimental import pallas as pl
from jax.experimental.pallas import tpu as pltpu
from jax.sharding import PartitionSpec as P

MESH = pl.DeviceIdType.MESH
TILES_X = 8
TILES_Y = 8
SLABS = 4
STEPS = 4
WAVES = 4
MON = 3
DEPTH = 8
TIME_STEP = 0.5
SIGMA_PEAK = 0.8
CX, CY, CZ = 16, 32, 128
F32 = jnp.float32
EDGES = ((1, 0, -1), (-1, 0, 1), (1, -1, 0), (-1, 1, 0), (0, 1, -1), (0, -1, 1))


def roll(value, shift, axis):
    return pltpu.roll(value, shift % value.shape[axis], axis)


def grade(level):
    scaled = level.astype(F32) / DEPTH
    return scaled * scaled


def magnetic(sigma):
    loss = sigma * (0.5 * TIME_STEP)
    return (1.0 - loss) / (1.0 + loss), TIME_STEP / (1.0 + loss)


def electric(sigma, permit):
    loss = sigma * (0.5 * TIME_STEP) / permit
    return (1.0 - loss) / (1.0 + loss), TIME_STEP / (permit * (1.0 + loss))


def kernel(
    e_in, h_in, m_in, focus_in, permit_in, pml_x_in, pml_y_in, pml_z_in, monitor_in, omega_in,
    e_out, h_out, spec_out, objective_out,
    focus, permit, pml_x, pml_y, pml_z, monitor, omega, spec,
    es, hs, kinds, ca, cb, da, db, grades_x, grades_y, trig, acc, planes, first, second,
    hy, hz, dax, day, daz, dby, dbz,
    s_hy, s_hz, r_hx, r_hy, r_hz,
    s_ey, s_ez, r_ex, r_ey, r_ez,
    s_ux, s_uy, s_uz, s_far, top, r_ux, r_uy, r_uz, r_edge,
    local_sem, small_sem, send_sem, recv_sem, plane_send, plane_recv, total_send, total_recv, ready,
):
    tile = lax.axis_index("xy")
    slab = lax.axis_index("gz")
    row, col = tile // TILES_Y, tile % TILES_Y
    half, core = slab // 2, slab % 2

    def valid(off):
        r, c, g = row + off[0], col + off[1], slab + off[2]
        return (r >= 0) & (r < TILES_X) & (c >= 0) & (c < TILES_Y) & (g >= 0) & (g < SLABS)

    def device(off):
        return ((row + off[0]) * TILES_Y + col + off[1], slab + off[2])

    def minus(off):
        return tuple(-o for o in off)

    class Move:
        def __init__(self, n, k, off, src, dst):
            self.off = off
            self.copy = lambda: pltpu.make_async_remote_copy(
                src_ref=src, dst_ref=dst, send_sem=send_sem.at[n, k], recv_sem=recv_sem.at[n, k],
                device_id=device(off), device_id_type=MESH)

        def start(self):
            @pl.when(valid(self.off))
            def _():
                self.copy().start()

        def wait_send(self):
            @pl.when(valid(self.off))
            def _():
                self.copy().wait_send()

        def wait_recv(self):
            @pl.when(valid(minus(self.off)))
            def _():
                self.copy().wait_recv()

    barrier = pltpu.get_barrier_semaphore()

    def greet(where):
        pl.semaphore_signal(barrier, inc=1, device_id=where, device_id_type=MESH)

    def in_row(i):
        k = (col * 2 + core + i) % (2 * TILES_Y)
        return row * TILES_Y + k // 2, half * 2 + k % 2

    def in_column(i):
        k = (row * 2 + half + i) % (2 * TILES_X)
        return k // 2 * TILES_Y + col, k % 2 * 2 + core

    for i in (1, 2, 14, 15):
        greet(in_row(i))
        greet(in_column(i))
    greet((tile, SLABS - 1 - slab))
    for off in EDGES:
        @pl.when(valid(off))
        def _(off=off):
            greet(device(off))

    loads = []
    for k in range(3):
        loads.append(pltpu.make_async_copy(
            h_in.at[0, k], hs.at[k, pl.ds(1, CX), pl.ds(8, CY), :], local_sem.at[k]))
    loads.append(pltpu.make_async_copy(m_in.at[0], kinds, local_sem.at[3]))
    for k in range(3):
        loads.append(pltpu.make_async_copy(
            e_in.at[0, k], es.at[k, pl.ds(0, CX), pl.ds(0, CY), :], local_sem.at[4 + k]))
    for load in loads:
        load.start()
    small = [pltpu.make_async_copy(source, target, small_sem.at[k]) for k, (source, target) in enumerate((
        (pml_x_in, pml_x), (pml_y_in, pml_y), (pml_z_in, pml_z), (permit_in, permit),
        (omega_in, omega), (monitor_in, monitor), (focus_in, focus)))]
    for load in small:
        load.start()

    lane8 = lax.broadcasted_iota(jnp.int32, (8, 128), 1)
    row8 = lax.broadcasted_iota(jnp.int32, (8, 128), 0)
    lane16 = lax.broadcasted_iota(jnp.int32, (16, 128), 1)
    row16 = lax.broadcasted_iota(jnp.int32, (16, 128), 0)
    lane32 = lax.broadcasted_iota(jnp.int32, (CY, 128), 1)
    row32 = lax.broadcasted_iota(jnp.int32, (CY, 128), 0)
    zero8 = jnp.zeros((8, 128), F32)

    def clear(off, *refs):
        @pl.when(jnp.logical_not(valid(minus(off))))
        def _():
            for ref in refs:
                ref[...] = jnp.zeros(ref.shape, F32)

    clear((1, 0, 0), r_hx, r_ux)
    clear((0, 1, 0), r_hy, r_uy)
    clear((0, 0, 1), r_hz, r_uz)
    clear((-1, 0, 0), r_ex)
    clear((0, -1, 0), r_ey)
    clear((0, 0, -1), r_ez)
    for k, off in enumerate(EDGES):
        clear(off, r_edge.at[k])

    def pack(total, field, source, start):
        for k in range(CY // 8):
            piece = roll(field[8 * k:8 * k + 8], start + k - source, 1)
            total = jnp.where(lane8 == start + k, piece, total)
        return total

    def unpack(packed, start, target):
        return jnp.concatenate([roll(packed, target - start - k, 1) for k in range(CY // 8)], axis=0)

    for k in range(3):
        loads[k].wait()

    total = zero8
    for x in range(CX):
        s_hy[0, x:x + 1, :] = hs[0, x + 1, 7 + CY:8 + CY, :]
        s_hy[1, x:x + 1, :] = hs[2, x + 1, 7 + CY:8 + CY, :]
        total = pack(total, hs[0, x + 1, 8:8 + CY, :], 127, 4 * x)
        total = pack(total, hs[1, x + 1, 8:8 + CY, :], 127, 64 + 4 * x)
    s_hz[...] = total

    greeted = 9
    for off in EDGES:
        greeted = greeted + jnp.where(valid(off), 1, 0)
    pl.semaphore_wait(barrier, greeted)

    opening = [
        Move(STEPS, 0, (1, 0, 0), hs.at[pl.ds(1, 2), CX, pl.ds(8, CY), :], r_hx),
        Move(STEPS, 1, (0, 1, 0), s_hy, r_hy),
        Move(STEPS, 2, (0, 0, 1), s_hz, r_hz),
    ]
    for move in opening:
        move.start()

    def tell(k, distance):
        for i in (distance, 16 - distance):
            pl.semaphore_signal(ready.at[k, 0], inc=1, device_id=in_row(i), device_id_type=MESH)
            pl.semaphore_signal(ready.at[k, 1], inc=1, device_id=in_column(i), device_id_type=MESH)

    def hear(k):
        pl.semaphore_wait(ready.at[k, 0], 2)
        pl.semaphore_wait(ready.at[k, 1], 2)

    tell(0, 2)

    for load in small:
        load.wait()
    for i in range(CX):
        grades_x[i:i + 1, :] = jnp.full((1, 128), grade(pml_x[row * CX + i]), F32)
    for j in range(CY):
        grades_y[j:j + 1, :] = jnp.full((1, 128), grade(pml_y[col * CY + j]), F32)

    def lay(k, levels):
        return jnp.where(lane8 == k, pml_z[slab * CZ + k], levels)

    along_z = grade(lax.fori_loop(0, CZ, lay, jnp.zeros((8, 128), jnp.int32)))
    along_z32 = jnp.concatenate([along_z] * 4, axis=0)

    loads[3].wait()

    def fill(x, _):
        g = jnp.full((CY, 128), grade(pml_x[row * CX + x]), F32)
        sigma = SIGMA_PEAK * ((g + grades_y[...]) + along_z32)
        kind = kinds[x]
        eps = jnp.full((CY, 128), permit[0], F32)
        for which in range(1, 4):
            eps = jnp.where(kind == which, permit[which], eps)
        ca[x], cb[x] = electric(sigma, eps)
        da[x], db[x] = magnetic(sigma)
        return 0

    lax.fori_loop(0, CX, fill, 0)
    total = zero8
    for x in range(CX):
        dby[x:x + 1, :] = db[x, CY - 1:CY, :]
        total = pack(total, db[x], 127, 4 * x)
    dbz[...] = total + roll(total, 64, 1)
    for k in (1, 2):
        es[k, CX, 0:CY, :] = jnp.zeros((CY, 128), F32)
    for x in range(CX):
        es[0, x, CY:CY + 1, :] = jnp.zeros((1, 128), F32)
        es[2, x, CY:CY + 1, :] = jnp.zeros((1, 128), F32)

    def below(ref, off, sigma):
        inside = jnp.where(valid(off), 1.0, 0.0).astype(F32)
        decay, drive = magnetic(sigma)
        ref[0] = decay * inside
        ref[1] = drive * inside

    g = grade(pml_x[jnp.maximum(row * CX - 1, 0)])
    below(dax, (-1, 0, 0), SIGMA_PEAK * ((g + grades_y[...]) + along_z32))
    g = grade(pml_y[jnp.maximum(col * CY - 1, 0)])
    below(day, (0, -1, 0), SIGMA_PEAK * ((grades_x[...] + g) + along_z32[0:CX]))
    g = grade(pml_z[jnp.maximum(slab * CZ - 1, 0)])
    packed_x = zero8
    for i in range(CX):
        packed_x = jnp.where((lane8 % 64) // 4 == i, grades_x[i:i + 1, :], packed_x)
    packed_y = zero8
    for k in range(CY // 8):
        packed_y = jnp.where(lane8 % 4 == k, grades_y[8 * k:8 * k + 8, :], packed_y)
    below(daz, (0, 0, -1), SIGMA_PEAK * ((packed_x + packed_y) + g))

    for n in range(STEPS):
        for w in range(WAVES):
            phase = jnp.full((8, 128), omega[w] * ((n + 1) * TIME_STEP), F32)
            trig[0, w, n] = jnp.cos(phase)
            trig[1, w, n] = -jnp.sin(phase)
    acc[...] = jnp.zeros(acc.shape, F32)

    for k in range(3):
        loads[4 + k].wait()
    hear(0)
    tell(1, 4)
    for move in opening:
        move.wait_recv()
    hs[1, 0, 8:8 + CY, :] = r_hx[0]
    hs[2, 0, 8:8 + CY, :] = r_hx[1]
    hy[...] = r_hy[...]
    hz[...] = r_hz[...]
    for move in opening:
        move.wait_send()

    def electric_planes(n, where, last, packs):
        for x in where:
            hs[0, x + 1, 7:8, :] = hy[0, x:x + 1, :]
            hs[2, x + 1, 7:8, :] = hy[1, x:x + 1, :]
        halo = hz[...]
        low, high, high2 = packs
        for x in where:
            h0 = hs[0, x + 1, 8:8 + CY, :]
            h1 = hs[1, x + 1, 8:8 + CY, :]
            h2 = hs[2, x + 1, 8:8 + CY, :]
            h0y = hs[0, x + 1, 7:7 + CY, :]
            h2y = hs[2, x + 1, 7:7 + CY, :]
            h1x = hs[1, x, 8:8 + CY, :]
            h2x = hs[2, x, 8:8 + CY, :]
            h0z = jnp.where(lane32 == 0, unpack(halo, 4 * x, 0), roll(h0, 1, 1))
            h1z = jnp.where(lane32 == 0, unpack(halo, 64 + 4 * x, 0), roll(h1, 1, 1))
            decay, drive = ca[x], cb[x]
            e0 = decay * es[0, x, 0:CY, :] + drive * ((h2 - h2y) - (h1 - h1z))
            e1 = decay * es[1, x, 0:CY, :] + drive * ((h0 - h0z) - (h2 - h2x))
            e2 = decay * es[2, x, 0:CY, :] + drive * ((h1 - h1x) - (h0 - h0y))
            es[0, x, 0:CY, :] = e0
            es[1, x, 0:CY, :] = e1
            es[2, x, 0:CY, :] = e2
            s_ey[n, 0, x:x + 1, :] = e0[0:1]
            s_ey[n, 1, x:x + 1, :] = e2[0:1]
            low = pack(pack(low, e0, 0, 4 * x), e1, 0, 64 + 4 * x)
            if not last:
                for k, e in enumerate((e0, e1, e2)):
                    top[k, x:x + 1, :] = e[CY - 1:CY]
                high = pack(pack(high, e0, 127, 4 * x), e1, 127, 64 + 4 * x)
                high2 = pack(pack(high2, e2, 127, 4 * x), e2, 127, 64 + 4 * x)
                if x == CX - 1:
                    e0z = jnp.where(lane32 == 127, 0.0, roll(e0, -1, 1))
                    e0y = jnp.where(row32 == CY - 1, 0.0, roll(e0, -1, 0))
                    s_ux[n, 0] = (e0z - e0) + e2
                    s_ux[n, 1] = (e0 - e0y) - e1
        return low, high, high2

    def electric_phase(n, last):
        first_moves = [Move(n, 0, (-1, 0, 0), es.at[pl.ds(1, 2), 0, pl.ds(0, CY), :], r_ex.at[n])]
        moves = [
            Move(n, 1, (0, -1, 0), s_ey.at[n], r_ey.at[n]),
            Move(n, 2, (0, 0, -1), s_ez.at[n], r_ez.at[n]),
        ]
        if not last:
            sources = (s_ez.at[n], s_far.at[n], es.at[0, CX - 1, pl.ds(0, 8), :],
                       es.at[1, 0, pl.ds(CY - 8, 8), :], s_ez.at[n], s_far.at[n])
            edges = [Move(n, 6 + k, off, sources[k], r_edge.at[k, n]) for k, off in enumerate(EDGES)]
            first_moves = edges[2:4] + [Move(n, 3, (1, 0, 0), s_ux.at[n], r_ux.at[n])] + first_moves
            moves = [moves[0], Move(n, 4, (0, 1, 0), s_uy.at[n], r_uy.at[n])] + edges[0:2] + edges[4:6] + [
                moves[1], Move(n, 5, (0, 0, 1), s_uz.at[n], r_uz.at[n])]
        packs = electric_planes(n, (0,) if last else (0, CX - 1), last, (zero8, zero8, zero8))
        for move in first_moves:
            move.start()
        low, high, high2 = electric_planes(n, range(1, CX if last else CX - 1), last, packs)
        s_ez[n] = low
        if not last:
            e0, e1, e2 = top[0], top[1], top[2]
            s_uy[n, 0] = (e1 - jnp.where(lane16 == 127, 0.0, roll(e1, -1, 1))) - e2
            s_uy[n, 1] = (jnp.where(row16 == CX - 1, 0.0, roll(e1, -1, 0)) - e1) + e0
            s_far[n] = high2
            up = roll(high2, -1, 0)
            e2y = jnp.where(row8 < 7, up, jnp.where(lane8 % 4 == 3, 0.0, roll(up, -1, 1)))
            e2x = jnp.where(lane8 >= 124, 0.0, roll(high2, -4, 1))
            e01 = roll(high, 64, 1)
            s_uz[n] = jnp.where(lane8 < 64, (e2y - high2) + e01, (high2 - e2x) - e01)
        if not last:
            for move in moves:
                move.start()
        return first_moves, moves

    def below_phase(n):
        curl1 = r_ux[n, 0] + jnp.where(lane32 == 127, unpack(r_edge[0, n], 60, 127), 0.0) - es[2, 0, 0:CY, :]
        curl2 = r_ux[n, 1] - jnp.where(row32 == CY - 1, r_edge[2, n, 0:1, :], 0.0) + es[1, 0, 0:CY, :]
        hs[1, 0, 8:8 + CY, :] = dax[0] * hs[1, 0, 8:8 + CY, :] - dax[1] * curl1
        hs[2, 0, 8:8 + CY, :] = dax[0] * hs[2, 0, 8:8 + CY, :] - dax[1] * curl2

        corner = jnp.broadcast_to(r_edge[4, n, 7:8, :], (CX, 128))
        corner = jnp.sum(jnp.where(lane16 == 67 + 4 * row16, corner, 0.0), axis=1, keepdims=True)
        curl0 = r_uy[n, 0] - jnp.where(lane16 == 127, corner, 0.0) + s_ey[n, 1]
        curl2 = r_uy[n, 1] + jnp.where(row16 == CX - 1, r_edge[3, n, 7:8, :], 0.0) - s_ey[n, 0]
        hy[0] = day[0] * hy[0] - day[1] * curl0
        hy[1] = day[0] * hy[1] - day[1] * curl2

        own = roll(s_ez[n], 64, 1)
        up_edge = roll(roll(r_edge[5, n], -1, 0), 3, 1)
        up_edge = jnp.where((row8 == 7) & (lane8 % 4 == 3), up_edge, 0.0) - own
        far_edge = jnp.where(lane8 >= 124, roll(r_edge[1, n], 124, 1), 0.0) - own
        curl = r_uz[n] + jnp.where(lane8 < 64, up_edge, -far_edge)
        hz[...] = daz[0] * hz[...] - daz[1] * curl

    def magnetic_phase():
        for x in range(CX):
            e0 = es[0, x, 0:CY, :]
            e1 = es[1, x, 0:CY, :]
            e2 = es[2, x, 0:CY, :]
            e0y = es[0, x, 1:1 + CY, :]
            e2y = es[2, x, 1:1 + CY, :]
            e1x = es[1, x + 1, 0:CY, :]
            e2x = es[2, x + 1, 0:CY, :]
            e0z = jnp.where(lane32 == 127, 0.0, roll(e0, -1, 1))
            e1z = jnp.where(lane32 == 127, 0.0, roll(e1, -1, 1))
            decay, drive = da[x], db[x]
            h0 = decay * hs[0, x + 1, 8:8 + CY, :] - drive * ((e2y - e2) - (e1z - e1))
            h1 = decay * hs[1, x + 1, 8:8 + CY, :] - drive * ((e0z - e0) - (e2x - e2))
            h2 = decay * hs[2, x + 1, 8:8 + CY, :] - drive * ((e1x - e1) - (e0y - e0))
            hs[0, x + 1, 8:8 + CY, :] = h0
            hs[1, x + 1, 8:8 + CY, :] = h1
            hs[2, x + 1, 8:8 + CY, :] = h2

    def arrivals(n, moves):
        for move in moves:
            move.wait_send()
        for move in moves:
            if move.off[0] == 0:
                move.wait_recv()
        term0, term2, packed = dby[...] * r_ey[n, 1], dby[...] * r_ey[n, 0], dbz[...] * r_ez[n]
        for x in range(CX):
            hs[0, x + 1, 7 + CY:8 + CY, :] = hs[0, x + 1, 7 + CY:8 + CY, :] - term0[x:x + 1]
            hs[2, x + 1, 7 + CY:8 + CY, :] = hs[2, x + 1, 7 + CY:8 + CY, :] + term2[x:x + 1]
        for x in range(CX):
            h0 = hs[0, x + 1, 8:8 + CY, :] + jnp.where(lane32 == 127, unpack(packed, 64 + 4 * x, 127), 0.0)
            h1 = hs[1, x + 1, 8:8 + CY, :] - jnp.where(lane32 == 127, unpack(packed, 4 * x, 127), 0.0)
            hs[0, x + 1, 8:8 + CY, :] = h0
            hs[1, x + 1, 8:8 + CY, :] = h1
        for move in reversed(moves):
            if move.off[0] != 0:
                move.wait_recv()
        drive = db[CX - 1]
        hs[1, CX, 8:8 + CY, :] = hs[1, CX, 8:8 + CY, :] + drive * r_ex[n, 1]
        hs[2, CX, 8:8 + CY, :] = hs[2, CX, 8:8 + CY, :] - drive * r_ex[n, 0]

    def extract_planes(n):
        weights = []
        for c in range(3):
            weight = jnp.zeros((16, 128), F32)
            for p in range(MON):
                weight = jnp.where((row16 == 3 * p + c) & (lane16 + slab * CZ == monitor[p]), 1.0, weight)
            weights += [weight.astype(jnp.bfloat16)] * 3
        weights = jnp.concatenate(weights, axis=1)
        planes[slab, n, 32:40, :] = zero8
        for k in range(0, CX // 4, 2):
            pieces = []
            for c in range(3):
                rest = es[c, 4 * k:4 * k + 8, 0:CY, :].reshape(256, 128)
                for _ in range(3):
                    pieces.append(rest.astype(jnp.bfloat16))
                    rest = rest - pieces[-1].astype(F32)
            total = lax.dot_general(weights, jnp.concatenate(pieces, axis=1), (((1,), (1,)), ((), ())),
                                    preferred_element_type=F32)
            for j in range(2):
                part = total[:, 128 * j:128 * j + 128]
                planes[slab, n, 8 * (k + j):8 * (k + j) + 8, :] = part[0:8]
                planes[slab, n, 32 + k + j:33 + k + j, :] = part[8:9]
        for k in range(5):
            whole = planes[slab, n, 8 * k:8 * k + 8, :]
            for q in range(2):
                for w in range(WAVES):
                    acc[q, w, k] = acc[q, w, k] + trig[q, w, n] * whole

    def plane_move(i, source):
        return pltpu.make_async_remote_copy(
            src_ref=planes.at[source], dst_ref=planes.at[source],
            send_sem=plane_send.at[i - 1], recv_sem=plane_recv.at[i - 1],
            device_id=(tile, (slab + i) % SLABS), device_id_type=MESH)

    for n in range(STEPS - 1):
        moves = sum(electric_phase(n, False), [])
        extract_planes(n)
        magnetic_phase()
        if n == 0:
            hear(1)
        arrivals(n, moves)
        below_phase(n)

    moves, later = electric_phase(STEPS - 1, True)
    extract_planes(STEPS - 1)

    part = jnp.zeros((1, 128), F32)
    odd = zero8
    for w in range(WAVES):
        odd = odd + (acc[0, w, 4] * acc[0, w, 4] + acc[1, w, 4] * acc[1, w, 4])
    for k in range(4):
        power = zero8
        for w in range(WAVES):
            power = power + (acc[0, w, k] * acc[0, w, k] + acc[1, w, k] * acc[1, w, k])
        power = jnp.sum(power, axis=0, keepdims=True) + odd[k:k + 1]
        part = part + power * focus[0:1, 128 * k:128 * k + 128]

    def send_totals(stage, mine, where):
        buf = (first, second)[stage]
        for i in sorted(range(1, 16), key=lambda i: -min(i, 16 - i)):
            pltpu.make_async_remote_copy(
                src_ref=buf.at[pl.ds(mine, 1), :], dst_ref=buf.at[pl.ds(mine, 1), :],
                send_sem=total_send.at[stage], recv_sem=total_recv.at[stage],
                device_id=where(i), device_id_type=MESH).start()

    def all_totals(stage):
        buf = (first, second)[stage].at[pl.ds(0, 15), :]
        return pltpu.make_async_remote_copy(
            src_ref=buf, dst_ref=buf, send_sem=total_send.at[stage], recv_sem=total_recv.at[stage],
            device_id=(in_row, in_column)[stage](1), device_id_type=MESH)

    first[pl.ds(col * 2 + core, 1), :] = part
    send_totals(0, col * 2 + core, in_row)
    for move in later:
        move.start()
    for i in range(1, SLABS):
        plane_move(i, slab).start()
    moves = moves + later

    stores = [pltpu.make_async_copy(
        es.at[k, pl.ds(0, CX), pl.ds(0, CY), :], e_out.at[0, k], local_sem.at[7 + k]) for k in range(3)]
    for store in stores:
        store.start()
    magnetic_phase()
    arrivals(STEPS - 1, moves)
    for k in range(3):
        stores.append(pltpu.make_async_copy(
            hs.at[k, pl.ds(1, CX), pl.ds(8, CY), :], h_out.at[0, k], local_sem.at[10 + k]))
        stores[-1].start()

    all_totals(0).wait_recv()
    second[pl.ds(row * 2 + half, 1), :] = jnp.sum(first[...], axis=0, keepdims=True)
    send_totals(1, row * 2 + half, in_column)

    for i in range(1, SLABS):
        plane_move(i, (slab + SLABS - i) % SLABS).wait_recv()
    for k in range(5):
        spectrum = [[zero8] * WAVES, [zero8] * WAVES]
        for n in range(STEPS):
            whole = planes[0, n, 8 * k:8 * k + 8, :]
            for g in range(1, SLABS):
                whole = whole + planes[g, n, 8 * k:8 * k + 8, :]
            for q in range(2):
                for w in range(WAVES):
                    spectrum[q][w] = spectrum[q][w] + trig[q, w, n] * whole
        for q in range(2):
            for w in range(WAVES):
                base = 36 * q + 9 * w
                if k < 4:
                    spec[0, base:base + 8, 128 * k:128 * k + 128] = spectrum[q][w]
                else:
                    for j in range(4):
                        spec[0, base + 8:base + 9, 128 * j:128 * j + 128] = spectrum[q][w][j:j + 1]

    stores.append(pltpu.make_async_copy(spec, spec_out, small_sem.at[7]))
    stores[-1].start()
    for i in range(1, SLABS):
        plane_move(i, slab).wait_send()
    all_totals(0).wait_send()
    for store in stores:
        store.wait()
    all_totals(1).wait_recv()
    cells = TILES_X * TILES_Y * WAVES * MON * 3 * CX * CY
    objective_out[0] = jnp.sum(second[...]) / jnp.float32(cells)
    all_totals(1).wait_send()


def hand_on(e_in, h_in, s_in, o_in, e_out, h_out, s_out, o_out, sem):
    pieces = [(e_in.at[0, k], e_out.at[0, k]) for k in range(3)]
    pieces += [(h_in.at[0, k], h_out.at[0, k]) for k in range(3)]
    pieces += [(s_in, s_out), (o_in, o_out)]
    copies = [pltpu.make_async_copy(a, b, sem.at[k]) for k, (a, b) in enumerate(pieces)]
    for copy in copies:
        copy.start()
    for copy in copies:
        copy.wait()


def step(e_field, h_field, material, permittivity, pml_x, pml_y, pml_z, monitor_z, omega, focus):
    vmem = lambda *shape: pltpu.VMEM(shape, F32)
    dma = lambda *shape: pltpu.SemaphoreType.DMA(shape)
    anywhere = pl.BlockSpec(memory_space=pl.ANY)
    early = STEPS - 1
    e_out, h_out, spectra, objective = pl.pallas_call(
        kernel,
        out_shape=(
            pltpu.VMEM(e_field.shape, F32),
            pltpu.VMEM(h_field.shape, F32),
            pltpu.VMEM((1, 2 * WAVES * MON * 3, CX * CY), F32),
            pltpu.SMEM((1,), F32),
        ),
        in_specs=[anywhere] * 10,
        out_specs=(anywhere,) * 3 + (pl.BlockSpec(memory_space=pltpu.SMEM),),
        scratch_shapes=[
            vmem(*focus.shape), pltpu.SMEM(permittivity.shape, F32), pltpu.SMEM(pml_x.shape, jnp.int32),
            pltpu.SMEM(pml_y.shape, jnp.int32), pltpu.SMEM(pml_z.shape, jnp.int32),
            pltpu.SMEM(monitor_z.shape, jnp.int32), pltpu.SMEM(omega.shape, F32),
            vmem(1, 2 * WAVES * MON * 3, CX * CY),
            vmem(3, CX + 1, CY + 8, CZ), vmem(3, CX + 1, CY + 8, CZ), pltpu.VMEM((CX, CY, CZ), jnp.int32),
            vmem(CX, CY, CZ), vmem(CX, CY, CZ), vmem(CX, CY, CZ), vmem(CX, CY, CZ),
            vmem(CX, 128), vmem(CY, 128),
            vmem(2, WAVES, STEPS, 8, 128), vmem(2, WAVES, 5, 8, 128), vmem(SLABS, STEPS, 40, 128),
            vmem(2 * TILES_Y, 128), vmem(2 * TILES_X, 128),
            vmem(2, CX, 128), vmem(8, 128), vmem(2, CY, 128), vmem(2, CX, 128), vmem(2, 8, 128), vmem(CX, 128), vmem(8, 128),
            vmem(2, CX, 128), vmem(8, 128), vmem(2, CY, 128), vmem(2, CX, 128), vmem(8, 128),
            vmem(STEPS, 2, CX, 128), vmem(STEPS, 8, 128),
            vmem(STEPS, 2, CY, 128), vmem(STEPS, 2, CX, 128), vmem(STEPS, 8, 128),
            vmem(early, 2, CY, 128), vmem(early, 2, CX, 128), vmem(early, 8, 128), vmem(early, 8, 128), vmem(3, CX, 128),
            vmem(early, 2, CY, 128), vmem(early, 2, CX, 128), vmem(early, 8, 128),
            vmem(6, early, 8, 128),
            dma(13), dma(8), dma(STEPS + 1, 12), dma(STEPS + 1, 12),
            dma(SLABS), dma(SLABS), dma(2), dma(2), pltpu.SemaphoreType.REGULAR((2, 2)),
        ],
        compiler_params=pltpu.CompilerParams(
            collective_id=0, has_side_effects=True, vmem_limit_bytes=60 * 1024 * 1024),
    )(e_field, h_field, material, focus, permittivity, pml_x, pml_y, pml_z, monitor_z, omega)
    results = (e_out, h_out, spectra, objective)
    e_out, h_out, spectra, objective = pl.pallas_call(
        hand_on,
        out_shape=tuple(jax.ShapeDtypeStruct(a.shape, F32) for a in results),
        in_specs=[anywhere] * 4,
        out_specs=(anywhere,) * 4,
        scratch_shapes=[dma(8)],
        compiler_params=pltpu.CompilerParams(vmem_limit_bytes=1024 * 1024),
    )(*results)
    return e_out, h_out, spectra, objective.reshape(())


def solution(mesh):
    field = P("xy", None, None, None, "gz")
    return jax.shard_map(
        step,
        mesh=mesh,
        in_specs=(field, field, P("xy", None, None, "gz"), P(), P(), P(), P(), P(), P(), P("xy", None)),
        out_specs=(field, field, P("xy", None, None), P()),
        check_vma=False,
    )
```

```python
import functools

import jax
import jax.numpy as jnp
from jax import lax
from jax.experimental import pallas as pl
from jax.experimental.pallas import tpu as pltpu
from jax.sharding import PartitionSpec as P

MESH = pl.DeviceIdType.MESH
TILES_X = 8
TILES_Y = 8
SLABS = 4
STEPS = 4
WAVES = 4
MON = 3
DEPTH = 8
TIME_STEP = 0.5
SIGMA_PEAK = 0.8
CX, CY, CZ = 16, 32, 128
F32 = jnp.float32
EDGES = ((1, 0, -1), (-1, 0, 1), (1, -1, 0), (-1, 1, 0), (0, 1, -1), (0, -1, 1))


def roll(value, shift, axis):
    return pltpu.roll(value, shift % value.shape[axis], axis)


def grade(level):
    scaled = level.astype(F32) / DEPTH
    return scaled * scaled


def magnetic(sigma):
    loss = sigma * (0.5 * TIME_STEP)
    return (1.0 - loss) / (1.0 + loss), TIME_STEP / (1.0 + loss)


def electric(sigma, permit):
    loss = sigma * (0.5 * TIME_STEP) / permit
    return (1.0 - loss) / (1.0 + loss), TIME_STEP / (permit * (1.0 + loss))


def kernel(
    e_in, h_in, m_in, focus_in, permit_in, pml_x_in, pml_y_in, pml_z_in, monitor_in, omega_in,
    e_out, h_out, spec_out, objective_out,
    focus, permit, pml_x, pml_y, pml_z, monitor, omega, spec,
    es, hs, kinds, ca, cb, da, db, grades_x, grades_y, trig, acc, planes, first, second,
    hy, hz, dax, day, daz, dby, dbz,
    s_hy, s_hz, r_hx, r_hy, r_hz,
    s_ey, s_ez, r_ex, r_ey, r_ez,
    s_ux, s_uy, s_uz, s_far, s_first, top, r_ux, r_uy, r_uz, r_edge,
    local_sem, small_sem, send_sem, recv_sem, plane_send, plane_recv, total_send, total_recv, ready,
):
    tile = lax.axis_index("xy")
    slab = lax.axis_index("gz")
    row, col = tile // TILES_Y, tile % TILES_Y
    half, core = slab // 2, slab % 2

    def valid(off):
        r, c, g = row + off[0], col + off[1], slab + off[2]
        return (r >= 0) & (r < TILES_X) & (c >= 0) & (c < TILES_Y) & (g >= 0) & (g < SLABS)

    def device(off):
        return ((row + off[0]) * TILES_Y + col + off[1], slab + off[2])

    def minus(off):
        return tuple(-o for o in off)

    class Move:
        def __init__(self, n, k, off, src, dst):
            self.off = off
            self.copy = lambda: pltpu.make_async_remote_copy(
                src_ref=src, dst_ref=dst, send_sem=send_sem.at[n, k], recv_sem=recv_sem.at[n, k],
                device_id=device(off), device_id_type=MESH)

        def start(self):
            @pl.when(valid(self.off))
            def _():
                self.copy().start()

        def wait_send(self):
            @pl.when(valid(self.off))
            def _():
                self.copy().wait_send()

        def wait_recv(self):
            @pl.when(valid(minus(self.off)))
            def _():
                self.copy().wait_recv()

    barrier = pltpu.get_barrier_semaphore()

    def greet(where):
        pl.semaphore_signal(barrier, inc=1, device_id=where, device_id_type=MESH)

    def in_row(i):
        k = (col * 2 + core + i) % (2 * TILES_Y)
        return row * TILES_Y + k // 2, half * 2 + k % 2

    def in_column(i):
        k = (row * 2 + half + i) % (2 * TILES_X)
        return k // 2 * TILES_Y + col, k % 2 * 2 + core

    for i in (1, 2, 14, 15):
        greet(in_row(i))
        greet(in_column(i))
    greet((tile, SLABS - 1 - slab))
    for off in EDGES:
        @pl.when(valid(off))
        def _(off=off):
            greet(device(off))

    loads = []
    for k in range(3):
        loads.append(pltpu.make_async_copy(
            h_in.at[0, k], hs.at[k, pl.ds(1, CX), pl.ds(8, CY), :], local_sem.at[k]))
    loads.append(pltpu.make_async_copy(m_in.at[0], kinds, local_sem.at[3]))
    for k in range(3):
        loads.append(pltpu.make_async_copy(
            e_in.at[0, k], es.at[k, pl.ds(0, CX), pl.ds(0, CY), :], local_sem.at[4 + k]))
    for load in loads:
        load.start()
    small = [pltpu.make_async_copy(source, target, small_sem.at[k]) for k, (source, target) in enumerate((
        (pml_x_in, pml_x), (pml_y_in, pml_y), (pml_z_in, pml_z), (permit_in, permit),
        (omega_in, omega), (monitor_in, monitor), (focus_in, focus)))]
    for load in small:
        load.start()

    lane8 = lax.broadcasted_iota(jnp.int32, (8, 128), 1)
    row8 = lax.broadcasted_iota(jnp.int32, (8, 128), 0)
    lane16 = lax.broadcasted_iota(jnp.int32, (16, 128), 1)
    row16 = lax.broadcasted_iota(jnp.int32, (16, 128), 0)
    lane32 = lax.broadcasted_iota(jnp.int32, (CY, 128), 1)
    row32 = lax.broadcasted_iota(jnp.int32, (CY, 128), 0)
    zero8 = jnp.zeros((8, 128), F32)

    def clear(off, *refs):
        @pl.when(jnp.logical_not(valid(minus(off))))
        def _():
            for ref in refs:
                ref[...] = jnp.zeros(ref.shape, F32)

    clear((1, 0, 0), r_hx, r_ux)
    clear((0, 1, 0), r_hy, r_uy)
    clear((0, 0, 1), r_hz, r_uz)
    clear((-1, 0, 0), r_ex)
    clear((0, -1, 0), r_ey)
    clear((0, 0, -1), r_ez)
    for k, off in enumerate(EDGES):
        clear(off, r_edge.at[k])

    def pack(total, field, source, start):
        for k in range(CY // 8):
            piece = roll(field[8 * k:8 * k + 8], start + k - source, 1)
            total = jnp.where(lane8 == start + k, piece, total)
        return total

    def unpack(packed, start, target):
        return jnp.concatenate([roll(packed, target - start - k, 1) for k in range(CY // 8)], axis=0)

    for k in range(3):
        loads[k].wait()

    total = zero8
    for x in range(CX):
        s_hy[0, x:x + 1, :] = hs[0, x + 1, 7 + CY:8 + CY, :]
        s_hy[1, x:x + 1, :] = hs[2, x + 1, 7 + CY:8 + CY, :]
        total = pack(total, hs[0, x + 1, 8:8 + CY, :], 127, 4 * x)
        total = pack(total, hs[1, x + 1, 8:8 + CY, :], 127, 64 + 4 * x)
    s_hz[...] = total

    greeted = 9
    for off in EDGES:
        greeted = greeted + jnp.where(valid(off), 1, 0)
    pl.semaphore_wait(barrier, greeted)

    opening = [
        Move(STEPS, 0, (1, 0, 0), hs.at[pl.ds(1, 2), CX, pl.ds(8, CY), :], r_hx),
        Move(STEPS, 1, (0, 1, 0), s_hy, r_hy),
        Move(STEPS, 2, (0, 0, 1), s_hz, r_hz),
    ]
    for move in opening:
        move.start()

    def tell(k, distance):
        for i in (distance, 16 - distance):
            pl.semaphore_signal(ready.at[k, 0], inc=1, device_id=in_row(i), device_id_type=MESH)
            pl.semaphore_signal(ready.at[k, 1], inc=1, device_id=in_column(i), device_id_type=MESH)

    def hear(k):
        pl.semaphore_wait(ready.at[k, 0], 2)
        pl.semaphore_wait(ready.at[k, 1], 2)

    tell(0, 2)

    for load in small:
        load.wait()
    for i in range(CX):
        grades_x[i:i + 1, :] = jnp.full((1, 128), grade(pml_x[row * CX + i]), F32)
    for j in range(CY):
        grades_y[j:j + 1, :] = jnp.full((1, 128), grade(pml_y[col * CY + j]), F32)

    def lay(k, levels):
        return jnp.where(lane8 == k, pml_z[slab * CZ + k], levels)

    along_z = grade(lax.fori_loop(0, CZ, lay, jnp.zeros((8, 128), jnp.int32)))
    along_z32 = jnp.concatenate([along_z] * 4, axis=0)

    loads[3].wait()

    def fill(x, _):
        g = jnp.full((CY, 128), grade(pml_x[row * CX + x]), F32)
        sigma = SIGMA_PEAK * ((g + grades_y[...]) + along_z32)
        kind = kinds[x]
        eps = jnp.full((CY, 128), permit[0], F32)
        for which in range(1, 4):
            eps = jnp.where(kind == which, permit[which], eps)
        ca[x], cb[x] = electric(sigma, eps)
        da[x], db[x] = magnetic(sigma)
        return 0

    lax.fori_loop(0, CX, fill, 0)
    total = zero8
    for x in range(CX):
        dby[x:x + 1, :] = db[x, CY - 1:CY, :]
        total = pack(total, db[x], 127, 4 * x)
    dbz[...] = total + roll(total, 64, 1)
    for k in (1, 2):
        es[k, CX, 0:CY, :] = jnp.zeros((CY, 128), F32)
    for x in range(CX):
        es[0, x, CY:CY + 1, :] = jnp.zeros((1, 128), F32)
        es[2, x, CY:CY + 1, :] = jnp.zeros((1, 128), F32)

    def below(ref, off, sigma):
        inside = jnp.where(valid(off), 1.0, 0.0).astype(F32)
        decay, drive = magnetic(sigma)
        ref[0] = decay * inside
        ref[1] = drive * inside

    g = grade(pml_x[jnp.maximum(row * CX - 1, 0)])
    below(dax, (-1, 0, 0), SIGMA_PEAK * ((g + grades_y[...]) + along_z32))
    g = grade(pml_y[jnp.maximum(col * CY - 1, 0)])
    below(day, (0, -1, 0), SIGMA_PEAK * ((grades_x[...] + g) + along_z32[0:CX]))
    g = grade(pml_z[jnp.maximum(slab * CZ - 1, 0)])
    packed_x = zero8
    for i in range(CX):
        packed_x = jnp.where((lane8 % 64) // 4 == i, grades_x[i:i + 1, :], packed_x)
    packed_y = zero8
    for k in range(CY // 8):
        packed_y = jnp.where(lane8 % 4 == k, grades_y[8 * k:8 * k + 8, :], packed_y)
    below(daz, (0, 0, -1), SIGMA_PEAK * ((packed_x + packed_y) + g))

    for n in range(STEPS):
        for w in range(WAVES):
            phase = jnp.full((8, 128), omega[w] * ((n + 1) * TIME_STEP), F32)
            trig[0, w, n] = jnp.cos(phase)
            trig[1, w, n] = -jnp.sin(phase)
    acc[...] = jnp.zeros(acc.shape, F32)

    for k in range(3):
        loads[4 + k].wait()
    hear(0)
    tell(1, 4)
    for move in opening:
        move.wait_recv()
    hs[1, 0, 8:8 + CY, :] = r_hx[0]
    hs[2, 0, 8:8 + CY, :] = r_hx[1]
    hy[...] = r_hy[...]
    hz[...] = r_hz[...]
    for move in opening:
        move.wait_send()

    def electric_planes(n, where, last, packs):
        for x in where:
            hs[0, x + 1, 7:8, :] = hy[0, x:x + 1, :]
            hs[2, x + 1, 7:8, :] = hy[1, x:x + 1, :]
        halo = hz[...]
        low, high, high2 = packs
        for x in where:
            h0 = hs[0, x + 1, 8:8 + CY, :]
            h1 = hs[1, x + 1, 8:8 + CY, :]
            h2 = hs[2, x + 1, 8:8 + CY, :]
            h0y = hs[0, x + 1, 7:7 + CY, :]
            h2y = hs[2, x + 1, 7:7 + CY, :]
            h1x = hs[1, x, 8:8 + CY, :]
            h2x = hs[2, x, 8:8 + CY, :]
            h0z = jnp.where(lane32 == 0, unpack(halo, 4 * x, 0), roll(h0, 1, 1))
            h1z = jnp.where(lane32 == 0, unpack(halo, 64 + 4 * x, 0), roll(h1, 1, 1))
            decay, drive = ca[x], cb[x]
            e0 = decay * es[0, x, 0:CY, :] + drive * ((h2 - h2y) - (h1 - h1z))
            e1 = decay * es[1, x, 0:CY, :] + drive * ((h0 - h0z) - (h2 - h2x))
            e2 = decay * es[2, x, 0:CY, :] + drive * ((h1 - h1x) - (h0 - h0y))
            es[0, x, 0:CY, :] = e0
            es[1, x, 0:CY, :] = e1
            es[2, x, 0:CY, :] = e2
            s_ey[n, 0, x:x + 1, :] = e0[0:1]
            s_ey[n, 1, x:x + 1, :] = e2[0:1]
            low = pack(pack(low, e0, 0, 4 * x), e1, 0, 64 + 4 * x)
            if not last:
                for k, e in enumerate((e0, e1, e2)):
                    top[k, x:x + 1, :] = e[CY - 1:CY]
                high = pack(pack(high, e0, 127, 4 * x), e1, 127, 64 + 4 * x)
                high2 = pack(high2, e2, 127, 4 * x)
                if x == CX - 1:
                    e0z = jnp.where(lane32 == 127, 0.0, roll(e0, -1, 1))
                    e0y = jnp.where(row32 == CY - 1, 0.0, roll(e0, -1, 0))
                    s_ux[n, 0] = (e0z - e0) + e2
                    s_ux[n, 1] = (e0 - e0y) - e1
        return low, high, high2

    def electric_phase(n, last):
        first_moves = [Move(n, 0, (-1, 0, 0), es.at[pl.ds(1, 2), 0, pl.ds(0, CY), :], r_ex.at[n])]
        moves = [
            Move(n, 1, (0, -1, 0), s_ey.at[n], r_ey.at[n]),
            Move(n, 2, (0, 0, -1), s_ez.at[n], r_ez.at[n]),
        ]
        if not last:
            sources = (s_first.at[n, 0], s_first.at[n, 1], es.at[0, CX - 1, pl.ds(0, 8), :],
                       es.at[1, 0, pl.ds(CY - 8, 8), :], s_ez.at[n], s_far.at[n])
            edges = [Move(n, 6 + k, off, sources[k], r_edge.at[k, n]) for k, off in enumerate(EDGES)]
            first_moves = edges[2:4] + [Move(n, 3, (1, 0, 0), s_ux.at[n], r_ux.at[n])] + first_moves + edges[0:2]
            moves = [moves[0], Move(n, 4, (0, 1, 0), s_uy.at[n], r_uy.at[n])] + edges[4:6] + [
                moves[1], Move(n, 5, (0, 0, 1), s_uz.at[n], r_uz.at[n])]
        packs = (zero8, zero8, zero8) if last else electric_planes(n, (0, CX - 1), last, (zero8, zero8, zero8))
        if not last:
            s_first[n, 0] = packs[0]
            s_first[n, 1] = packs[2]
        if not last:
            for move in first_moves:
                move.start()
        low, high, high2 = electric_planes(n, range(CX) if last else range(1, CX - 1), last, packs)
        s_ez[n] = low
        if not last:
            e0, e1, e2 = top[0], top[1], top[2]
            s_uy[n, 0] = (e1 - jnp.where(lane16 == 127, 0.0, roll(e1, -1, 1))) - e2
            s_uy[n, 1] = (jnp.where(row16 == CX - 1, 0.0, roll(e1, -1, 0)) - e1) + e0
            s_far[n] = high2
            high2 = high2 + roll(high2, 64, 1)
            up = roll(high2, -1, 0)
            e2y = jnp.where(row8 < 7, up, jnp.where(lane8 % 4 == 3, 0.0, roll(up, -1, 1)))
            e2x = jnp.where(lane8 >= 124, 0.0, roll(high2, -4, 1))
            e01 = roll(high, 64, 1)
            s_uz[n] = jnp.where(lane8 < 64, (e2y - high2) + e01, (high2 - e2x) - e01)
        if not last:
            for move in moves:
                move.start()
        return first_moves, moves

    def below_phase(n):
        curl1 = r_ux[n, 0] + jnp.where(lane32 == 127, unpack(r_edge[0, n], 60, 127), 0.0) - es[2, 0, 0:CY, :]
        curl2 = r_ux[n, 1] - jnp.where(row32 == CY - 1, r_edge[2, n, 0:1, :], 0.0) + es[1, 0, 0:CY, :]
        hs[1, 0, 8:8 + CY, :] = dax[0] * hs[1, 0, 8:8 + CY, :] - dax[1] * curl1
        hs[2, 0, 8:8 + CY, :] = dax[0] * hs[2, 0, 8:8 + CY, :] - dax[1] * curl2

        corner = jnp.broadcast_to(r_edge[4, n, 7:8, :], (CX, 128))
        corner = jnp.sum(jnp.where(lane16 == 67 + 4 * row16, corner, 0.0), axis=1, keepdims=True)
        curl0 = r_uy[n, 0] - jnp.where(lane16 == 127, corner, 0.0) + s_ey[n, 1]
        curl2 = r_uy[n, 1] + jnp.where(row16 == CX - 1, r_edge[3, n, 7:8, :], 0.0) - s_ey[n, 0]
        hy[0] = day[0] * hy[0] - day[1] * curl0
        hy[1] = day[0] * hy[1] - day[1] * curl2

        own = roll(s_ez[n], 64, 1)
        up_edge = roll(roll(r_edge[5, n], -1, 0), 3, 1)
        up_edge = jnp.where((row8 == 7) & (lane8 % 4 == 3), up_edge, 0.0) - own
        far_edge = jnp.where(lane8 >= 124, roll(r_edge[1, n], 124, 1), 0.0) - own
        curl = r_uz[n] + jnp.where(lane8 < 64, up_edge, -far_edge)
        hz[...] = daz[0] * hz[...] - daz[1] * curl

    def magnetic_phase():
        for x in range(CX):
            e0 = es[0, x, 0:CY, :]
            e1 = es[1, x, 0:CY, :]
            e2 = es[2, x, 0:CY, :]
            e0y = es[0, x, 1:1 + CY, :]
            e2y = es[2, x, 1:1 + CY, :]
            e1x = es[1, x + 1, 0:CY, :]
            e2x = es[2, x + 1, 0:CY, :]
            e0z = jnp.where(lane32 == 127, 0.0, roll(e0, -1, 1))
            e1z = jnp.where(lane32 == 127, 0.0, roll(e1, -1, 1))
            decay, drive = da[x], db[x]
            h0 = decay * hs[0, x + 1, 8:8 + CY, :] - drive * ((e2y - e2) - (e1z - e1))
            h1 = decay * hs[1, x + 1, 8:8 + CY, :] - drive * ((e0z - e0) - (e2x - e2))
            h2 = decay * hs[2, x + 1, 8:8 + CY, :] - drive * ((e1x - e1) - (e0y - e0))
            hs[0, x + 1, 8:8 + CY, :] = h0
            hs[1, x + 1, 8:8 + CY, :] = h1
            hs[2, x + 1, 8:8 + CY, :] = h2

    def arrivals(n, moves):
        for move in moves:
            move.wait_send()
        for move in moves:
            if move.off[0] == 0:
                move.wait_recv()
        term0, term2, packed = dby[...] * r_ey[n, 1], dby[...] * r_ey[n, 0], dbz[...] * r_ez[n]
        for x in range(CX):
            hs[0, x + 1, 7 + CY:8 + CY, :] = hs[0, x + 1, 7 + CY:8 + CY, :] - term0[x:x + 1]
            hs[2, x + 1, 7 + CY:8 + CY, :] = hs[2, x + 1, 7 + CY:8 + CY, :] + term2[x:x + 1]
        for x in range(CX):
            h0 = hs[0, x + 1, 8:8 + CY, :] + jnp.where(lane32 == 127, unpack(packed, 64 + 4 * x, 127), 0.0)
            h1 = hs[1, x + 1, 8:8 + CY, :] - jnp.where(lane32 == 127, unpack(packed, 4 * x, 127), 0.0)
            hs[0, x + 1, 8:8 + CY, :] = h0
            hs[1, x + 1, 8:8 + CY, :] = h1
        for move in reversed(moves):
            if move.off[0] != 0:
                move.wait_recv()
        drive = db[CX - 1]
        hs[1, CX, 8:8 + CY, :] = hs[1, CX, 8:8 + CY, :] + drive * r_ex[n, 1]
        hs[2, CX, 8:8 + CY, :] = hs[2, CX, 8:8 + CY, :] - drive * r_ex[n, 0]

    def extract_planes(n):
        weights = []
        for c in range(3):
            weight = jnp.zeros((16, 128), F32)
            for p in range(MON):
                weight = jnp.where((row16 == 3 * p + c) & (lane16 + slab * CZ == monitor[p]), 1.0, weight)
            weights += [weight.astype(jnp.bfloat16)] * 3
        weights = jnp.concatenate(weights, axis=1)
        planes[slab, n, 32:40, :] = zero8
        for k in range(0, CX // 4, 2):
            pieces = []
            for c in range(3):
                rest = es[c, 4 * k:4 * k + 8, 0:CY, :].reshape(256, 128)
                for _ in range(3):
                    pieces.append(rest.astype(jnp.bfloat16))
                    rest = rest - pieces[-1].astype(F32)
            total = lax.dot_general(weights, jnp.concatenate(pieces, axis=1), (((1,), (1,)), ((), ())),
                                    preferred_element_type=F32)
            for j in range(2):
                part = total[:, 128 * j:128 * j + 128]
                planes[slab, n, 8 * (k + j):8 * (k + j) + 8, :] = part[0:8]
                planes[slab, n, 32 + k + j:33 + k + j, :] = part[8:9]
        for k in range(5):
            whole = planes[slab, n, 8 * k:8 * k + 8, :]
            for q in range(2):
                for w in range(WAVES):
                    acc[q, w, k] = acc[q, w, k] + trig[q, w, n] * whole

    def plane_move(i, source):
        return pltpu.make_async_remote_copy(
            src_ref=planes.at[source], dst_ref=planes.at[source],
            send_sem=plane_send.at[i - 1], recv_sem=plane_recv.at[i - 1],
            device_id=(tile, (slab + i) % SLABS), device_id_type=MESH)

    for n in range(STEPS - 1):
        moves = sum(electric_phase(n, False), [])
        extract_planes(n)
        magnetic_phase()
        if n == 0:
            hear(1)
        arrivals(n, moves)
        below_phase(n)

    moves, later = electric_phase(STEPS - 1, True)
    extract_planes(STEPS - 1)

    part = jnp.zeros((1, 128), F32)
    odd = zero8
    for w in range(WAVES):
        odd = odd + (acc[0, w, 4] * acc[0, w, 4] + acc[1, w, 4] * acc[1, w, 4])
    for k in range(4):
        power = zero8
        for w in range(WAVES):
            power = power + (acc[0, w, k] * acc[0, w, k] + acc[1, w, k] * acc[1, w, k])
        power = jnp.sum(power, axis=0, keepdims=True) + odd[k:k + 1]
        part = part + power * focus[0:1, 128 * k:128 * k + 128]

    def send_totals(stage, mine, where):
        buf = (first, second)[stage]
        for i in sorted(range(1, 16), key=lambda i: -min(i, 16 - i)):
            pltpu.make_async_remote_copy(
                src_ref=buf.at[pl.ds(mine, 1), :], dst_ref=buf.at[pl.ds(mine, 1), :],
                send_sem=total_send.at[stage], recv_sem=total_recv.at[stage],
                device_id=where(i), device_id_type=MESH).start()

    def all_totals(stage):
        buf = (first, second)[stage].at[pl.ds(0, 15), :]
        return pltpu.make_async_remote_copy(
            src_ref=buf, dst_ref=buf, send_sem=total_send.at[stage], recv_sem=total_recv.at[stage],
            device_id=(in_row, in_column)[stage](1), device_id_type=MESH)

    first[pl.ds(col * 2 + core, 1), :] = part
    send_totals(0, col * 2 + core, in_row)
    for move in moves + later:
        move.start()
    for i in range(1, SLABS):
        plane_move(i, slab).start()
    moves = moves + later

    stores = [pltpu.make_async_copy(
        es.at[k, pl.ds(0, CX), pl.ds(0, CY), :], e_out.at[0, k], local_sem.at[7 + k]) for k in range(3)]
    for store in stores:
        store.start()
    magnetic_phase()
    arrivals(STEPS - 1, moves)
    for k in range(3):
        stores.append(pltpu.make_async_copy(
            hs.at[k, pl.ds(1, CX), pl.ds(8, CY), :], h_out.at[0, k], local_sem.at[10 + k]))
        stores[-1].start()

    all_totals(0).wait_recv()
    second[pl.ds(row * 2 + half, 1), :] = jnp.sum(first[...], axis=0, keepdims=True)
    send_totals(1, row * 2 + half, in_column)

    for i in range(1, SLABS):
        plane_move(i, (slab + SLABS - i) % SLABS).wait_recv()
    for k in range(5):
        spectrum = [[zero8] * WAVES, [zero8] * WAVES]
        for n in range(STEPS):
            whole = planes[0, n, 8 * k:8 * k + 8, :]
            for g in range(1, SLABS):
                whole = whole + planes[g, n, 8 * k:8 * k + 8, :]
            for q in range(2):
                for w in range(WAVES):
                    spectrum[q][w] = spectrum[q][w] + trig[q, w, n] * whole
        for q in range(2):
            for w in range(WAVES):
                base = 36 * q + 9 * w
                if k < 4:
                    spec[0, base:base + 8, 128 * k:128 * k + 128] = spectrum[q][w]
                else:
                    for j in range(4):
                        spec[0, base + 8:base + 9, 128 * j:128 * j + 128] = spectrum[q][w][j:j + 1]

    stores.append(pltpu.make_async_copy(spec, spec_out, small_sem.at[7]))
    stores[-1].start()
    for i in range(1, SLABS):
        plane_move(i, slab).wait_send()
    all_totals(0).wait_send()
    for store in stores:
        store.wait()
    all_totals(1).wait_recv()
    cells = TILES_X * TILES_Y * WAVES * MON * 3 * CX * CY
    objective_out[0] = jnp.sum(second[...]) / jnp.float32(cells)
    all_totals(1).wait_send()


def hand_on(e_in, h_in, s_in, o_in, e_out, h_out, s_out, o_out, sem):
    pieces = [(e_in.at[0, k], e_out.at[0, k]) for k in range(3)]
    pieces += [(h_in.at[0, k], h_out.at[0, k]) for k in range(3)]
    pieces += [(s_in, s_out), (o_in, o_out)]
    copies = [pltpu.make_async_copy(a, b, sem.at[k]) for k, (a, b) in enumerate(pieces)]
    for copy in copies:
        copy.start()
    for copy in copies:
        copy.wait()


def step(e_field, h_field, material, permittivity, pml_x, pml_y, pml_z, monitor_z, omega, focus):
    vmem = lambda *shape: pltpu.VMEM(shape, F32)
    dma = lambda *shape: pltpu.SemaphoreType.DMA(shape)
    anywhere = pl.BlockSpec(memory_space=pl.ANY)
    early = STEPS - 1
    e_out, h_out, spectra, objective = pl.pallas_call(
        kernel,
        out_shape=(
            pltpu.VMEM(e_field.shape, F32),
            pltpu.VMEM(h_field.shape, F32),
            pltpu.VMEM((1, 2 * WAVES * MON * 3, CX * CY), F32),
            pltpu.SMEM((1,), F32),
        ),
        in_specs=[anywhere] * 10,
        out_specs=(anywhere,) * 3 + (pl.BlockSpec(memory_space=pltpu.SMEM),),
        scratch_shapes=[
            vmem(*focus.shape), pltpu.SMEM(permittivity.shape, F32), pltpu.SMEM(pml_x.shape, jnp.int32),
            pltpu.SMEM(pml_y.shape, jnp.int32), pltpu.SMEM(pml_z.shape, jnp.int32),
            pltpu.SMEM(monitor_z.shape, jnp.int32), pltpu.SMEM(omega.shape, F32),
            vmem(1, 2 * WAVES * MON * 3, CX * CY),
            vmem(3, CX + 1, CY + 8, CZ), vmem(3, CX + 1, CY + 8, CZ), pltpu.VMEM((CX, CY, CZ), jnp.int32),
            vmem(CX, CY, CZ), vmem(CX, CY, CZ), vmem(CX, CY, CZ), vmem(CX, CY, CZ),
            vmem(CX, 128), vmem(CY, 128),
            vmem(2, WAVES, STEPS, 8, 128), vmem(2, WAVES, 5, 8, 128), vmem(SLABS, STEPS, 40, 128),
            vmem(2 * TILES_Y, 128), vmem(2 * TILES_X, 128),
            vmem(2, CX, 128), vmem(8, 128), vmem(2, CY, 128), vmem(2, CX, 128), vmem(2, 8, 128), vmem(CX, 128), vmem(8, 128),
            vmem(2, CX, 128), vmem(8, 128), vmem(2, CY, 128), vmem(2, CX, 128), vmem(8, 128),
            vmem(STEPS, 2, CX, 128), vmem(STEPS, 8, 128),
            vmem(STEPS, 2, CY, 128), vmem(STEPS, 2, CX, 128), vmem(STEPS, 8, 128),
            vmem(early, 2, CY, 128), vmem(early, 2, CX, 128), vmem(early, 8, 128), vmem(early, 8, 128),
            vmem(early, 2, 8, 128), vmem(3, CX, 128),
            vmem(early, 2, CY, 128), vmem(early, 2, CX, 128), vmem(early, 8, 128),
            vmem(6, early, 8, 128),
            dma(13), dma(8), dma(STEPS + 1, 12), dma(STEPS + 1, 12),
            dma(SLABS), dma(SLABS), dma(2), dma(2), pltpu.SemaphoreType.REGULAR((2, 2)),
        ],
        compiler_params=pltpu.CompilerParams(
            collective_id=0, has_side_effects=True, vmem_limit_bytes=60 * 1024 * 1024),
    )(e_field, h_field, material, focus, permittivity, pml_x, pml_y, pml_z, monitor_z, omega)
    results = (e_out, h_out, spectra, objective)
    e_out, h_out, spectra, objective = pl.pallas_call(
        hand_on,
        out_shape=tuple(jax.ShapeDtypeStruct(a.shape, F32) for a in results),
        in_specs=[anywhere] * 4,
        out_specs=(anywhere,) * 4,
        scratch_shapes=[dma(8)],
        compiler_params=pltpu.CompilerParams(vmem_limit_bytes=1024 * 1024),
    )(*results)
    return e_out, h_out, spectra, objective.reshape(())


def solution(mesh):
    field = P("xy", None, None, None, "gz")
    return jax.shard_map(
        step,
        mesh=mesh,
        in_specs=(field, field, P("xy", None, None, "gz"), P(), P(), P(), P(), P(), P(), P("xy", None)),
        out_specs=(field, field, P("xy", None, None), P()),
        check_vma=False,
    )
```
